32 devices in a mesh: expert: 8 (over y, x, core), tensor: 4 (over z).
Axes of the slice: x: 2, y: 2, z: 4, core: 2. Of those that a mesh axis runs over, the one named last changes fastest.
Arguments:
- tokens: bfloat16 [12608, 512], P(('expert', 'tensor')), may hold values from -6 to 6
- norm1_gain: float32 [512], replicated, may hold values from 0.1 to 1.9
- w_qkv: bfloat16 [512, 3, 512], P(None, None, 'tensor'), may hold values from -0.25 to 0.25
- w_out: bfloat16 [512, 512], P('tensor'), may hold values from -1.5 to 1.5
- norm2_gain: float32 [512], replicated, may hold values from 0.1 to 1.9
- w_router: bfloat16 [512, 8], replicated, may hold values from -0.125 to 0.125
- noise: float32 [12608, 8], P(('expert', 'tensor')), may hold values from -3 to 3
- routes: int32 [12608, 2], P(('expert', 'tensor')), may hold values from 0 to 7, all different within a row; in each aligned block of 394 rows (0 to 393, 394 to 787, ...) at most 197 rows name the same one
- w_in: bfloat16 [8, 512, 2048], P('expert', None, 'tensor'), may hold values from -0.25 to 0.25
- w_back: bfloat16 [8, 2048, 512], P('expert', 'tensor'), may hold values from -3 to 3
- cotangent: bfloat16 [12608, 512], P(('expert', 'tensor')), may hold values from -6 to 6
Outputs:
- output: bfloat16 [12608, 512], P(('expert', 'tensor'))
- grad_tokens: float32 [12608, 512], P(('expert', 'tensor'))
- grad_norm1: float32 [512], replicated
- grad_qkv: float32 [512, 3, 512], P(None, None, 'tensor')
- grad_out: float32 [512, 512], P('tensor')
- grad_norm2: float32 [512], replicated
- grad_router: float32 [512, 8], replicated
- grad_in: float32 [8, 512, 2048], P('expert', None, 'tensor')
- grad_back: float32 [8, 2048, 512], P('expert', 'tensor')
The draws below stay inside these ranges and needn't reach their ends.
Inputs may be any that keep to these rules, and one draw needn't show every extreme that they name: `routes`: within the rows of one device (aligned blocks of 394 rows) no expert is named by more than 197 rows, a bound that some block reaches; a row names two different experts.
All inputs are finite; a program needn't handle non-finite values.
Results may differ from the reference program's by a relative error of at most 0.023.
Values may be sent and summed in bfloat16 or wider, within the bound.
A program may use at most 192 MiB of HBM per device.

```python
import math
import jax
import jax.numpy as jnp
import numpy as np
from jax import lax

D = 512
HEADS = 8
HD = 64
FF = 2048
TOP = 2
SEQ = 197
IMG_DEV = 8
EXPERTS = 8
TOK_DEV = 1576
TOK_SP = 394
TOKENS = 12608
CAP = 197
N_EXPERT = 8
N_TENSOR = 4


def level_of(own_key, extent, shards, smallest, high):
    factor_of, own = 1.0, jax.random.fold_in(own_key, 6)
    for axis_at, shards_of in shards:
        steps = jnp.exp(jax.random.uniform(jax.random.fold_in(own, axis_at), (shards_of,), jnp.float32, smallest / len(shards), high / len(shards)))
        factor_of = factor_of * jnp.repeat(steps, extent[axis_at] // shards_of).reshape([-1 if axis == axis_at else 1 for axis in range(len(extent))])
    return factor_of


def routed_block(key, own, number, rows, number_of, top, most, slope):
    order = jax.random.permutation(key, number_of)
    crowded, ordinary = portions_of(number_of, rows * top, most, slope, True), portions_of(number_of, rows * top, most, slope, False)
    places = jnp.arange(number_of)

    def named(lengths, rotation):
        used = int((lengths > 0).sum())
        fixed = max(1, used // 4)
        shifted = fixed + (places - fixed + rotation * (used - fixed)) % max(1, number_of - fixed)
        return jnp.zeros((number_of,), jnp.int32).at[order[jnp.where(places < fixed, places, shifted)]].set(jnp.asarray(lengths, jnp.int32))

    lengths = jnp.where(number % 4 == 0, named(crowded, number // 4), named(ordinary, number - number // 4 - 1))
    mixed = jax.random.permutation(jax.random.fold_in(own, 3), number_of)
    donor, sink = mixed[0:number_of // 2 * 2:2], mixed[1:number_of // 2 * 2:2]
    room = jnp.minimum(lengths[donor] - 1, most - lengths[sink]) // 2
    room = jnp.where((donor == order[0]) | (sink == order[0]) | (lengths[sink] == 0), 0, jnp.maximum(room, 0))
    shifted = jax.random.randint(jax.random.fold_in(own, 4), (number_of // 2,), 0, 1 << 20) % (room + 1)
    lengths = lengths.at[donor].add(-shifted).at[sink].add(shifted)
    labels = jnp.searchsorted(jnp.cumsum(lengths), jnp.arange(rows * top), side="right").astype(jnp.int32)
    table = labels.reshape(top, rows).T
    table = table[jax.random.permutation(jax.random.fold_in(own, 1), rows)]
    rotation = jax.random.randint(jax.random.fold_in(own, 2), (rows, 1), 0, top)
    return jnp.take_along_axis(table, (jnp.arange(top)[None, :] + rotation) % top, axis=1)


def portions_of(count, total, bound, slope, full):
    portions = [(1 << 20) // math.isqrt(standing ** slope) + 1 for standing in range(1, count + 1)]
    largest = bound if full else min(bound, max(-(-total // count), total * portions[0] // sum(portions)))
    least = 1 if total - largest >= count - 1 else 0
    counts, rest = [largest] + [least] * (count - 1), total - largest - least * (count - 1)
    while rest > 0:
        candidates = [i for i in range(1, count) if counts[i] < largest] or [i for i in range(1, count) if counts[i] < bound]
        whole, remaining = sum([portions[i] for i in candidates]), rest
        for i in candidates:
            extra = min(bound - counts[i], max(1, remaining * portions[i] // whole), rest)
            counts[i] = counts[i] + extra
            rest = rest - extra
    return np.array(counts)


def normal_values(key, extent, scale, most, shards=(), kind=jnp.bfloat16):
    values = jax.random.normal(key, extent, jnp.float32) * scale
    if len(shards) > 0:
        values = level_of(key, extent, shards, -0.22, 0.18) * values
    return jnp.clip(values, min=-most, max=most).astype(kind)


def setup_inputs(seed: int = 0) -> dict:
    arg_keys = jax.random.split(jax.random.key(seed), 12)
    tokens = normal_values(arg_keys[0], (TOKENS, D), 1.0, 6.0, ((0, 32),))
    norm1_gain = jnp.clip(1.0 + 0.18 * jax.random.normal(arg_keys[1], (D,), jnp.float32), 0.1, 1.9)
    w_qkv = normal_values(arg_keys[2], (D, 3, D), D ** -0.5, 0.25, ((2, 4),))
    w_out = normal_values(arg_keys[3], (D, D), (D // 32) ** -0.5, 1.5, ((0, 4),))
    norm2_gain = jnp.clip(1.0 + 0.18 * jax.random.normal(arg_keys[4], (D,), jnp.float32), 0.1, 1.9)
    w_router = normal_values(arg_keys[5], (D, EXPERTS), (4 * D) ** -0.5, 0.125)
    noise = normal_values(arg_keys[6], (TOKENS, EXPERTS), 0.5, 3.0, ((0, 32),), jnp.float32)
    routes_keys = jax.random.split(jax.random.fold_in(arg_keys[7], 1), TOKENS // TOK_SP)
    routes_turns = jax.random.permutation(jax.random.fold_in(arg_keys[7], 3), TOKENS // TOK_SP)
    routes = jax.vmap(lambda own, number: routed_block(jax.random.fold_in(arg_keys[7], 2), own, number, TOK_SP, EXPERTS, TOP, CAP, 1))(routes_keys, routes_turns).reshape((TOKENS, TOP))
    w_in = normal_values(arg_keys[8], (EXPERTS, D, FF), D ** -0.5, 0.25, ((0, 8), (2, 4)))
    w_back = normal_values(arg_keys[9], (EXPERTS, FF, D), (max(FF // 512, 1)) ** -0.5, 3.0, ((0, 8), (1, 4)))
    cotangent = normal_values(arg_keys[10], (TOKENS, D), 1.0, 6.0, ((0, 32),))
    return {"tokens": tokens, "norm1_gain": norm1_gain, "w_qkv": w_qkv, "w_out": w_out, "norm2_gain": norm2_gain, "w_router": w_router, "noise": noise, "routes": routes, "w_in": w_in, "w_back": w_back, "cotangent": cotangent}


epsilon = 1e-06
highest = lax.Precision.HIGHEST

@jax.custom_vjp
def low(v):
    return lax.optimization_barrier(v.astype(jnp.bfloat16)).astype(jnp.float32)

@jax.custom_vjp
def low_back(v):
    return v

def low_keep(v):
    return (low(v), None)

def low_pass(kept, grad):
    return (grad,)

def back_keep(v):
    return (v, None)

def back_low(kept, grad):
    return (low(grad),)
low.defvjp(low_keep, low_pass)
low_back.defvjp(back_keep, back_low)

def layer_norm(values, gain_vec):
    center = values - lax.optimization_barrier(jnp.mean(values, -1, keepdims=True))
    spread = lax.optimization_barrier(jnp.mean(center * center, -1, keepdims=True))
    return center * lax.rsqrt(spread + epsilon) * gain_vec

def group_block(weights, inputs, noise_rows, route_rows):
    norm1, w_qkv, w_out, norm2, w_router, w_in, w_back = weights
    normed = low(layer_norm(inputs, norm1))
    projected = jnp.einsum('td,dcn->tcn', normed, w_qkv, precision=highest)
    shaped = (IMG_DEV, SEQ, HEADS, HD)
    queries = low(low_back(projected[:, 0])).reshape(shaped)
    key_rows = low(low_back(projected[:, 1])).reshape(shaped)
    value_rows = low(low_back(projected[:, 2])).reshape(shaped)
    scores = low_back(jnp.einsum('bqhd,bkhd->bhqk', queries, key_rows, precision=highest) * HD ** (-0.5))
    attend = jax.nn.softmax(scores, axis=-1)
    mixed = jnp.einsum('bhqk,bkhd->bqhd', low(attend), value_rows, precision=highest)
    mixed = low(low_back(mixed)).reshape(TOK_DEV, D)
    attention = low_back(jnp.dot(mixed, w_out, precision=highest))
    residual = inputs + attention
    normed2 = low(layer_norm(residual, norm2))
    router = jax.nn.softmax(jnp.dot(normed2, w_router, precision=highest) + noise_rows, axis=-1)
    gate_vals = jnp.take_along_axis(router, route_rows, axis=1)
    picked = route_rows.reshape(N_TENSOR, TOK_SP * TOP).astype(jnp.int32)
    one_hot = (picked[:, :, None] == jnp.arange(EXPERTS, dtype=jnp.int32)[None, None, :]).astype(jnp.int32)
    ranks = (jnp.cumsum(one_hot, axis=1) - 1).astype(jnp.int32)
    places = lax.optimization_barrier(jnp.sum(one_hot * ranks, axis=-1)).astype(jnp.int32)
    blocks = jnp.arange(N_TENSOR, dtype=jnp.int32)[:, None]
    slot_ids = ((blocks * EXPERTS + picked) * CAP + places).reshape(-1).astype(jnp.int32)
    owners = jnp.zeros((N_TENSOR * EXPERTS * CAP,), jnp.int32)
    owners = owners.at[slot_ids].set(jnp.arange(TOK_DEV * TOP, dtype=jnp.int32) + 1)
    source = (jnp.maximum(owners - 1, 0) // TOP).astype(jnp.int32)
    routed = jnp.where((owners > 0)[:, None], normed2[source], jnp.zeros((), normed2.dtype))
    routed = low_back(routed).reshape(N_TENSOR, EXPERTS, CAP, D)
    pre_act = low_back(jnp.einsum('tecd,edf->etcf', routed, w_in, precision=highest))
    hidden = low(jax.nn.gelu(pre_act, approximate=False))
    returned = jnp.einsum('etcf,efd->tecd', hidden, w_back, precision=highest)
    returned = low(low_back(returned)).reshape(N_TENSOR * EXPERTS * CAP, D)
    paired = returned[slot_ids].reshape(TOK_DEV, TOP, D)
    return residual + lax.optimization_barrier(jnp.sum(gate_vals[:, :, None] * paired, axis=1))

def reference(tokens, norm1_gain, w_qkv, w_out, norm2_gain, w_router, noise, routes, w_in, w_back, cotangent):
    saved_block = jax.checkpoint(group_block)
    inputs = tokens.astype(jnp.float32)
    groups = (noise.reshape(N_EXPERT, TOK_DEV, EXPERTS), routes.reshape(N_EXPERT, TOK_DEV, TOP))

    def forward(rows, norm1, wqkv, wout, norm2, wrouter, win, wback):
        weights = (norm1, wqkv, wout, norm2, wrouter, win, wback)

        def scan_step(unused, group_item):
            return (unused, saved_block(weights, group_item[0], group_item[1], group_item[2]))
        unused, results = lax.scan(scan_step, 0.0, (rows.reshape(N_EXPERT, TOK_DEV, D), groups[0], groups[1]))
        return results.reshape(TOKENS, D)
    output, pullback = jax.vjp(forward, inputs, norm1_gain.astype(jnp.float32), w_qkv.astype(jnp.float32), w_out.astype(jnp.float32), norm2_gain.astype(jnp.float32), w_router.astype(jnp.float32), w_in.astype(jnp.float32), w_back.astype(jnp.float32))
    gradients = pullback(cotangent.astype(jnp.float32))
    return (output.astype(jnp.bfloat16), gradients[0], gradients[1], gradients[2], gradients[3], gradients[4], gradients[5], gradients[6], gradients[7])
```

```python
import functools

import jax
import jax.numpy as jnp
from jax import lax
from jax.experimental import pallas as pl
from jax.experimental.pallas import tpu as pltpu
from jax.sharding import PartitionSpec as P

D = 512
HD = 64
TOP = 2
SEQ = 197
LANES = 128
TILE = 16
CHUNK = 256
EPSILON = 1e-06
BF = jnp.bfloat16
F32 = jnp.float32
VMEM_BYTES = 56 * 1024 * 1024

NN = (((1,), (0,)), ((), ()))
NT = (((1,), (1,)), ((), ()))
TN = (((0,), (0,)), ((), ()))


def up(value, unit):
    return (value + unit - 1) // unit * unit


SP = up(SEQ, TILE)


def mm(a, b, dims=NN):
    return lax.dot_general(a, b, dims, preferred_element_type=F32)


def call(body, out_shape, scratch=(), flops=0, moved=0, prefetch=None, **more):
    params = pltpu.CompilerParams(vmem_limit_bytes=VMEM_BYTES, **more)
    vmem = pl.BlockSpec(memory_space=pltpu.VMEM)
    cost = pl.CostEstimate(flops=flops, bytes_accessed=moved, transcendentals=0)

    def run(*args):
        specs = [vmem] * len(args)
        for place in prefetch or ():
            specs[place] = pl.BlockSpec(memory_space=pltpu.SMEM)
        return pl.pallas_call(
            body,
            out_shape=out_shape,
            in_specs=specs,
            out_specs=jax.tree.map(lambda _: vmem, out_shape),
            scratch_shapes=list(scratch),
            compiler_params=params,
            cost_estimate=cost,
        )(*args)

    return run


def shape(dims, dtype=BF):
    return jax.ShapeDtypeStruct(dims, dtype)


def unit_norm(values):
    center = values - jnp.mean(values, -1, keepdims=True)
    spread = jnp.mean(center * center, -1, keepdims=True)
    inverse = lax.rsqrt(spread + EPSILON)
    return center * inverse, inverse


def norm_back(grad_rows, normed, inverse, gain):
    scaled = grad_rows * gain
    inner = (
        scaled
        - jnp.mean(scaled, -1, keepdims=True)
        - normed * jnp.mean(scaled * normed, -1, keepdims=True)
    )
    return inverse * inner, jnp.sum(grad_rows * normed, axis=0, keepdims=True)


def ids(shape_of, dim):
    return lax.broadcasted_iota(jnp.int32, shape_of, dim)


def slots_by_lane(routes_t, experts):
    rows = routes_t.shape[1]
    which = ids((experts, rows), 0)
    named = (routes_t[0:1] == which) | (routes_t[1:2] == which)
    before = (ids((rows, rows), 0) < ids((rows, rows), 1)).astype(F32).astype(BF)
    rank = mm(named.astype(F32).astype(BF), before)
    return jnp.where(named, rank, -1.0)


def slots_by_row(routes, experts):
    rows = routes.shape[0]
    which = ids((rows, experts), 1)
    named = (routes[:, 0:1] == which) | (routes[:, 1:2] == which)
    before = (ids((rows, rows), 1) < ids((rows, rows), 0)).astype(F32).astype(BF)
    rank = mm(before, named.astype(F32).astype(BF))
    return jnp.where(named, rank, -1.0)


def send_rows(slots, rows, out_ref, experts):
    count = out_ref.shape[1]
    place = ids((count, rows.shape[0]), 0).astype(F32)
    for e in range(experts):
        pick = (place == slots[e : e + 1, :]).astype(F32).astype(BF)
        out_ref[e] = mm(pick, rows).astype(BF)


def take_rows(slots, in_ref, experts):
    count = in_ref.shape[1]
    rows = slots.shape[0]
    place = ids((rows, count), 1).astype(F32)
    total = None
    for e in range(experts):
        pick = (place == slots[:, e : e + 1]).astype(F32).astype(BF)
        part = mm(pick, in_ref[e])
        total = part if total is None else total + part
    return total


def early_kernel(experts, routes_t_ref, cot_ref, noise_ref, out_ref):
    lane = ids(noise_ref.shape, 1)
    noise = noise_ref[...]
    high = noise.astype(BF)
    rest = noise - high.astype(F32)
    middle = rest.astype(BF)
    low = (rest - middle.astype(F32)).astype(BF)
    parts = jnp.where(
        lane < experts,
        high.astype(F32),
        jnp.where(
            lane < 2 * experts,
            middle.astype(F32),
            jnp.where(lane < 3 * experts, low.astype(F32), noise),
        ),
    ).astype(BF)
    slots = slots_by_lane(routes_t_ref[...], experts)
    send_rows(slots, jnp.concatenate([cot_ref[...], parts], axis=1), out_ref, experts)


def attend_kernel(
    experts, images, routes_t_ref, x_ref, gain1_ref, w_qkv_ref, w_out_ref, gain2_ref,
    qkv_ref, attend_ref, mixed_ref, residual_ref, send_ref,
):
    groups, _, wide = w_qkv_ref.shape
    width = wide // 3
    heads = width // HD
    x = x_ref[...].astype(F32)
    unit1, _ = unit_norm(x)
    normed1 = (unit1 * gain1_ref[...]).astype(BF)
    lane = ids((SP, width), 1) // HD
    live = ids((SP, SP), 1) < SEQ
    for t in range(groups):
        qkv_ref[t] = mm(normed1, w_qkv_ref[t]).astype(BF)
        for i in range(images):
            rows = slice(i * SP, (i + 1) * SP)
            q = qkv_ref[t, rows, 0:width]
            k = qkv_ref[t, rows, width : 2 * width]
            v = qkv_ref[t, rows, 2 * width : 3 * width]
            mixed = None
            for j in range(heads):
                q_j = q if heads == 1 else jnp.where(lane == j, q, jnp.zeros_like(q))
                scores = mm(q_j, k, NT) * HD ** (-0.5)
                scores = jnp.where(live, scores, -1e30)
                power = jnp.exp(scores - jnp.max(scores, -1, keepdims=True))
                attend = (power / jnp.sum(power, -1, keepdims=True)).astype(BF)
                attend_ref[i, t * heads + j] = attend
                part = mm(attend, v)
                mixed = part if mixed is None else jnp.where(lane == j, part, mixed)
            mixed_ref[rows, t * width : (t + 1) * width] = mixed.astype(BF)
    residual = x + mm(mixed_ref[...], w_out_ref[...])
    residual_ref[...] = residual
    unit2, _ = unit_norm(residual)
    normed2 = (unit2 * gain2_ref[...]).astype(BF)
    send_rows(slots_by_lane(routes_t_ref[...], experts), normed2, send_ref, experts)


def gelu_parts(pre):
    density = jnp.exp(pre * pre * -0.5)
    size = jnp.abs(pre) * (0.5**0.5)
    t = 1.0 / (1.0 + 0.3275911 * size)
    series = t * (
        0.254829592
        + t * (-0.284496736 + t * (1.421413741 + t * (-1.453152027 + t * 1.061405429)))
    )
    tail = 0.5 * series * density
    return jnp.where(pre < 0, tail, 1.0 - tail), density * 0.3989422804014327


def expert_kernel(
    experts, own_ref, count_ref, x_in, early_in, w_router_ref, w_in_ref, w_back_ref,
    out_ref, back_ref, grads_ref, router_grad_ref,
    xs, es, dexp, hidden, dpre, outs, backs, total,
):
    sources, slots, _ = x_in.shape
    parts = w_in_ref.shape[0]
    width = w_in_ref.shape[2]
    own = own_ref[0]

    base = jnp.int32(0)
    for s in range(sources):
        tiles = (count_ref[s] + TILE - 1) // TILE

        def copy_in(j, _, s=s, base=base):
            to = pl.ds(pl.multiple_of((base + j) * TILE, TILE), TILE)
            at = pl.ds(pl.multiple_of(j * TILE, TILE), TILE)
            xs[to, :] = x_in[s, at, :]
            es[to, :] = early_in[s, at, :]
            return 0

        lax.fori_loop(0, tiles, copy_in, 0)
        base = base + tiles
    per = CHUNK // TILE
    chunks = (base + per - 1) // per

    def clear(j, _):
        to = pl.ds(pl.multiple_of(j * TILE, TILE), TILE)
        xs[to, :] = jnp.zeros((TILE, xs.shape[1]), BF)
        es[to, :] = jnp.zeros((TILE, es.shape[1]), BF)
        return 0

    lax.fori_loop(base, chunks * per, clear, 0)

    lane = ids((CHUNK, LANES), 1)
    fold_from, fold_to = ids((LANES, LANES), 0), ids((LANES, LANES), 1)
    fold = (
        (fold_from < 3 * experts) & (lax.rem(fold_from, experts) == fold_to)
    ).astype(F32).astype(BF)
    router_grad_ref[...] = jnp.zeros_like(router_grad_ref)

    def rows_of(c):
        return pl.ds(pl.multiple_of(c * CHUNK, CHUNK), CHUNK)

    def forward(c, _):
        rows = rows_of(c)
        x = xs[rows, :]
        cot = es[rows, 0:D].astype(F32)
        logits = mm(x, w_router_ref[...]) + mm(es[rows, D : D + LANES], fold)
        logits = jnp.where(lane < experts, logits, -1e30)
        power = jnp.exp(logits - jnp.max(logits, -1, keepdims=True))
        router = power / jnp.sum(power, -1, keepdims=True)
        mine = lane == own
        gate = jnp.sum(jnp.where(mine, router, 0.0), -1, keepdims=True)
        d_exp = (gate * cot).astype(BF)
        dexp[rows, :] = d_exp
        out = jnp.zeros((CHUNK, D), F32)
        back = jnp.zeros((CHUNK, D), F32)
        for f in range(parts):
            pre = mm(x, w_in_ref[f])
            normal, density = gelu_parts(pre)
            low = (pre * normal).astype(BF)
            hidden[f, rows, :] = low
            w_b = w_back_ref[f]
            out = out + mm(low, w_b)
            d_pre = (mm(d_exp, w_b, NT) * (normal + pre * density)).astype(BF)
            dpre[f, rows, :] = d_pre
            back = back + mm(d_pre, w_in_ref[f], NT)
        out = out.astype(BF).astype(F32)
        outs[rows, :] = (gate * out).astype(BF)
        d_gate = jnp.sum(cot * out, -1, keepdims=True)
        d_logits = (d_gate * gate * (mine.astype(F32) - router)).astype(BF)
        backs[rows, :] = (back + mm(d_logits, w_router_ref[...], NT)).astype(BF)
        router_grad_ref[...] += mm(x, d_logits, TN)
        return 0

    lax.fori_loop(0, chunks, forward, 0)

    def grads(f, _):
        def add_in(c, _):
            total[0] += mm(xs[rows_of(c), :], dpre[f, rows_of(c), :], TN)
            total[1] += mm(dexp[rows_of(c), :], hidden[f, rows_of(c), :], TN)
            return 0

        total[...] = jnp.zeros_like(total)
        lax.fori_loop(0, chunks, add_in, 0)
        grads_ref[f] = total[...].astype(BF)
        return 0

    lax.fori_loop(0, parts, grads, 0)

    base = jnp.int32(0)
    for s in range(sources):
        tiles = (count_ref[s] + TILE - 1) // TILE

        def copy_out(j, _, s=s, base=base):
            at = pl.ds(pl.multiple_of((base + j) * TILE, TILE), TILE)
            to = pl.ds(pl.multiple_of(j * TILE, TILE), TILE)
            out_ref[s, to, :] = outs[at, :]
            back_ref[s, to, :] = backs[at, :]
            return 0

        def clear_out(j, _, s=s):
            to = pl.ds(pl.multiple_of(j * TILE, TILE), TILE)
            out_ref[s, to, :] = jnp.zeros((TILE, D), BF)
            back_ref[s, to, :] = jnp.zeros((TILE, D), BF)
            return 0

        lax.fori_loop(0, tiles, copy_out, 0)
        lax.fori_loop(tiles, slots // TILE, clear_out, 0)
        base = base + tiles


def backward_kernel(
    experts, images, routes_ref, back_ref, residual_ref, cot_ref, x_ref, gain1_ref, gain2_ref,
    w_qkv_ref, w_out_ref, qkv_ref, attend_ref, mixed_ref,
    tokens_grad_ref, qkv_grad_ref, out_grad_ref, norm1_ref, norm2_ref, d_mixed_ref, d_qkv_ref,
):
    groups, _, wide = w_qkv_ref.shape
    width = wide // 3
    heads = width // HD
    slots = slots_by_row(routes_ref[...], experts)
    d_normed2 = take_rows(slots, back_ref, experts)
    unit2, inverse2 = unit_norm(residual_ref[...])
    d_rows, norm2 = norm_back(d_normed2, unit2, inverse2, gain2_ref[...])
    norm2_ref[...] = norm2
    d_residual = cot_ref[...].astype(F32) + d_rows
    tokens_grad_ref[...] = d_residual
    d_attention = d_residual.astype(BF)
    out_grad = mm(mixed_ref[...], d_attention, TN).astype(BF)
    for t in range(groups):
        out_grad_ref[t] = out_grad[t * width : (t + 1) * width]
    d_mixed = mm(d_attention, w_out_ref[...], NT).astype(BF)
    for t in range(groups):
        d_mixed_ref[t] = d_mixed[:, t * width : (t + 1) * width]
    x = x_ref[...].astype(F32)
    unit1, inverse1 = unit_norm(x)
    normed1 = (unit1 * gain1_ref[...]).astype(BF)
    lane = ids((SP, width), 1) // HD
    scaling = HD ** (-0.5)
    d_normed1 = None
    for t in range(groups):
        for i in range(images):
            rows = slice(i * SP, (i + 1) * SP)
            q = qkv_ref[t, rows, 0:width]
            k = qkv_ref[t, rows, width : 2 * width]
            v = qkv_ref[t, rows, 2 * width : 3 * width]
            do = d_mixed_ref[t, rows, :]
            dq = dk = dv = None
            for j in range(heads):
                own = lane == j
                do_j = do if heads == 1 else jnp.where(own, do, jnp.zeros_like(do))
                q_j = q if heads == 1 else jnp.where(own, q, jnp.zeros_like(q))
                attend_low = attend_ref[i, t * heads + j]
                attend = attend_low.astype(F32)
                part_v = mm(attend_low, do_j, TN)
                d_attend = mm(do_j, v, NT)
                inner = jnp.sum(attend * d_attend, -1, keepdims=True)
                ds = (attend * (d_attend - inner)).astype(BF)
                part_q = mm(ds, k) * scaling
                part_k = mm(ds, q_j, TN) * scaling
                dq = part_q if dq is None else jnp.where(own, part_q, dq)
                dk = part_k if dk is None else dk + part_k
                dv = part_v if dv is None else dv + part_v
            d_qkv_ref[t, rows, 0:width] = dq.astype(BF)
            d_qkv_ref[t, rows, width : 2 * width] = dk.astype(BF)
            d_qkv_ref[t, rows, 2 * width : 3 * width] = dv.astype(BF)
        d_t = d_qkv_ref[t]
        qkv_grad_ref[t] = mm(normed1, d_t, TN).astype(BF)
        part = mm(d_t, w_qkv_ref[t], NT)
        d_normed1 = part if d_normed1 is None else d_normed1 + part
    d_rows, norm1 = norm_back(d_normed1, unit1, inverse1, gain1_ref[...])
    norm1_ref[...] = norm1
    tokens_grad_ref[...] += d_rows


def output_kernel(experts, routes_ref, out_in, residual_ref, output_ref):
    slots = slots_by_row(routes_ref[...], experts)
    output_ref[...] = (residual_ref[...] + take_rows(slots, out_in, experts)).astype(BF)


def per_device(
    tokens, norm1_gain, w_qkv, w_out, norm2_gain, w_router, noise, routes, w_in, w_back, cotangent
):
    own_rows = tokens.shape[0]
    experts = noise.shape[1]
    tensor = lax.axis_size("tensor")
    images = own_rows // SEQ
    rows = images * SP
    capacity = (2 * own_rows * TOP + experts - 1) // experts
    slots = up(capacity, TILE)
    width = w_out.shape[0]
    hidden = w_in.shape[2]

    def padded(a, fill=0):
        a = a.reshape(images, SEQ, a.shape[1])
        a = jnp.pad(a, ((0, 0), (0, SP - SEQ), (0, 0)), constant_values=fill)
        return a.reshape(rows, a.shape[2])

    def own(a):
        return a.reshape(images, SP, a.shape[1])[:, :SEQ].reshape(own_rows, a.shape[1])

    w_qkv_all = lax.all_gather(w_qkv.reshape(D, 3 * width), "tensor", axis=0)
    w_out_all = lax.all_gather(w_out, "tensor", axis=0, tiled=True)
    w_in_all = lax.all_gather(w_in[0], "tensor", axis=0)
    w_back_all = lax.all_gather(w_back[0], "tensor", axis=0)

    x = padded(tokens)
    cot = padded(cotangent)
    routes_p = padded(routes, -1)
    routes_t = routes_p.T
    spread = jnp.concatenate(
        [noise] * 3
        + [jnp.ones((own_rows, 1), F32), jnp.zeros((own_rows, LANES - 3 * experts - 1), F32)],
        axis=1,
    )
    early = call(
        functools.partial(early_kernel, experts), shape((experts, slots, D + LANES))
    )(routes_t, cot, padded(spread))
    early = lax.all_to_all(early, "expert", split_axis=0, concat_axis=0, tiled=True)
    counts = jnp.sum(early[:, :, D + 3 * experts].astype(F32), axis=1).astype(jnp.int32)

    gain1, gain2 = norm1_gain.reshape(1, D), norm2_gain.reshape(1, D)
    heads = tensor * width // HD
    qkv, attend, mixed, residual, send = call(
        functools.partial(attend_kernel, experts, images),
        (
            shape((tensor, rows, 3 * width)),
            shape((images, heads, SP, SP)),
            shape((rows, D)),
            shape((rows, D), F32),
            shape((experts, slots, D)),
        ),
        flops=2 * rows * D * D * 4,
        moved=10_000_000,
    )(routes_t, x, gain1, w_qkv_all, w_out_all, gain2)
    routed = lax.all_to_all(send, "expert", split_axis=0, concat_axis=0, tiled=True)

    w_router_wide = jnp.pad(w_router, ((0, 0), (0, LANES - experts)))
    most = up(experts * slots, CHUNK)
    own_expert = lax.axis_index("expert").astype(jnp.int32).reshape(1)
    outs, backs, grads, router_grad = call(
        functools.partial(expert_kernel, experts),
        (
            shape((experts, slots, D)),
            shape((experts, slots, D)),
            shape((tensor, 2, D, hidden)),
            shape((D, LANES), F32),
        ),
        scratch=(
            pltpu.VMEM((most, D), BF),
            pltpu.VMEM((most, D + LANES), BF),
            pltpu.VMEM((most, D), BF),
            pltpu.VMEM((tensor, most, hidden), BF),
            pltpu.VMEM((tensor, most, hidden), BF),
            pltpu.VMEM((most, D), BF),
            pltpu.VMEM((most, D), BF),
            pltpu.VMEM((2, D, hidden), F32),
        ),
        flops=12 * experts * slots * D * tensor * hidden,
        moved=20_000_000,
        prefetch=(0, 1),
    )(own_expert, counts, routed, early, w_router_wide, w_in_all, w_back_all)

    returned = lax.all_to_all(backs, "expert", split_axis=0, concat_axis=0, tiled=True)
    returned_out = lax.all_to_all(outs, "expert", split_axis=0, concat_axis=0, tiled=True)
    grads = lax.psum_scatter(grads, "tensor", scatter_dimension=0, tiled=True)[0]

    grad_tokens, qkv_grad, out_grad, norm1, norm2 = call(
        functools.partial(backward_kernel, experts, images),
        (
            shape((rows, D), F32),
            shape((tensor, D, 3 * width)),
            shape((tensor, width, D)),
            shape((1, D), F32),
            shape((1, D), F32),
        ),
        scratch=(
            pltpu.VMEM((tensor, rows, width), BF),
            pltpu.VMEM((tensor, rows, 3 * width), BF),
        ),
        flops=2 * rows * D * D * 10,
        moved=10_000_000,
    )(
        routes_p, returned, residual, cot, x, gain1, gain2,
        w_qkv_all, w_out_all, qkv, attend, mixed,
    )
    output = call(functools.partial(output_kernel, experts), shape((rows, D)))(
        routes_p, returned_out, residual
    )
    both = jnp.concatenate(
        [qkv_grad.reshape(tensor, 3 * width, D), out_grad.reshape(tensor, width, D)], axis=1
    )
    both = lax.psum_scatter(both, "tensor", scatter_dimension=0, tiled=True)[0]
    both = lax.psum(both, "expert").astype(F32)
    router_grad, norm1, norm2 = lax.psum(
        (router_grad[:, :experts], norm1, norm2), ("expert", "tensor")
    )
    return (
        own(output),
        own(grad_tokens),
        norm1.reshape(D),
        both[: 3 * width].reshape(D, 3, width),
        both[3 * width :],
        norm2.reshape(D),
        router_grad,
        grads[0].astype(F32)[None],
        grads[1].T.astype(F32)[None],
    )


def solution(mesh):
    rows = P(("expert", "tensor"), None)
    placed = (
        rows,
        P(),
        P(None, None, "tensor"),
        P("tensor", None),
        P(),
        P(),
        rows,
        rows,
        P("expert", None, "tensor"),
        P("expert", "tensor", None),
        rows,
    )
    return jax.shard_map(
        per_device,
        mesh=mesh,
        in_specs=placed,
        out_specs=(
            rows,
            rows,
            P(),
            P(None, None, "tensor"),
            P("tensor", None),
            P(),
            P(),
            P("expert", None, "tensor"),
            P("expert", "tensor", None),
        ),
        check_vma=False,
    )
```

```python
import functools

import jax
import jax.numpy as jnp
from jax import lax
from jax.experimental import pallas as pl
from jax.experimental.pallas import tpu as pltpu
from jax.sharding import PartitionSpec as P

D = 512
HD = 64
TOP = 2
SEQ = 197
LANES = 128
TILE = 16
CHUNK = 256
EPSILON = 1e-06
BF = jnp.bfloat16
F32 = jnp.float32
VMEM_BYTES = 56 * 1024 * 1024

NN = (((1,), (0,)), ((), ()))
NT = (((1,), (1,)), ((), ()))
TN = (((0,), (0,)), ((), ()))


def up(value, unit):
    return (value + unit - 1) // unit * unit


SP = up(SEQ, TILE)


def mm(a, b, dims=NN):
    return lax.dot_general(a, b, dims, preferred_element_type=F32)


def call(
    body, out_shape, scratch=(), flops=0, moved=0, prefetch=(), far_in=(), far_out=(), **more
):
    params = pltpu.CompilerParams(vmem_limit_bytes=VMEM_BYTES, **more)
    cost = pl.CostEstimate(flops=flops, bytes_accessed=moved, transcendentals=0)

    def spec(place, far, scalar=()):
        if place in scalar:
            return pl.BlockSpec(memory_space=pltpu.SMEM)
        return pl.BlockSpec(memory_space=pl.ANY if place in far else pltpu.VMEM)

    def run(*args):
        return pl.pallas_call(
            body,
            out_shape=out_shape,
            in_specs=[spec(place, far_in, prefetch) for place in range(len(args))],
            out_specs=tuple(spec(place, far_out) for place in range(len(out_shape))),
            scratch_shapes=list(scratch),
            compiler_params=params,
            cost_estimate=cost,
        )(*args)

    return run


def shape(dims, dtype=BF):
    return jax.ShapeDtypeStruct(dims, dtype)


def unit_norm(values):
    center = values - jnp.mean(values, -1, keepdims=True)
    spread = jnp.mean(center * center, -1, keepdims=True)
    inverse = lax.rsqrt(spread + EPSILON)
    return center * inverse, inverse


def norm_back(grad_rows, normed, inverse, gain):
    scaled = grad_rows * gain
    inner = (
        scaled
        - jnp.mean(scaled, -1, keepdims=True)
        - normed * jnp.mean(scaled * normed, -1, keepdims=True)
    )
    return inverse * inner, jnp.sum(grad_rows * normed, axis=0, keepdims=True)


def ids(shape_of, dim):
    return lax.broadcasted_iota(jnp.int32, shape_of, dim)


def slots_by_lane(routes_t, experts):
    rows = routes_t.shape[1]
    which = ids((experts, rows), 0)
    named = (routes_t[0:1] == which) | (routes_t[1:2] == which)
    before = (ids((rows, rows), 0) < ids((rows, rows), 1)).astype(F32).astype(BF)
    rank = mm(named.astype(F32).astype(BF), before)
    return jnp.where(named, rank, -1.0)


def slots_by_row(routes, experts):
    rows = routes.shape[0]
    which = ids((rows, experts), 1)
    named = (routes[:, 0:1] == which) | (routes[:, 1:2] == which)
    before = (ids((rows, rows), 1) < ids((rows, rows), 0)).astype(F32).astype(BF)
    rank = mm(before, named.astype(F32).astype(BF))
    return jnp.where(named, rank, -1.0)


def send_rows(slots, rows, out_ref, experts):
    count = out_ref.shape[1]
    place = ids((count, rows.shape[0]), 0).astype(F32)
    for e in range(experts):
        pick = (place == slots[e : e + 1, :]).astype(F32).astype(BF)
        out_ref[e] = mm(pick, rows).astype(BF)


def take_rows(slots, in_ref, experts):
    count = in_ref.shape[1]
    rows = slots.shape[0]
    place = ids((rows, count), 1).astype(F32)
    total = None
    for e in range(experts):
        pick = (place == slots[:, e : e + 1]).astype(F32).astype(BF)
        part = mm(pick, in_ref[e])
        total = part if total is None else total + part
    return total


MESH = pl.DeviceIdType.MESH


def greet(axes):
    barrier = pltpu.get_barrier_semaphore()
    for name, size in axes:
        me = lax.axis_index(name)

        def hello(d, _, name=name, size=size, me=me):
            pl.semaphore_signal(
                barrier, inc=1, device_id={name: lax.rem(me + d, size)}, device_id_type=MESH
            )
            return 0

        lax.fori_loop(1, size, hello, 0)
    pl.semaphore_wait(barrier, sum(size - 1 for _, size in axes))


def remote(src, dst, send_sem, recv_sem, name, to):
    return pltpu.make_async_remote_copy(
        src_ref=src,
        dst_ref=dst,
        send_sem=send_sem,
        recv_sem=recv_sem,
        device_id={name: to},
        device_id_type=MESH,
    )


def each(size, step):
    def body(d, _):
        step(d)
        return 0

    lax.fori_loop(1, size, body, 0)


class Line:
    def __init__(self, size, own, everyone, send_sem, recv_sem):
        self.size, self.own, self.all = size, own, everyone
        self.send_sem, self.recv_sem = send_sem, recv_sem
        self.me = lax.axis_index("tensor")

    def copy(self, way, step, arriving):
        toward = 1 if way == 0 else -1
        owner = self.me - toward * (step + (1 if arriving else 0))
        src = self.own if step == 0 else self.all.at[owner]
        return remote(
            src, self.all.at[owner], self.send_sem.at[way, step], self.recv_sem.at[way, step],
            "tensor", self.me + toward,
        )

    def sends(self, way, step):
        last = self.size - 1
        if way == 0:
            return (self.me >= step) & (self.me < last)
        return (self.me <= last - step) & (self.me > 0)

    def receives(self, way, step):
        if way == 0:
            return self.me >= step + 1
        return self.me <= self.size - 2 - step

    def start(self, step):
        for way in (0, 1):
            pl.when(self.sends(way, step))(lambda way=way: self.copy(way, step, False).start())

    def arrive(self, step):
        for way in (0, 1):
            pl.when(self.receives(way, step))(
                lambda way=way: self.copy(way, step, True).wait_recv()
            )

    def finish(self):
        for step in range(self.size - 1):
            for way in (0, 1):
                pl.when(self.sends(way, step))(
                    lambda way=way, step=step: self.copy(way, step, False).wait_send()
                )


def forward_kernel(
    experts, tensor, images, routes_t_ref, x_ref, cot_ref, noise_ref, gain1_ref, gain2_ref,
    w_own_ref, w_in_own, w_back_own,
    w_ref, qkv_ref, attend_ref, mixed_ref, residual_ref, routed_ref, early_ref, w_in_all, w_back_all,
    slots_ref, send_ref, early_send, own_sem, piece_sems, plane_sems, early_sems, route_sems,
    in_sems, back_sems,
):
    wide = w_own_ref.shape[1]
    width = wide // 4
    heads = width // HD
    me_e, me_t = lax.axis_index("expert"), lax.axis_index("tensor")
    piece = D // experts
    mine = pl.ds(pl.multiple_of(me_e * piece, piece), piece)

    def piece_copy(d, arriving):
        owner = lax.rem(me_t + tensor - d, tensor) if arriving else me_t
        return remote(
            w_own_ref.at[mine], w_ref.at[owner, mine], piece_sems.at[0, d], piece_sems.at[1, d],
            "tensor", lax.rem(me_t + d, tensor),
        )

    def plane_copy(z, d, arriving):
        owner = lax.rem(me_t + tensor - z, tensor)
        other = lax.rem(me_e + experts - d, experts) if arriving else me_e
        rows = pl.ds(pl.multiple_of(other * piece, piece), piece)
        block = w_ref.at[owner, rows]
        return remote(
            block, block, plane_sems.at[0, z, d], plane_sems.at[1, z, d],
            "expert", lax.rem(me_e + d, experts),
        )

    def swap_copy(src, dst, sems, d, arriving):
        to = lax.rem(me_e + d, experts)
        place = lax.rem(me_e + experts - d, experts) if arriving else me_e
        return remote(src.at[to], dst.at[place], sems.at[0, d], sems.at[1, d], "expert", to)

    greet((("expert", experts), ("tensor", tensor)))
    each(tensor, lambda d: piece_copy(d, False).start())
    line_in = Line(tensor, w_in_own, w_in_all, in_sems.at[0], in_sems.at[1])
    line_back = Line(tensor, w_back_own, w_back_all, back_sems.at[0], back_sems.at[1])
    line_in.start(0)
    line_back.start(0)
    keep = [
        pltpu.make_async_copy(w_own_ref, w_ref.at[me_t], own_sem.at[0]),
        pltpu.make_async_copy(w_in_own, w_in_all.at[me_t], own_sem.at[1]),
        pltpu.make_async_copy(w_back_own, w_back_all.at[me_t], own_sem.at[2]),
    ]
    for copy in keep:
        copy.start()

    lane = ids(noise_ref.shape, 1)
    noise = noise_ref[...]
    high = noise.astype(BF)
    rest = noise - high.astype(F32)
    middle = rest.astype(BF)
    low = (rest - middle.astype(F32)).astype(BF)
    parts = jnp.where(
        lane < experts,
        high.astype(F32),
        jnp.where(
            lane < 2 * experts,
            middle.astype(F32),
            jnp.where(lane < 3 * experts, low.astype(F32), noise),
        ),
    ).astype(BF)
    slots_ref[...] = slots_by_lane(routes_t_ref[...], experts)
    count = send_ref.shape[1]
    place = ids((count, slots_ref.shape[1]), 0).astype(F32)

    def pick_rows(rows, out_ref, dst, sems, own_copy):
        for d in range(1, experts + 1):
            e = lax.rem(me_e + d, experts)
            pick = (place == slots_ref[pl.ds(e, 1), :]).astype(F32).astype(BF)
            out_ref[e] = mm(pick, rows).astype(BF)
            if d < experts:
                swap_copy(out_ref, dst, sems, d, False).start()
            else:
                own_copy.start()

    def forward_piece(z):
        piece_copy(z, True).wait_recv()
        each(experts, lambda d: plane_copy(z, d, False).start())

    each(tensor, forward_piece)
    own_early = pltpu.make_async_copy(early_send.at[me_e], early_ref.at[me_e], own_sem.at[3])
    pick_rows(
        jnp.concatenate([cot_ref[...], parts], axis=1), early_send, early_ref, early_sems, own_early
    )
    x = x_ref[...].astype(F32)
    unit1, _ = unit_norm(x)
    normed1 = (unit1 * gain1_ref[...]).astype(BF)
    line_in.arrive(0)
    line_in.start(1)
    line_back.arrive(0)
    line_back.start(1)
    keep[0].wait()
    each(tensor, lambda z: each(experts, lambda d: plane_copy(z, d, True).wait_recv()))

    lane = ids((SP, width), 1) // HD
    live = ids((SP, SP), 1) < SEQ
    for t in range(tensor):
        qkv_ref[t] = mm(normed1, w_ref[t, :, 0 : 3 * width]).astype(BF)
        for i in range(images):
            rows = slice(i * SP, (i + 1) * SP)
            q = qkv_ref[t, rows, 0:width]
            k = qkv_ref[t, rows, width : 2 * width]
            v = qkv_ref[t, rows, 2 * width : 3 * width]
            mixed = None
            for j in range(heads):
                q_j = q if heads == 1 else jnp.where(lane == j, q, jnp.zeros_like(q))
                scores = mm(q_j, k, NT) * HD ** (-0.5)
                scores = jnp.where(live, scores, -1e30)
                power = jnp.exp(scores - jnp.max(scores, -1, keepdims=True))
                attend = (power / jnp.sum(power, -1, keepdims=True)).astype(BF)
                attend_ref[i, t * heads + j] = attend
                part = mm(attend, v)
                mixed = part if mixed is None else jnp.where(lane == j, part, mixed)
            mixed_ref[t, rows, :] = mixed.astype(BF)
    residual = x
    for t in range(tensor):
        residual = residual + mm(mixed_ref[t], w_ref[t, :, 3 * width : wide], NT)
    residual_ref[...] = residual
    unit2, _ = unit_norm(residual)
    normed2 = (unit2 * gain2_ref[...]).astype(BF)
    own_route = pltpu.make_async_copy(send_ref.at[me_e], routed_ref.at[me_e], own_sem.at[4])
    pick_rows(normed2, send_ref, routed_ref, route_sems, own_route)

    for step in range(1, tensor - 1):
        for line in (line_in, line_back):
            line.arrive(step)
            if step + 1 < tensor - 1:
                line.start(step + 1)
    each(tensor, lambda d: piece_copy(d, False).wait_send())
    each(tensor, lambda z: each(experts, lambda d: plane_copy(z, d, False).wait_send()))

    def swapped(d):
        swap_copy(early_send, early_ref, early_sems, d, False).wait_send()
        swap_copy(early_send, early_ref, early_sems, d, True).wait_recv()
        swap_copy(send_ref, routed_ref, route_sems, d, False).wait_send()
        swap_copy(send_ref, routed_ref, route_sems, d, True).wait_recv()

    each(experts, swapped)
    line_in.finish()
    line_back.finish()
    for copy in [keep[1], keep[2], own_early, own_route]:
        copy.wait()


def gelu_parts(pre):
    density = jnp.exp(pre * pre * -0.5)
    size = jnp.abs(pre) * (0.5**0.5)
    t = 1.0 / (1.0 + 0.3275911 * size)
    series = t * (
        0.254829592
        + t * (-0.284496736 + t * (1.421413741 + t * (-1.453152027 + t * 1.061405429)))
    )
    tail = 0.5 * series * density
    return jnp.where(pre < 0, tail, 1.0 - tail), density * 0.3989422804014327


def expert_kernel(
    experts, own_ref, count_ref, x_in, early_in, w_router_ref, w_in_ref, w_back_ref,
    out_ref, back_ref, grads_ref, router_grad_ref,
    xs, es, dexp, hidden, dpre, outs, backs, total,
):
    sources, slots, _ = x_in.shape
    parts = w_in_ref.shape[0]
    width = w_in_ref.shape[2]
    own = own_ref[0]

    base = jnp.int32(0)
    for s in range(sources):
        tiles = (count_ref[s] + TILE - 1) // TILE

        def copy_in(j, _, s=s, base=base):
            to = pl.ds(pl.multiple_of((base + j) * TILE, TILE), TILE)
            at = pl.ds(pl.multiple_of(j * TILE, TILE), TILE)
            xs[to, :] = x_in[s, at, :]
            es[to, :] = early_in[s, at, :]
            return 0

        lax.fori_loop(0, tiles, copy_in, 0)
        base = base + tiles
    per = CHUNK // TILE
    chunks = (base + per - 1) // per

    def clear(j, _):
        to = pl.ds(pl.multiple_of(j * TILE, TILE), TILE)
        xs[to, :] = jnp.zeros((TILE, xs.shape[1]), BF)
        es[to, :] = jnp.zeros((TILE, es.shape[1]), BF)
        return 0

    lax.fori_loop(base, chunks * per, clear, 0)

    lane = ids((CHUNK, LANES), 1)
    fold_from, fold_to = ids((LANES, LANES), 0), ids((LANES, LANES), 1)
    fold = (
        (fold_from < 3 * experts) & (lax.rem(fold_from, experts) == fold_to)
    ).astype(F32).astype(BF)
    router_grad_ref[...] = jnp.zeros_like(router_grad_ref)

    def rows_of(c):
        return pl.ds(pl.multiple_of(c * CHUNK, CHUNK), CHUNK)

    def forward(c, _):
        rows = rows_of(c)
        x = xs[rows, :]
        cot = es[rows, 0:D].astype(F32)
        logits = mm(x, w_router_ref[...]) + mm(es[rows, D : D + LANES], fold)
        logits = jnp.where(lane < experts, logits, -1e30)
        power = jnp.exp(logits - jnp.max(logits, -1, keepdims=True))
        router = power / jnp.sum(power, -1, keepdims=True)
        mine = lane == own
        gate = jnp.sum(jnp.where(mine, router, 0.0), -1, keepdims=True)
        d_exp = (gate * cot).astype(BF)
        dexp[rows, :] = d_exp
        out = jnp.zeros((CHUNK, D), F32)
        back = jnp.zeros((CHUNK, D), F32)
        for f in range(parts):
            pre = mm(x, w_in_ref[f])
            normal, density = gelu_parts(pre)
            low = (pre * normal).astype(BF)
            hidden[f, rows, :] = low
            w_b = w_back_ref[f]
            out = out + mm(low, w_b)
            d_pre = (mm(d_exp, w_b, NT) * (normal + pre * density)).astype(BF)
            dpre[f, rows, :] = d_pre
            back = back + mm(d_pre, w_in_ref[f], NT)
        out = out.astype(BF).astype(F32)
        outs[rows, :] = (gate * out).astype(BF)
        d_gate = jnp.sum(cot * out, -1, keepdims=True)
        d_logits = (d_gate * gate * (mine.astype(F32) - router)).astype(BF)
        backs[rows, :] = (back + mm(d_logits, w_router_ref[...], NT)).astype(BF)
        router_grad_ref[...] += mm(x, d_logits, TN)
        return 0

    lax.fori_loop(0, chunks, forward, 0)

    def grads(f, _):
        def add_in(c, _):
            total[0] += mm(xs[rows_of(c), :], dpre[f, rows_of(c), :], TN)
            total[1] += mm(dexp[rows_of(c), :], hidden[f, rows_of(c), :], TN)
            return 0

        total[...] = jnp.zeros_like(total)
        lax.fori_loop(0, chunks, add_in, 0)
        grads_ref[f] = total[...].astype(BF)
        return 0

    lax.fori_loop(0, parts, grads, 0)

    base = jnp.int32(0)
    for s in range(sources):
        tiles = (count_ref[s] + TILE - 1) // TILE

        def copy_out(j, _, s=s, base=base):
            at = pl.ds(pl.multiple_of((base + j) * TILE, TILE), TILE)
            to = pl.ds(pl.multiple_of(j * TILE, TILE), TILE)
            out_ref[s, to, :] = outs[at, :]
            back_ref[s, to, :] = backs[at, :]
            return 0

        def clear_out(j, _, s=s):
            to = pl.ds(pl.multiple_of(j * TILE, TILE), TILE)
            out_ref[s, to, :] = jnp.zeros((TILE, D), BF)
            back_ref[s, to, :] = jnp.zeros((TILE, D), BF)
            return 0

        lax.fori_loop(0, tiles, copy_out, 0)
        lax.fori_loop(tiles, slots // TILE, clear_out, 0)
        base = base + tiles


def backward_kernel(
    experts, images, routes_ref, back_ref, residual_ref, cot_ref, x_ref, gain1_ref, gain2_ref,
    w_ref, qkv_ref, attend_ref, mixed_ref,
    tokens_grad_ref, w_grad_ref, norm1_ref, norm2_ref, d_qkv_ref,
):
    groups, _, wide = w_ref.shape
    width = wide // 4
    heads = width // HD
    slots = slots_by_row(routes_ref[...], experts)
    d_normed2 = take_rows(slots, back_ref, experts)
    unit2, inverse2 = unit_norm(residual_ref[...])
    d_rows, norm2 = norm_back(d_normed2, unit2, inverse2, gain2_ref[...])
    norm2_ref[...] = norm2
    d_residual = cot_ref[...].astype(F32) + d_rows
    tokens_grad_ref[...] = d_residual
    d_attention = d_residual.astype(BF)
    x = x_ref[...].astype(F32)
    unit1, inverse1 = unit_norm(x)
    normed1 = (unit1 * gain1_ref[...]).astype(BF)
    lane = ids((SP, width), 1) // HD
    scaling = HD ** (-0.5)
    d_normed1 = None
    for t in range(groups):
        w_grad_ref[t, :, 3 * width : wide] = mm(d_attention, mixed_ref[t], TN).astype(BF)
        d_mixed = mm(d_attention, w_ref[t, :, 3 * width : wide]).astype(BF)
        for i in range(images):
            rows = slice(i * SP, (i + 1) * SP)
            q = qkv_ref[t, rows, 0:width]
            k = qkv_ref[t, rows, width : 2 * width]
            v = qkv_ref[t, rows, 2 * width : 3 * width]
            do = d_mixed[rows]
            dq = dk = dv = None
            for j in range(heads):
                own = lane == j
                do_j = do if heads == 1 else jnp.where(own, do, jnp.zeros_like(do))
                q_j = q if heads == 1 else jnp.where(own, q, jnp.zeros_like(q))
                attend_low = attend_ref[i, t * heads + j]
                attend = attend_low.astype(F32)
                part_v = mm(attend_low, do_j, TN)
                d_attend = mm(do_j, v, NT)
                inner = jnp.sum(attend * d_attend, -1, keepdims=True)
                ds = (attend * (d_attend - inner)).astype(BF)
                part_q = mm(ds, k) * scaling
                part_k = mm(ds, q_j, TN) * scaling
                dq = part_q if dq is None else jnp.where(own, part_q, dq)
                dk = part_k if dk is None else dk + part_k
                dv = part_v if dv is None else dv + part_v
            d_qkv_ref[rows, 0:width] = dq.astype(BF)
            d_qkv_ref[rows, width : 2 * width] = dk.astype(BF)
            d_qkv_ref[rows, 2 * width : 3 * width] = dv.astype(BF)
        d_t = d_qkv_ref[...]
        w_grad_ref[t, :, 0 : 3 * width] = mm(normed1, d_t, TN).astype(BF)
        part = mm(d_t, w_ref[t, :, 0 : 3 * width], NT)
        d_normed1 = part if d_normed1 is None else d_normed1 + part
    d_rows, norm1 = norm_back(d_normed1, unit1, inverse1, gain1_ref[...])
    norm1_ref[...] = norm1
    tokens_grad_ref[...] += d_rows


def output_kernel(experts, routes_ref, out_in, residual_ref, output_ref):
    slots = slots_by_row(routes_ref[...], experts)
    output_ref[...] = (residual_ref[...] + take_rows(slots, out_in, experts)).astype(BF)


def per_device(
    tokens, norm1_gain, w_qkv, w_out, norm2_gain, w_router, noise, routes, w_in, w_back, cotangent
):
    own_rows = tokens.shape[0]
    experts = noise.shape[1]
    tensor = lax.axis_size("tensor")
    images = own_rows // SEQ
    rows = images * SP
    capacity = (2 * own_rows * TOP + experts - 1) // experts
    slots = up(capacity, TILE)
    width = w_out.shape[0]
    hidden = w_in.shape[2]

    def padded(a, fill=0):
        a = a.reshape(images, SEQ, a.shape[1])
        a = jnp.pad(a, ((0, 0), (0, SP - SEQ), (0, 0)), constant_values=fill)
        return a.reshape(rows, a.shape[2])

    def own(a):
        return a.reshape(images, SP, a.shape[1])[:, :SEQ].reshape(own_rows, a.shape[1])

    w_own = jnp.concatenate([w_qkv.reshape(D, 3 * width), w_out.T], axis=1)
    x = padded(tokens)
    cot = padded(cotangent)
    routes_p = padded(routes, -1)
    routes_t = routes_p.T
    spread = jnp.concatenate(
        [noise] * 3
        + [jnp.ones((own_rows, 1), F32), jnp.zeros((own_rows, LANES - 3 * experts - 1), F32)],
        axis=1,
    )
    gain1, gain2 = norm1_gain.reshape(1, D), norm2_gain.reshape(1, D)
    heads = tensor * width // HD
    dma = pltpu.SemaphoreType.DMA
    w_all, qkv, attend, mixed, residual, routed, early, w_in_all, w_back_all = call(
        functools.partial(forward_kernel, experts, tensor, images),
        (
            shape((tensor, D, 4 * width)),
            shape((tensor, rows, 3 * width)),
            shape((images, heads, SP, SP)),
            shape((tensor, rows, width)),
            shape((rows, D), F32),
            shape((experts, slots, D)),
            shape((experts, slots, D + LANES)),
            shape((tensor, D, hidden)),
            shape((tensor, hidden, D)),
        ),
        scratch=(
            pltpu.VMEM((experts, rows), F32),
            pltpu.VMEM((experts, slots, D), BF),
            pltpu.VMEM((experts, slots, D + LANES), BF),
            dma((5,)),
            dma((2, tensor)),
            dma((2, tensor, experts)),
            dma((2, experts)),
            dma((2, experts)),
            dma((2, 2, tensor - 1)),
            dma((2, 2, tensor - 1)),
        ),
        flops=2 * rows * D * D * 4,
        moved=20_000_000,
        far_in=(6, 7, 8),
        far_out=(5, 6, 7, 8),
        collective_id=0,
        has_side_effects=True,
    )(routes_t, x, cot, padded(spread), gain1, gain2, w_own, w_in[0], w_back[0])
    counts = jnp.sum(early[:, :, D + 3 * experts].astype(F32), axis=1).astype(jnp.int32)

    w_router_wide = jnp.pad(w_router, ((0, 0), (0, LANES - experts)))
    most = up(experts * slots, CHUNK)
    own_expert = lax.axis_index("expert").astype(jnp.int32).reshape(1)
    outs, backs, grads, router_grad = call(
        functools.partial(expert_kernel, experts),
        (
            shape((experts, slots, D)),
            shape((experts, slots, D)),
            shape((tensor, 2, D, hidden)),
            shape((D, LANES), F32),
        ),
        scratch=(
            pltpu.VMEM((most, D), BF),
            pltpu.VMEM((most, D + LANES), BF),
            pltpu.VMEM((most, D), BF),
            pltpu.VMEM((tensor, most, hidden), BF),
            pltpu.VMEM((tensor, most, hidden), BF),
            pltpu.VMEM((most, D), BF),
            pltpu.VMEM((most, D), BF),
            pltpu.VMEM((2, D, hidden), F32),
        ),
        flops=12 * experts * slots * D * tensor * hidden,
        moved=20_000_000,
        prefetch=(0, 1),
    )(own_expert, counts, routed, early, w_router_wide, w_in_all, w_back_all)

    returned = lax.all_to_all(backs, "expert", split_axis=0, concat_axis=0, tiled=True)
    returned_out = lax.all_to_all(outs, "expert", split_axis=0, concat_axis=0, tiled=True)
    grads = lax.psum_scatter(grads, "tensor", scatter_dimension=0, tiled=True)[0]

    grad_tokens, w_grad, norm1, norm2 = call(
        functools.partial(backward_kernel, experts, images),
        (
            shape((rows, D), F32),
            shape((tensor, D, 4 * width)),
            shape((1, D), F32),
            shape((1, D), F32),
        ),
        scratch=(pltpu.VMEM((rows, 3 * width), BF),),
        flops=2 * rows * D * D * 10,
        moved=10_000_000,
    )(routes_p, returned, residual, cot, x, gain1, gain2, w_all, qkv, attend, mixed)
    (output,) = call(functools.partial(output_kernel, experts), (shape((rows, D)),))(
        routes_p, returned_out, residual
    )
    w_grad = lax.psum_scatter(w_grad, "tensor", scatter_dimension=0, tiled=True)[0]
    w_grad = lax.psum(w_grad, "expert").astype(F32)
    router_grad, norm1, norm2 = lax.psum(
        (router_grad[:, :experts], norm1, norm2), ("expert", "tensor")
    )
    return (
        own(output),
        own(grad_tokens),
        norm1.reshape(D),
        w_grad[:, : 3 * width].reshape(D, 3, width),
        w_grad[:, 3 * width :].T,
        norm2.reshape(D),
        router_grad,
        grads[0].astype(F32)[None],
        grads[1].T.astype(F32)[None],
    )


def solution(mesh):
    rows = P(("expert", "tensor"), None)
    placed = (
        rows,
        P(),
        P(None, None, "tensor"),
        P("tensor", None),
        P(),
        P(),
        rows,
        rows,
        P("expert", None, "tensor"),
        P("expert", "tensor", None),
        rows,
    )
    return jax.shard_map(
        per_device,
        mesh=mesh,
        in_specs=placed,
        out_specs=(
            rows,
            rows,
            P(),
            P(None, None, "tensor"),
            P("tensor", None),
            P(),
            P(),
            P("expert", None, "tensor"),
            P("expert", "tensor", None),
        ),
        check_vma=False,
    )
```

```python
import functools

import jax
import jax.numpy as jnp
from jax import lax
from jax.experimental import pallas as pl
from jax.experimental.pallas import tpu as pltpu
from jax.sharding import PartitionSpec as P

D = 512
HD = 64
TOP = 2
SEQ = 197
LANES = 128
TILE = 16
CHUNK = 256
EPSILON = 1e-06
BF = jnp.bfloat16
F32 = jnp.float32
VMEM_BYTES = 56 * 1024 * 1024

NN = (((1,), (0,)), ((), ()))
NT = (((1,), (1,)), ((), ()))
TN = (((0,), (0,)), ((), ()))


def up(value, unit):
    return (value + unit - 1) // unit * unit


SP = up(SEQ, TILE)


def mm(a, b, dims=NN):
    return lax.dot_general(a, b, dims, preferred_element_type=F32)


def call(
    body, out_shape, scratch=(), flops=0, moved=0, prefetch=(), far_in=(), far_out=(), **more
):
    params = pltpu.CompilerParams(vmem_limit_bytes=VMEM_BYTES, **more)
    cost = pl.CostEstimate(flops=flops, bytes_accessed=moved, transcendentals=0)

    def spec(place, far, scalar=()):
        if place in scalar:
            return pl.BlockSpec(memory_space=pltpu.SMEM)
        return pl.BlockSpec(memory_space=pl.ANY if place in far else pltpu.VMEM)

    def run(*args):
        return pl.pallas_call(
            body,
            out_shape=out_shape,
            in_specs=[spec(place, far_in, prefetch) for place in range(len(args))],
            out_specs=tuple(spec(place, far_out) for place in range(len(out_shape))),
            scratch_shapes=list(scratch),
            compiler_params=params,
            cost_estimate=cost,
        )(*args)

    return run


def shape(dims, dtype=BF):
    return jax.ShapeDtypeStruct(dims, dtype)


def unit_norm(values):
    center = values - jnp.mean(values, -1, keepdims=True)
    spread = jnp.mean(center * center, -1, keepdims=True)
    inverse = lax.rsqrt(spread + EPSILON)
    return center * inverse, inverse


def norm_back(grad_rows, normed, inverse, gain):
    scaled = grad_rows * gain
    inner = (
        scaled
        - jnp.mean(scaled, -1, keepdims=True)
        - normed * jnp.mean(scaled * normed, -1, keepdims=True)
    )
    return inverse * inner, jnp.sum(grad_rows * normed, axis=0, keepdims=True)


def ids(shape_of, dim):
    return lax.broadcasted_iota(jnp.int32, shape_of, dim)


def slots_by_lane(routes_t, experts):
    rows = routes_t.shape[1]
    which = ids((experts, rows), 0)
    named = (routes_t[0:1] == which) | (routes_t[1:2] == which)
    before = (ids((rows, rows), 0) < ids((rows, rows), 1)).astype(F32).astype(BF)
    rank = mm(named.astype(F32).astype(BF), before)
    return jnp.where(named, rank, -1.0)


def slots_by_row(routes, experts):
    rows = routes.shape[0]
    which = ids((rows, experts), 1)
    named = (routes[:, 0:1] == which) | (routes[:, 1:2] == which)
    before = (ids((rows, rows), 1) < ids((rows, rows), 0)).astype(F32).astype(BF)
    rank = mm(before, named.astype(F32).astype(BF))
    return jnp.where(named, rank, -1.0)


def send_rows(slots, rows, out_ref, experts):
    count = out_ref.shape[1]
    place = ids((count, rows.shape[0]), 0).astype(F32)
    for e in range(experts):
        pick = (place == slots[e : e + 1, :]).astype(F32).astype(BF)
        out_ref[e] = mm(pick, rows).astype(BF)


def take_rows(slots, in_ref, experts):
    count = in_ref.shape[1]
    rows = slots.shape[0]
    place = ids((rows, count), 1).astype(F32)
    total = None
    for e in range(experts):
        pick = (place == slots[:, e : e + 1]).astype(F32).astype(BF)
        part = mm(pick, in_ref[e])
        total = part if total is None else total + part
    return total


MESH = pl.DeviceIdType.MESH


def greet(axes):
    barrier = pltpu.get_barrier_semaphore()
    for name, size in axes:
        me = lax.axis_index(name)

        def hello(d, _, name=name, size=size, me=me):
            pl.semaphore_signal(
                barrier, inc=1, device_id={name: lax.rem(me + d, size)}, device_id_type=MESH
            )
            return 0

        lax.fori_loop(1, size, hello, 0)
    pl.semaphore_wait(barrier, sum(size - 1 for _, size in axes))


def remote(src, dst, send_sem, recv_sem, name, to):
    return pltpu.make_async_remote_copy(
        src_ref=src,
        dst_ref=dst,
        send_sem=send_sem,
        recv_sem=recv_sem,
        device_id={name: to},
        device_id_type=MESH,
    )


def each(size, step):
    def body(d, _):
        step(d)
        return 0

    lax.fori_loop(1, size, body, 0)


class Line:
    def __init__(self, size, own, everyone, send_sem, recv_sem):
        self.size, self.own, self.all = size, own, everyone
        self.send_sem, self.recv_sem = send_sem, recv_sem
        self.me = lax.axis_index("tensor")

    def copy(self, way, step, arriving):
        toward = 1 if way == 0 else -1
        owner = self.me - toward * (step + (1 if arriving else 0))
        src = self.own if step == 0 else self.all.at[owner]
        return remote(
            src, self.all.at[owner], self.send_sem.at[way, step], self.recv_sem.at[way, step],
            "tensor", self.me + toward,
        )

    def sends(self, way, step):
        last = self.size - 1
        if way == 0:
            return (self.me >= step) & (self.me < last)
        return (self.me <= last - step) & (self.me > 0)

    def receives(self, way, step):
        if way == 0:
            return self.me >= step + 1
        return self.me <= self.size - 2 - step

    def start(self, step):
        for way in (0, 1):
            pl.when(self.sends(way, step))(lambda way=way: self.copy(way, step, False).start())

    def arrive(self, step):
        for way in (0, 1):
            pl.when(self.receives(way, step))(
                lambda way=way: self.copy(way, step, True).wait_recv()
            )

    def finish(self):
        for step in range(self.size - 1):
            for way in (0, 1):
                pl.when(self.sends(way, step))(
                    lambda way=way, step=step: self.copy(way, step, False).wait_send()
                )


def forward_kernel(
    experts, tensor, images, routes_t_ref, x_ref, cot_ref, noise_ref, gain1_ref, gain2_ref,
    w_own_ref, w_in_own, w_back_own,
    w_ref, qkv_ref, attend_ref, mixed_ref, residual_ref, routed_ref, early_ref, w_in_all, w_back_all,
    slots_ref, send_ref, early_send, own_sem, piece_sems, plane_sems, early_sems, route_sems,
    in_sems, back_sems,
):
    wide = w_own_ref.shape[1]
    width = wide // 4
    heads = width // HD
    me_e, me_t = lax.axis_index("expert"), lax.axis_index("tensor")
    piece = D // experts
    mine = pl.ds(pl.multiple_of(me_e * piece, piece), piece)

    def piece_copy(d, arriving):
        owner = lax.rem(me_t + tensor - d, tensor) if arriving else me_t
        return remote(
            w_own_ref.at[mine], w_ref.at[owner, mine], piece_sems.at[0, d], piece_sems.at[1, d],
            "tensor", lax.rem(me_t + d, tensor),
        )

    def plane_copy(z, d, arriving):
        owner = lax.rem(me_t + tensor - z, tensor)
        other = lax.rem(me_e + experts - d, experts) if arriving else me_e
        rows = pl.ds(pl.multiple_of(other * piece, piece), piece)
        block = w_ref.at[owner, rows]
        return remote(
            block, block, plane_sems.at[0, z, d], plane_sems.at[1, z, d],
            "expert", lax.rem(me_e + d, experts),
        )

    def swap_copy(src, dst, sems, d, arriving):
        to = lax.rem(me_e + d, experts)
        place = lax.rem(me_e + experts - d, experts) if arriving else me_e
        return remote(src.at[to], dst.at[place], sems.at[0, d], sems.at[1, d], "expert", to)

    greet((("expert", experts), ("tensor", tensor)))
    each(tensor, lambda d: piece_copy(d, False).start())
    line_in = Line(tensor, w_in_own, w_in_all, in_sems.at[0], in_sems.at[1])
    line_back = Line(tensor, w_back_own, w_back_all, back_sems.at[0], back_sems.at[1])
    line_in.start(0)
    line_back.start(0)
    keep = [
        pltpu.make_async_copy(w_own_ref, w_ref.at[me_t], own_sem.at[0]),
        pltpu.make_async_copy(w_in_own, w_in_all.at[me_t], own_sem.at[1]),
        pltpu.make_async_copy(w_back_own, w_back_all.at[me_t], own_sem.at[2]),
    ]
    for copy in keep:
        copy.start()

    lane = ids(noise_ref.shape, 1)
    noise = noise_ref[...]
    high = noise.astype(BF)
    rest = noise - high.astype(F32)
    middle = rest.astype(BF)
    low = (rest - middle.astype(F32)).astype(BF)
    parts = jnp.where(
        lane < experts,
        high.astype(F32),
        jnp.where(
            lane < 2 * experts,
            middle.astype(F32),
            jnp.where(lane < 3 * experts, low.astype(F32), noise),
        ),
    ).astype(BF)
    slots_ref[...] = slots_by_lane(routes_t_ref[...], experts)
    count = send_ref.shape[1]
    place = ids((count, slots_ref.shape[1]), 0).astype(F32)

    def pick_rows(rows, out_ref, dst, sems, own_copy):
        for d in range(1, experts + 1):
            e = lax.rem(me_e + d, experts)
            pick = (place == slots_ref[pl.ds(e, 1), :]).astype(F32).astype(BF)
            out_ref[e] = mm(pick, rows).astype(BF)
            if d < experts:
                swap_copy(out_ref, dst, sems, d, False).start()
            else:
                own_copy.start()

    def forward_piece(z):
        piece_copy(z, True).wait_recv()
        each(experts, lambda d: plane_copy(z, d, False).start())

    each(tensor, forward_piece)
    own_early = pltpu.make_async_copy(early_send.at[me_e], early_ref.at[me_e], own_sem.at[3])
    pick_rows(
        jnp.concatenate([cot_ref[...], parts], axis=1), early_send, early_ref, early_sems, own_early
    )
    x = x_ref[...].astype(F32)
    unit1, _ = unit_norm(x)
    normed1 = (unit1 * gain1_ref[...]).astype(BF)
    line_in.arrive(0)
    line_in.start(1)
    line_back.arrive(0)
    line_back.start(1)
    keep[0].wait()
    each(tensor, lambda z: each(experts, lambda d: plane_copy(z, d, True).wait_recv()))

    lane = ids((SP, width), 1) // HD
    live = ids((SP, SP), 1) < SEQ
    for t in range(tensor):
        qkv_ref[t] = mm(normed1, w_ref[t, :, 0 : 3 * width]).astype(BF)
        for i in range(images):
            rows = slice(i * SP, (i + 1) * SP)
            q = qkv_ref[t, rows, 0:width]
            k = qkv_ref[t, rows, width : 2 * width]
            v = qkv_ref[t, rows, 2 * width : 3 * width]
            mixed = None
            for j in range(heads):
                q_j = q if heads == 1 else jnp.where(lane == j, q, jnp.zeros_like(q))
                scores = mm(q_j, k, NT) * HD ** (-0.5)
                scores = jnp.where(live, scores, -1e30)
                power = jnp.exp(scores - jnp.max(scores, -1, keepdims=True))
                attend = (power / jnp.sum(power, -1, keepdims=True)).astype(BF)
                attend_ref[i, t * heads + j] = attend
                part = mm(attend, v)
                mixed = part if mixed is None else jnp.where(lane == j, part, mixed)
            mixed_ref[t, rows, :] = mixed.astype(BF)
    residual = x
    for t in range(tensor):
        residual = residual + mm(mixed_ref[t], w_ref[t, :, 3 * width : wide], NT)
    residual_ref[...] = residual
    unit2, _ = unit_norm(residual)
    normed2 = (unit2 * gain2_ref[...]).astype(BF)
    own_route = pltpu.make_async_copy(send_ref.at[me_e], routed_ref.at[me_e], own_sem.at[4])
    pick_rows(normed2, send_ref, routed_ref, route_sems, own_route)

    for step in range(1, tensor - 1):
        for line in (line_in, line_back):
            line.arrive(step)
            if step + 1 < tensor - 1:
                line.start(step + 1)
    each(tensor, lambda d: piece_copy(d, False).wait_send())
    each(tensor, lambda z: each(experts, lambda d: plane_copy(z, d, False).wait_send()))

    def swapped(d):
        swap_copy(early_send, early_ref, early_sems, d, False).wait_send()
        swap_copy(early_send, early_ref, early_sems, d, True).wait_recv()
        swap_copy(send_ref, routed_ref, route_sems, d, False).wait_send()
        swap_copy(send_ref, routed_ref, route_sems, d, True).wait_recv()

    each(experts, swapped)
    line_in.finish()
    line_back.finish()
    for copy in [keep[1], keep[2], own_early, own_route]:
        copy.wait()


def gelu_parts(pre):
    density = jnp.exp(pre * pre * -0.5)
    size = jnp.abs(pre) * (0.5**0.5)
    t = 1.0 / (1.0 + 0.3275911 * size)
    series = t * (
        0.254829592
        + t * (-0.284496736 + t * (1.421413741 + t * (-1.453152027 + t * 1.061405429)))
    )
    tail = 0.5 * series * density
    return jnp.where(pre < 0, tail, 1.0 - tail), density * 0.3989422804014327


def expert_kernel(
    experts, own_ref, count_ref, x_in, early_in, w_router_ref, w_in_ref, w_back_ref,
    out_ref, back_ref, grads_ref, router_grad_ref,
    xs, es, dexp, hidden, dpre, outs, backs, total,
):
    sources, slots, _ = x_in.shape
    parts = w_in_ref.shape[0]
    width = w_in_ref.shape[2]
    own = own_ref[0]

    base = jnp.int32(0)
    for s in range(sources):
        tiles = (count_ref[s] + TILE - 1) // TILE

        def copy_in(j, _, s=s, base=base):
            to = pl.ds(pl.multiple_of((base + j) * TILE, TILE), TILE)
            at = pl.ds(pl.multiple_of(j * TILE, TILE), TILE)
            xs[to, :] = x_in[s, at, :]
            es[to, :] = early_in[s, at, :]
            return 0

        lax.fori_loop(0, tiles, copy_in, 0)
        base = base + tiles
    per = CHUNK // TILE
    chunks = (base + per - 1) // per

    def clear(j, _):
        to = pl.ds(pl.multiple_of(j * TILE, TILE), TILE)
        xs[to, :] = jnp.zeros((TILE, xs.shape[1]), BF)
        es[to, :] = jnp.zeros((TILE, es.shape[1]), BF)
        return 0

    lax.fori_loop(base, chunks * per, clear, 0)

    lane = ids((CHUNK, LANES), 1)
    fold_from, fold_to = ids((LANES, LANES), 0), ids((LANES, LANES), 1)
    fold = (
        (fold_from < 3 * experts) & (lax.rem(fold_from, experts) == fold_to)
    ).astype(F32).astype(BF)
    router_grad_ref[...] = jnp.zeros_like(router_grad_ref)

    def rows_of(c):
        return pl.ds(pl.multiple_of(c * CHUNK, CHUNK), CHUNK)

    def forward(c, _):
        rows = rows_of(c)
        x = xs[rows, :]
        cot = es[rows, 0:D].astype(F32)
        logits = mm(x, w_router_ref[...]) + mm(es[rows, D : D + LANES], fold)
        logits = jnp.where(lane < experts, logits, -1e30)
        power = jnp.exp(logits - jnp.max(logits, -1, keepdims=True))
        router = power / jnp.sum(power, -1, keepdims=True)
        mine = lane == own
        gate = jnp.sum(jnp.where(mine, router, 0.0), -1, keepdims=True)
        d_exp = (gate * cot).astype(BF)
        dexp[rows, :] = d_exp
        out = jnp.zeros((CHUNK, D), F32)
        back = jnp.zeros((CHUNK, D), F32)
        for f in range(parts):
            pre = mm(x, w_in_ref[f])
            normal, density = gelu_parts(pre)
            low = (pre * normal).astype(BF)
            hidden[f, rows, :] = low
            w_b = w_back_ref[f]
            out = out + mm(low, w_b)
            d_pre = (mm(d_exp, w_b, NT) * (normal + pre * density)).astype(BF)
            dpre[f, rows, :] = d_pre
            back = back + mm(d_pre, w_in_ref[f], NT)
        out = out.astype(BF).astype(F32)
        outs[rows, :] = (gate * out).astype(BF)
        d_gate = jnp.sum(cot * out, -1, keepdims=True)
        d_logits = (d_gate * gate * (mine.astype(F32) - router)).astype(BF)
        backs[rows, :] = (back + mm(d_logits, w_router_ref[...], NT)).astype(BF)
        router_grad_ref[...] += mm(d_logits, x, TN)
        return 0

    lax.fori_loop(0, chunks, forward, 0)

    def grads(f, _):
        def add_in(c, _):
            total[0] += mm(xs[rows_of(c), :], dpre[f, rows_of(c), :], TN)
            total[1] += mm(dexp[rows_of(c), :], hidden[f, rows_of(c), :], TN)
            return 0

        total[...] = jnp.zeros_like(total)
        lax.fori_loop(0, chunks, add_in, 0)
        grads_ref[f] = total[...].astype(BF)
        return 0

    lax.fori_loop(0, parts, grads, 0)

    base = jnp.int32(0)
    for s in range(sources):
        tiles = (count_ref[s] + TILE - 1) // TILE

        def copy_out(j, _, s=s, base=base):
            at = pl.ds(pl.multiple_of((base + j) * TILE, TILE), TILE)
            to = pl.ds(pl.multiple_of(j * TILE, TILE), TILE)
            out_ref[s, to, :] = outs[at, :]
            back_ref[s, to, :] = backs[at, :]
            return 0

        def clear_out(j, _, s=s):
            to = pl.ds(pl.multiple_of(j * TILE, TILE), TILE)
            out_ref[s, to, :] = jnp.zeros((TILE, D), BF)
            back_ref[s, to, :] = jnp.zeros((TILE, D), BF)
            return 0

        lax.fori_loop(0, tiles, copy_out, 0)
        lax.fori_loop(tiles, slots // TILE, clear_out, 0)
        base = base + tiles


class Sums:
    def __init__(self, size, own, held, send_sem, recv_sem):
        self.size, self.own, self.held = size, own, held
        self.send_sem, self.recv_sem = send_sem, recv_sem
        self.me = lax.axis_index("tensor")

    def hops(self, way):
        return self.me if way == 0 else self.size - 1 - self.me

    def block(self, way, step):
        ahead = self.size - 1 + self.hops(way) - step
        return ahead if way == 0 else self.size - 1 - ahead

    def copy(self, way, step, part, first):
        toward = 1 if way == 0 else -1
        if first:
            src = self.own.at[self.block(way, step), part]
        else:
            src = self.held.at[way, max(step - 1, 0), part]
        return remote(
            src, self.held.at[way, step, part],
            self.send_sem.at[way, step, part], self.recv_sem.at[way, step, part],
            "tensor", self.me + toward,
        )

    def start_first(self):
        for step in range(self.size - 1):
            for part in (0, 1):
                for way in (0, 1):
                    pl.when(self.hops(way) == 0)(
                        lambda way=way, step=step, part=part: self.copy(
                            way, step, part, True
                        ).start()
                    )

    def middle(self, way, step):
        hops = self.hops(way)
        return (hops >= 1) & (hops <= step) & (hops < self.size - 1)

    def forward(self, step, part):
        for way in (0, 1):

            def go(way=way):
                self.copy(way, step - 1, part, False).wait_recv()
                held = self.held.at[way, step - 1, part]
                mine = self.own.at[self.block(way, step), part]
                add_into(held, mine)
                self.copy(way, step, part, False).start()

            pl.when(self.middle(way, step))(go)

    def last(self, part):
        for way in (0, 1):
            pl.when(self.hops(way) >= 1)(
                lambda way=way: self.copy(way, self.size - 2, part, False).wait_recv()
            )

    def finish(self):
        for part in (0, 1):
            for step in range(self.size - 1):
                for way in (0, 1):
                    sends = (self.hops(way) == 0) | self.middle(way, step)
                    pl.when(sends)(
                        lambda way=way, step=step, part=part: self.copy(
                            way, step, part, False
                        ).wait_send()
                    )


def add_into(held, mine):
    rows = held.shape[0]
    block = min(rows, 128)

    def body(r, _):
        at = pl.ds(pl.multiple_of(r * block, block), block)
        held[at, :] = (held[at, :].astype(F32) + mine[at, :].astype(F32)).astype(BF)
        return 0

    lax.fori_loop(0, rows // block, body, 0)


def backward_kernel(
    experts, tensor, images, routes_ref, residual_ref, cot_ref, x_ref, gain1_ref, gain2_ref,
    w_ref, qkv_ref, attend_ref, mixed_ref, grads_ref, router_ref, back_own, out_own,
    tokens_grad_ref, output_ref, w_sum_ref, small_sum_ref, in_grad_ref, back_grad_ref,
    d_qkv_ref, back_ref, out_ref, w_grad_ref, held, pieces, piece_send, piece_line,
    final_ref, small_ref, small_plane, small_line_send, small_line,
    own_sem, back_sems, out_sems, sum_send, sum_recv, w_sems, piece_sems, final_sems,
    small_sems, small_line_sems,
):
    wide = w_ref.shape[2]
    width = wide // 4
    heads = width // HD
    me_e, me_t = lax.axis_index("expert"), lax.axis_index("tensor")
    piece = D // experts
    mine = pl.ds(pl.multiple_of(me_e * piece, piece), piece)

    def place(d, arriving):
        return lax.rem(me_e + experts - d, experts) if arriving else me_e

    def swap_copy(src, dst, sems, d, arriving):
        to = lax.rem(me_e + d, experts)
        return remote(
            src.at[to], dst.at[place(d, arriving)], sems.at[0, d], sems.at[1, d], "expert", to
        )

    def w_copy(t, d, arriving):
        to = lax.rem(me_e + d, experts)
        rows = pl.ds(pl.multiple_of(to * piece, piece), piece)
        return remote(
            w_grad_ref.at[t, rows], pieces.at[place(d, arriving), t],
            w_sems.at[0, t, d], w_sems.at[1, t, d], "expert", to,
        )

    def line_copy(src, dst, sems, d, arriving):
        owner = lax.rem(me_t + tensor - d, tensor) if arriving else me_t
        return remote(
            src, dst.at[owner], sems.at[0, d], sems.at[1, d],
            "tensor", lax.rem(me_t + d, tensor),
        )

    def piece_copy(d, arriving):
        src = piece_send.at[lax.rem(me_t + d, tensor)]
        return line_copy(src, piece_line, piece_sems, d, arriving)

    def final_copy(d, arriving):
        rows = pl.ds(pl.multiple_of(place(d, arriving) * piece, piece), piece)
        block = final_ref.at[rows]
        return remote(
            block, block, final_sems.at[0, d], final_sems.at[1, d],
            "expert", lax.rem(me_e + d, experts),
        )

    def small_copy(d, arriving):
        return remote(
            small_ref, small_plane.at[place(d, arriving)], small_sems.at[0, d],
            small_sems.at[1, d], "expert", lax.rem(me_e + d, experts),
        )

    def small_line_copy(d, arriving):
        return line_copy(small_line_send, small_line, small_line_sems, d, arriving)

    greet((("expert", experts), ("tensor", tensor)))
    each(experts, lambda d: swap_copy(back_own, back_ref, back_sems, d, False).start())
    keep_back = pltpu.make_async_copy(back_own.at[me_e], back_ref.at[me_e], own_sem.at[0])
    keep_back.start()
    sums = Sums(tensor, grads_ref, held, sum_send, sum_recv)
    sums.start_first()

    slots = slots_by_row(routes_ref[...], experts)
    unit2, inverse2 = unit_norm(residual_ref[...])
    x = x_ref[...].astype(F32)
    unit1, inverse1 = unit_norm(x)
    normed1 = (unit1 * gain1_ref[...]).astype(BF)

    keep_back.wait()
    each(experts, lambda d: swap_copy(back_own, back_ref, back_sems, d, True).wait_recv())
    d_normed2 = take_rows(slots, back_ref, experts)
    d_rows, norm2 = norm_back(d_normed2, unit2, inverse2, gain2_ref[...])
    small_ref[...] = jnp.zeros_like(small_ref)
    small_ref[0:experts, :] = router_ref[0:experts, :]
    small_ref[experts + 1 : experts + 2, :] = norm2
    d_residual = cot_ref[...].astype(F32) + d_rows
    tokens_grad_ref[...] = d_residual
    d_attention = d_residual.astype(BF)
    lane = ids((SP, width), 1) // HD
    scaling = HD ** (-0.5)
    d_normed1 = None
    line_steps = [(step, part) for step in range(1, tensor - 1) for part in (0, 1)]
    for t in range(tensor):
        w_grad_ref[t, :, 3 * width : wide] = mm(d_attention, mixed_ref[t], TN).astype(BF)
        d_mixed = mm(d_attention, w_ref[t, :, 3 * width : wide]).astype(BF)
        for i in range(images):
            rows = slice(i * SP, (i + 1) * SP)
            q = qkv_ref[t, rows, 0:width]
            k = qkv_ref[t, rows, width : 2 * width]
            v = qkv_ref[t, rows, 2 * width : 3 * width]
            do = d_mixed[rows]
            dq = dk = dv = None
            for j in range(heads):
                own = lane == j
                do_j = do if heads == 1 else jnp.where(own, do, jnp.zeros_like(do))
                q_j = q if heads == 1 else jnp.where(own, q, jnp.zeros_like(q))
                attend_low = attend_ref[i, t * heads + j]
                attend = attend_low.astype(F32)
                part_v = mm(attend_low, do_j, TN)
                d_attend = mm(do_j, v, NT)
                inner = jnp.sum(attend * d_attend, -1, keepdims=True)
                ds = (attend * (d_attend - inner)).astype(BF)
                part_q = mm(ds, k) * scaling
                part_k = mm(ds, q_j, TN) * scaling
                dq = part_q if dq is None else jnp.where(own, part_q, dq)
                dk = part_k if dk is None else dk + part_k
                dv = part_v if dv is None else dv + part_v
            d_qkv_ref[t, rows, 0:width] = dq.astype(BF)
            d_qkv_ref[t, rows, width : 2 * width] = dk.astype(BF)
            d_qkv_ref[t, rows, 2 * width : 3 * width] = dv.astype(BF)
        w_grad_ref[t, :, 0 : 3 * width] = mm(normed1, d_qkv_ref[t], TN).astype(BF)
        each(experts, lambda d, t=t: w_copy(t, d, False).start())
        if t in (0, tensor // 2) and line_steps:
            sums.forward(*line_steps.pop(0))
    each(experts, lambda d: swap_copy(out_own, out_ref, out_sems, d, False).start())
    keep_out = pltpu.make_async_copy(out_own.at[me_e], out_ref.at[me_e], own_sem.at[1])
    keep_out.start()
    for t in range(tensor):
        part = mm(d_qkv_ref[t], w_ref[t, :, 0 : 3 * width], NT)
        d_normed1 = part if d_normed1 is None else d_normed1 + part
    d_rows, norm1 = norm_back(d_normed1, unit1, inverse1, gain1_ref[...])
    tokens_grad_ref[...] += d_rows
    small_ref[experts : experts + 1, :] = norm1
    each(experts, lambda d: small_copy(d, False).start())
    small_plane[me_e] = small_ref[...]

    for t in range(tensor):
        pieces[me_e, t] = w_grad_ref[t, mine, :]
    for t in range(tensor):
        each(experts, lambda d, t=t: w_copy(t, d, True).wait_recv())
        total = pieces[0, t].astype(F32)
        for e in range(1, experts):
            total = total + pieces[e, t].astype(F32)
        piece_send[t] = total.astype(BF)
    each(tensor, lambda d: piece_copy(d, False).start())
    piece_line[me_t] = piece_send[me_t]
    each(experts, lambda d: small_copy(d, True).wait_recv())
    total = small_plane[0]
    for e in range(1, experts):
        total = total + small_plane[e]
    small_line_send[...] = total
    each(tensor, lambda d: small_line_copy(d, False).start())
    small_line[me_t] = total
    if line_steps:
        sums.forward(*line_steps.pop(0))
    each(tensor, lambda d: piece_copy(d, True).wait_recv())
    total = piece_line[0].astype(F32)
    for t in range(1, tensor):
        total = total + piece_line[t].astype(F32)
    final_ref[mine, :] = total.astype(BF)
    each(experts, lambda d: final_copy(d, False).start())
    for step, part in line_steps:
        sums.forward(step, part)

    keep_out.wait()
    each(experts, lambda d: swap_copy(out_own, out_ref, out_sems, d, True).wait_recv())
    output_ref[...] = (residual_ref[...] + take_rows(slots, out_ref, experts)).astype(BF)
    each(tensor, lambda d: small_line_copy(d, True).wait_recv())
    total = small_line[0]
    for t in range(1, tensor):
        total = total + small_line[t]
    small_sum_ref[...] = total
    each(experts, lambda d: final_copy(d, True).wait_recv())
    w_sum_ref[...] = final_ref[...].astype(F32)

    for part in (0, 1):
        sums.last(part)
        total = grads_ref[me_t, part].astype(F32)
        for way in (0, 1):
            came = held[way, tensor - 2, part].astype(F32)
            total = total + jnp.where(sums.hops(way) >= 1, came, jnp.zeros_like(came))
        if part == 0:
            in_grad_ref[...] = total
        else:
            back_grad_ref[...] = total.T
    sums.finish()

    def sent(d):
        swap_copy(back_own, back_ref, back_sems, d, False).wait_send()
        swap_copy(out_own, out_ref, out_sems, d, False).wait_send()
        for t in range(tensor):
            w_copy(t, d, False).wait_send()
        final_copy(d, False).wait_send()
        small_copy(d, False).wait_send()

    each(experts, sent)

    def sent_line(d):
        piece_copy(d, False).wait_send()
        small_line_copy(d, False).wait_send()

    each(tensor, sent_line)


def per_device(
    tokens, norm1_gain, w_qkv, w_out, norm2_gain, w_router, noise, routes, w_in, w_back, cotangent
):
    own_rows = tokens.shape[0]
    experts = noise.shape[1]
    tensor = lax.axis_size("tensor")
    images = own_rows // SEQ
    rows = images * SP
    capacity = (2 * own_rows * TOP + experts - 1) // experts
    slots = up(capacity, TILE)
    width = w_out.shape[0]
    hidden = w_in.shape[2]

    def padded(a, fill=0):
        a = a.reshape(images, SEQ, a.shape[1])
        a = jnp.pad(a, ((0, 0), (0, SP - SEQ), (0, 0)), constant_values=fill)
        return a.reshape(rows, a.shape[2])

    def own(a):
        return a.reshape(images, SP, a.shape[1])[:, :SEQ].reshape(own_rows, a.shape[1])

    w_own = jnp.concatenate([w_qkv.reshape(D, 3 * width), w_out.T], axis=1)
    x = padded(tokens)
    cot = padded(cotangent)
    routes_p = padded(routes, -1)
    routes_t = routes_p.T
    spread = jnp.concatenate(
        [noise] * 3
        + [jnp.ones((own_rows, 1), F32), jnp.zeros((own_rows, LANES - 3 * experts - 1), F32)],
        axis=1,
    )
    gain1, gain2 = norm1_gain.reshape(1, D), norm2_gain.reshape(1, D)
    heads = tensor * width // HD
    dma = pltpu.SemaphoreType.DMA
    w_all, qkv, attend, mixed, residual, routed, early, w_in_all, w_back_all = call(
        functools.partial(forward_kernel, experts, tensor, images),
        (
            shape((tensor, D, 4 * width)),
            shape((tensor, rows, 3 * width)),
            shape((images, heads, SP, SP)),
            shape((tensor, rows, width)),
            shape((rows, D), F32),
            shape((experts, slots, D)),
            shape((experts, slots, D + LANES)),
            shape((tensor, D, hidden)),
            shape((tensor, hidden, D)),
        ),
        scratch=(
            pltpu.VMEM((experts, rows), F32),
            pltpu.VMEM((experts, slots, D), BF),
            pltpu.VMEM((experts, slots, D + LANES), BF),
            dma((5,)),
            dma((2, tensor)),
            dma((2, tensor, experts)),
            dma((2, experts)),
            dma((2, experts)),
            dma((2, 2, tensor - 1)),
            dma((2, 2, tensor - 1)),
        ),
        flops=2 * rows * D * D * 4,
        moved=20_000_000,
        far_in=(6, 7, 8),
        far_out=(5, 6, 7, 8),
        collective_id=0,
        has_side_effects=True,
    )(routes_t, x, cot, padded(spread), gain1, gain2, w_own, w_in[0], w_back[0])
    counts = jnp.sum(early[:, :, D + 3 * experts].astype(F32), axis=1).astype(jnp.int32)

    w_router_wide = jnp.pad(w_router, ((0, 0), (0, LANES - experts)))
    most = up(experts * slots, CHUNK)
    own_expert = lax.axis_index("expert").astype(jnp.int32).reshape(1)
    outs, backs, grads, router_grad = call(
        functools.partial(expert_kernel, experts),
        (
            shape((experts, slots, D)),
            shape((experts, slots, D)),
            shape((tensor, 2, D, hidden)),
            shape((LANES, D), F32),
        ),
        scratch=(
            pltpu.VMEM((most, D), BF),
            pltpu.VMEM((most, D + LANES), BF),
            pltpu.VMEM((most, D), BF),
            pltpu.VMEM((tensor, most, hidden), BF),
            pltpu.VMEM((tensor, most, hidden), BF),
            pltpu.VMEM((most, D), BF),
            pltpu.VMEM((most, D), BF),
            pltpu.VMEM((2, D, hidden), F32),
        ),
        flops=12 * experts * slots * D * tensor * hidden,
        moved=20_000_000,
        prefetch=(0, 1),
    )(own_expert, counts, routed, early, w_router_wide, w_in_all, w_back_all)

    small_rows = up(experts + 2, 8)
    piece = D // experts
    grad_tokens, output, w_sum, small, grad_in, grad_back = call(
        functools.partial(backward_kernel, experts, tensor, images),
        (
            shape((rows, D), F32),
            shape((rows, D)),
            shape((D, 4 * width), F32),
            shape((small_rows, D), F32),
            shape((D, hidden), F32),
            shape((hidden, D), F32),
        ),
        scratch=(
            pltpu.VMEM((tensor, rows, 3 * width), BF),
            pltpu.VMEM((experts, slots, D), BF),
            pltpu.VMEM((experts, slots, D), BF),
            pltpu.VMEM((tensor, D, 4 * width), BF),
            pltpu.VMEM((2, tensor - 1, 2, D, hidden), BF),
            pltpu.VMEM((experts, tensor, piece, 4 * width), BF),
            pltpu.VMEM((tensor, piece, 4 * width), BF),
            pltpu.VMEM((tensor, piece, 4 * width), BF),
            pltpu.VMEM((D, 4 * width), BF),
            pltpu.VMEM((small_rows, D), F32),
            pltpu.VMEM((experts, small_rows, D), F32),
            pltpu.VMEM((small_rows, D), F32),
            pltpu.VMEM((tensor, small_rows, D), F32),
            dma((2,)),
            dma((2, experts)),
            dma((2, experts)),
            dma((2, tensor - 1, 2)),
            dma((2, tensor - 1, 2)),
            dma((2, tensor, experts)),
            dma((2, tensor)),
            dma((2, experts)),
            dma((2, experts)),
            dma((2, tensor)),
        ),
        flops=2 * rows * D * D * 10,
        moved=20_000_000,
        far_in=(12, 13),
        collective_id=1,
        has_side_effects=True,
    )(
        routes_p, residual, cot, x, gain1, gain2, w_all, qkv, attend, mixed, grads, router_grad,
        backs, outs,
    )
    return (
        own(output),
        own(grad_tokens),
        small[experts],
        w_sum[:, : 3 * width].reshape(D, 3, width),
        w_sum[:, 3 * width :].T,
        small[experts + 1],
        small[:experts].T,
        grad_in[None],
        grad_back[None],
    )


def solution(mesh):
    rows = P(("expert", "tensor"), None)
    placed = (
        rows,
        P(),
        P(None, None, "tensor"),
        P("tensor", None),
        P(),
        P(),
        rows,
        rows,
        P("expert", None, "tensor"),
        P("expert", "tensor", None),
        rows,
    )
    return jax.shard_map(
        per_device,
        mesh=mesh,
        in_specs=placed,
        out_specs=(
            rows,
            rows,
            P(),
            P(None, None, "tensor"),
            P("tensor", None),
            P(),
            P(),
            P("expert", None, "tensor"),
            P("expert", "tensor", None),
        ),
        check_vma=False,
    )
```

```python
import functools

import jax
import jax.numpy as jnp
from jax import lax
from jax.experimental import pallas as pl
from jax.experimental.pallas import tpu as pltpu
from jax.sharding import PartitionSpec as P

D = 512
HD = 64
TOP = 2
SEQ = 197
LANES = 128
TILE = 16
EPSILON = 1e-06
BF = jnp.bfloat16
F32 = jnp.float32
VMEM_BYTES = 62 * 1024 * 1024

NN = (((1,), (0,)), ((), ()))
NT = (((1,), (1,)), ((), ()))
TN = (((0,), (0,)), ((), ()))


def up(value, unit):
    return (value + unit - 1) // unit * unit


SP = up(SEQ, TILE)


def mm(a, b, dims=NN):
    return lax.dot_general(a, b, dims, preferred_element_type=F32)


def call(
    body, out_shape, scratch=(), flops=0, moved=0, prefetch=(), far_in=(), far_out=(), **more
):
    params = pltpu.CompilerParams(vmem_limit_bytes=VMEM_BYTES, **more)
    cost = pl.CostEstimate(flops=flops, bytes_accessed=moved, transcendentals=0)

    def spec(place, far, scalar=()):
        if place in scalar:
            return pl.BlockSpec(memory_space=pltpu.SMEM)
        return pl.BlockSpec(memory_space=pl.ANY if place in far else pltpu.VMEM)

    def run(*args):
        return pl.pallas_call(
            body,
            out_shape=out_shape,
            in_specs=[spec(place, far_in, prefetch) for place in range(len(args))],
            out_specs=tuple(spec(place, far_out) for place in range(len(out_shape))),
            scratch_shapes=list(scratch),
            compiler_params=params,
            cost_estimate=cost,
        )(*args)

    return run


def shape(dims, dtype=BF):
    return jax.ShapeDtypeStruct(dims, dtype)


def unit_norm(values):
    center = values - jnp.mean(values, -1, keepdims=True)
    spread = jnp.mean(center * center, -1, keepdims=True)
    inverse = lax.rsqrt(spread + EPSILON)
    return center * inverse, inverse


def norm_back(grad_rows, normed, inverse, gain):
    scaled = grad_rows * gain
    inner = (
        scaled
        - jnp.mean(scaled, -1, keepdims=True)
        - normed * jnp.mean(scaled * normed, -1, keepdims=True)
    )
    return inverse * inner, jnp.sum(grad_rows * normed, axis=0, keepdims=True)


def ids(shape_of, dim):
    return lax.broadcasted_iota(jnp.int32, shape_of, dim)


def slots_by_row(routes, experts):
    rows = routes.shape[0]
    which = ids((rows, experts), 1)
    named = (routes[:, 0:1] == which) | (routes[:, 1:2] == which)
    before = (ids((rows, rows), 1) < ids((rows, rows), 0)).astype(F32).astype(BF)
    rank = mm(before, named.astype(F32).astype(BF))
    return jnp.where(named, rank, -1.0)


def take_rows(slots, in_ref, experts):
    count = in_ref.shape[1]
    rows = slots.shape[0]
    place = ids((rows, count), 1).astype(F32)
    total = None
    for e in range(experts):
        pick = (place == slots[:, e : e + 1]).astype(F32).astype(BF)
        part = mm(pick, in_ref[e])
        total = part if total is None else total + part
    return total


MESH = pl.DeviceIdType.MESH


def greet(axes):
    barrier = pltpu.get_barrier_semaphore()
    for name, size in axes:
        me = lax.axis_index(name)

        def hello(d, _, name=name, size=size, me=me):
            pl.semaphore_signal(
                barrier, inc=1, device_id={name: lax.rem(me + d, size)}, device_id_type=MESH
            )
            return 0

        lax.fori_loop(1, size, hello, 0)
    pl.semaphore_wait(barrier, sum(size - 1 for _, size in axes))


def remote(src, dst, send_sem, recv_sem, name, to):
    return pltpu.make_async_remote_copy(
        src_ref=src,
        dst_ref=dst,
        send_sem=send_sem,
        recv_sem=recv_sem,
        device_id={name: to},
        device_id_type=MESH,
    )


def each(size, step):
    def body(d, _):
        step(d)
        return 0

    lax.fori_loop(1, size, body, 0)


class Line:
    def __init__(self, size, own, everyone, send_sem, recv_sem):
        self.size, self.own, self.all = size, own, everyone
        self.send_sem, self.recv_sem = send_sem, recv_sem
        self.me = lax.axis_index("tensor")

    def copy(self, way, step, arriving):
        toward = 1 if way == 0 else -1
        owner = self.me - toward * (step + (1 if arriving else 0))
        src = self.own if step == 0 else self.all.at[owner]
        return remote(
            src, self.all.at[owner], self.send_sem.at[way, step], self.recv_sem.at[way, step],
            "tensor", self.me + toward,
        )

    def sends(self, way, step):
        last = self.size - 1
        if way == 0:
            return (self.me >= step) & (self.me < last)
        return (self.me <= last - step) & (self.me > 0)

    def receives(self, way, step):
        if way == 0:
            return self.me >= step + 1
        return self.me <= self.size - 2 - step

    def start(self, step):
        for way in (0, 1):
            pl.when(self.sends(way, step))(lambda way=way: self.copy(way, step, False).start())

    def arrive(self, step):
        for way in (0, 1):
            pl.when(self.receives(way, step))(
                lambda way=way: self.copy(way, step, True).wait_recv()
            )

    def finish(self):
        for step in range(self.size - 1):
            for way in (0, 1):
                pl.when(self.sends(way, step))(
                    lambda way=way, step=step: self.copy(way, step, False).wait_send()
                )


def gelu_parts(pre):
    density = jnp.exp(pre * pre * -0.5)
    size = jnp.abs(pre) * (0.5**0.5)
    t = 1.0 / (1.0 + 0.3275911 * size)
    series = t * (
        0.254829592
        + t * (-0.284496736 + t * (1.421413741 + t * (-1.453152027 + t * 1.061405429)))
    )
    tail = 0.5 * series * density
    return jnp.where(pre < 0, tail, 1.0 - tail), density * 0.3989422804014327


class Sums:
    def __init__(self, size, own, held, send_sem, recv_sem):
        self.size, self.own, self.held = size, own, held
        self.send_sem, self.recv_sem = send_sem, recv_sem
        self.me = lax.axis_index("tensor")

    def hops(self, way):
        return self.me if way == 0 else self.size - 1 - self.me

    def block(self, way, step):
        ahead = self.size - 1 + self.hops(way) - step
        return ahead if way == 0 else self.size - 1 - ahead

    def copy(self, way, step, part, first):
        toward = 1 if way == 0 else -1
        if first:
            src = self.own(self.block(way, step), part)
        else:
            src = self.held.at[way, max(step - 1, 0), part]
        return remote(
            src, self.held.at[way, step, part],
            self.send_sem.at[way, step, part], self.recv_sem.at[way, step, part],
            "tensor", self.me + toward,
        )

    def start_first(self, way, step):
        for part in (0, 1):
            pl.when(self.hops(way) == 0)(
                lambda part=part: self.copy(way, step, part, True).start()
            )

    def middle(self, way, step):
        hops = self.hops(way)
        return (hops >= 1) & (hops <= step) & (hops < self.size - 1)

    def forward(self, step, part):
        for way in (0, 1):

            def go(way=way):
                self.copy(way, step - 1, part, False).wait_recv()
                held = self.held.at[way, step - 1, part]
                mine = self.own(self.block(way, step), part)
                add_into(held, mine)
                self.copy(way, step, part, False).start()

            pl.when(self.middle(way, step))(go)

    def last(self, part):
        for way in (0, 1):
            pl.when(self.hops(way) >= 1)(
                lambda way=way: self.copy(way, self.size - 2, part, False).wait_recv()
            )

    def finish(self):
        for part in (0, 1):
            for step in range(self.size - 1):
                for way in (0, 1):
                    sends = (self.hops(way) == 0) | self.middle(way, step)
                    pl.when(sends)(
                        lambda way=way, step=step, part=part: self.copy(
                            way, step, part, False
                        ).wait_send()
                    )


def add_into(held, mine):
    rows = held.shape[0]
    block = min(rows, 128)

    def body(r, _):
        at = pl.ds(pl.multiple_of(r * block, block), block)
        held[at, :] = (held[at, :].astype(F32) + mine[at, :].astype(F32)).astype(BF)
        return 0

    lax.fori_loop(0, rows // block, body, 0)


def block_kernel(
    experts, tensor, images, group,
    routes_ref, tokens_ref, cotangent_ref, noise_ref, gain1_ref, gain2_ref, w_router_ref,
    w_own_ref, w_in_own, w_back_own,
    output_ref, tokens_grad_ref, w_sum_ref, small_sum_ref, in_grad_ref, back_grad_ref,
    w_ref, w_in_all, w_back_all, narrow, x_ref, cot_ref, rows_ref, lanes_ref,
    qkv_ref, attend_ref, mixed_ref, residual_ref, d_qkv_ref,
    send_ref, routed_ref, early_send, early_ref, noise_send, noise_all, router_ref,
    hidden_ref, slope_ref, back_ref, out_ref, held,
    w_grad_ref, pieces, piece_send, piece_line,
    small_ref, small_plane, small_line_send, small_line,
    own_sem, first_sems, plane_sems, in_sems, in_back_sems, route_sems, early_sems, noise_sems,
    back_sems, out_sems, sum_send, sum_recv, w_sems, piece_sems, final_sems,
    small_sems, small_line_sems,
):
    own_rows = tokens_ref.shape[0]
    wide = w_own_ref.shape[1]
    width = wide // 4
    heads = width // HD
    slots = send_ref.shape[1]
    parts = w_in_all.shape[0]
    chunk = group * slots
    me_e, me_t = lax.axis_index("expert"), lax.axis_index("tensor")
    piece = D // experts

    def rows_at(e):
        return pl.ds(pl.multiple_of(e * piece, piece), piece)

    mine = rows_at(me_e)

    def after(d):
        return lax.rem(me_e + d, experts)

    def place(d, arriving):
        return lax.rem(me_e + experts - d, experts) if arriving else me_e

    def swap_copy(src, dst, sems, d, arriving):
        to = after(d)
        return remote(
            src.at[to], dst.at[place(d, arriving)], sems.at[0, d], sems.at[1, d], "expert", to
        )

    def line_copy(src, dst, sems, d, arriving):
        owner = lax.rem(me_t + tensor - d, tensor) if arriving else me_t
        return remote(
            src, dst(owner), sems.at[0, d], sems.at[1, d],
            "tensor", lax.rem(me_t + d, tensor),
        )

    def first_copy(d, arriving):
        return line_copy(
            w_own_ref.at[mine], lambda owner: w_ref.at[owner, mine], first_sems, d, arriving
        )

    def plane_copy(z, d, arriving):
        owner = lax.rem(me_t + tensor - z, tensor)
        block = w_ref.at[owner, rows_at(place(d, arriving))]
        return remote(
            block, block, plane_sems.at[0, z, d], plane_sems.at[1, z, d], "expert", after(d)
        )

    def route_copy(d, arriving):
        return swap_copy(send_ref, routed_ref, route_sems, d, arriving)

    def early_copy(d, arriving):
        return swap_copy(early_send, early_ref, early_sems, d, arriving)

    def noise_copy(d, arriving):
        return swap_copy(noise_send, noise_all, noise_sems, d, arriving)

    def back_copy(d, arriving):
        return swap_copy(early_send, back_ref, back_sems, d, arriving)

    def out_copy(d, arriving):
        return swap_copy(send_ref, out_ref, out_sems, d, arriving)

    def w_copy(t, d, arriving):
        return remote(
            w_grad_ref.at[t, rows_at(after(d))], pieces.at[place(d, arriving), t],
            w_sems.at[0, t, d], w_sems.at[1, t, d], "expert", after(d),
        )

    def piece_copy(d, arriving):
        src = piece_send.at[lax.rem(me_t + d, tensor)]
        return line_copy(src, lambda owner: piece_line.at[owner], piece_sems, d, arriving)

    def final_copy(d, arriving):
        block = w_sum_ref.at[rows_at(place(d, arriving))]
        return remote(block, block, final_sems.at[0, d], final_sems.at[1, d], "expert", after(d))

    def small_copy(d, arriving):
        return remote(
            small_ref, small_plane.at[place(d, arriving)], small_sems.at[0, d],
            small_sems.at[1, d], "expert", after(d),
        )

    def small_line_copy(d, arriving):
        return line_copy(
            small_line_send, lambda owner: small_line.at[owner], small_line_sems, d, arriving
        )

    greet((("expert", experts), ("tensor", tensor)))
    each(tensor, lambda d: first_copy(d, False).start())
    line_in = Line(tensor, w_in_own, w_in_all, in_sems.at[0], in_sems.at[1])
    line_back = Line(tensor, w_back_own, w_back_all, in_back_sems.at[0], in_back_sems.at[1])
    line_in.start(0)
    keep = [
        pltpu.make_async_copy(w_own_ref, w_ref.at[me_t], own_sem.at[0]),
        pltpu.make_async_copy(w_in_own, w_in_all.at[me_t], own_sem.at[1]),
        pltpu.make_async_copy(w_back_own, w_back_all.at[me_t], own_sem.at[2]),
    ]
    for copy in keep:
        copy.start()

    def spread(compact, to_ref, fill=0.0):
        columns = compact.shape[1]
        narrow[0:own_rows, 0:columns] = compact
        to_ref[...] = jnp.full(to_ref.shape, fill, F32)
        for i in range(images):
            to_ref[i * SP : i * SP + SEQ, 0:columns] = narrow[
                i * SEQ : (i + 1) * SEQ, 0:columns
            ]

    def compact(padded):
        for i in range(images):
            narrow[i * SEQ : (i + 1) * SEQ, :] = padded[i * SP : i * SP + SEQ, :]
        return narrow[0:own_rows, :]

    spread(noise_ref[...], rows_ref)
    noise = rows_ref[...].T[0:experts, :]
    high = noise.astype(BF).astype(F32)
    middle = (noise - high).astype(BF).astype(F32)
    low = noise - high - middle
    noise_parts = [high, middle, low]
    if noise_send.shape[1] > 3 * experts:
        noise_parts.append(jnp.zeros((noise_send.shape[1] - 3 * experts, noise.shape[1]), F32))
    noise = jnp.concatenate(noise_parts, axis=0).astype(BF)
    spread(slots_by_row(routes_ref[...], experts), rows_ref, -1.0)
    lanes_ref[...] = rows_ref[...].T[0:experts, :]
    spread(cotangent_ref[...].astype(F32), cot_ref)
    cot_low = cot_ref[...].astype(BF)
    spot = ids((slots, lanes_ref.shape[1]), 0).astype(F32)

    def pick_of(e):
        return (spot == lanes_ref[pl.ds(e, 1), :]).astype(F32).astype(BF)

    def forward_piece(z):
        first_copy(z, True).wait_recv()
        each(experts, lambda d: plane_copy(z, d, False).start())

    each(tensor, forward_piece)
    for d in range(1, experts + 1):
        e = after(d)
        pick = pick_of(e)
        rows_of_e = mm(pick, cot_low).astype(BF)
        noise_of_e = mm(noise, pick, NT).astype(BF)
        if d < experts:
            early_send[e] = rows_of_e
            noise_send[e] = noise_of_e
            early_copy(d, False).start()
            noise_copy(d, False).start()
        else:
            early_ref[e] = rows_of_e
            noise_all[e] = noise_of_e
    spread(tokens_ref[...].astype(F32), x_ref)
    x = x_ref[...]
    unit1, inverse1 = unit_norm(x)
    normed1 = (unit1 * gain1_ref[...]).astype(BF)
    line_in.arrive(0)
    if tensor > 2:
        line_in.start(1)
    line_back.start(0)
    keep[0].wait()
    each(tensor, lambda z: each(experts, lambda d: plane_copy(z, d, True).wait_recv()))

    lane = ids((SP, width), 1) // HD
    live = ids((SP, SP), 1) < SEQ
    for t in range(tensor):
        qkv_ref[t] = mm(normed1, w_ref[t, :, 0 : 3 * width]).astype(BF)
        for i in range(images):
            rows = slice(i * SP, (i + 1) * SP)
            q = qkv_ref[t, rows, 0:width]
            k = qkv_ref[t, rows, width : 2 * width]
            v = qkv_ref[t, rows, 2 * width : 3 * width]
            mixed = None
            for j in range(heads):
                q_j = q if heads == 1 else jnp.where(lane == j, q, jnp.zeros_like(q))
                scores = mm(q_j, k, NT) * HD ** (-0.5)
                scores = jnp.where(live, scores, -1e30)
                power = jnp.exp(scores - jnp.max(scores, -1, keepdims=True))
                attend = (power / jnp.sum(power, -1, keepdims=True)).astype(BF)
                attend_ref[i, t * heads + j] = attend
                part = mm(attend, v)
                mixed = part if mixed is None else jnp.where(lane == j, part, mixed)
            mixed_ref[t, rows, :] = mixed.astype(BF)
        if t == tensor // 2 - 1 and tensor > 3:
            line_in.arrive(1)
            line_in.start(2)
    residual = x
    for t in range(tensor):
        residual = residual + mm(mixed_ref[t], w_ref[t, :, 3 * width : wide], NT)
    residual_ref[...] = residual
    unit2, inverse2 = unit_norm(residual)
    normed2 = (unit2 * gain2_ref[...]).astype(BF)
    for d in range(1, experts + 1):
        e = after(d)
        rows_of_e = mm(pick_of(e), normed2).astype(BF)
        if d < experts:
            send_ref[e] = rows_of_e
            route_copy(d, False).start()
        else:
            routed_ref[e] = rows_of_e
    done_in, done_back = (2 if tensor > 3 else 1), 0
    for step in range(tensor - 1):
        if step >= done_in:
            line_in.arrive(step)
            if step + 1 < tensor - 1:
                line_in.start(step + 1)
        if step < tensor - 2:
            line_back.arrive(step)
            line_back.start(step + 1)
    if done_in > tensor - 2:
        line_in.arrive(tensor - 2)
    keep[1].wait()

    fold_from, fold_to = ids((noise_all.shape[1], LANES), 0), ids((noise_all.shape[1], LANES), 1)
    fold = (
        (fold_from < 3 * experts) & (lax.rem(fold_from, experts) == fold_to)
    ).astype(F32).astype(BF)
    expert_lane = ids((chunk, LANES), 1)
    groups = experts // group

    def block_rows(at):
        return pl.ds(pl.multiple_of(at * chunk, chunk), chunk)

    def all_slots(ref, at):
        if group == 1:
            return ref[at]
        return ref[pl.ds(at * group, group)].reshape(chunk, ref.shape[2])

    def hidden_units(turn, _):
        at = lax.rem(me_e // group + groups - turn, groups)
        for k in range(group):
            d = lax.rem(me_e + experts - (at * group + k), experts)

            @pl.when(d > 0)
            def _(d=d):
                route_copy(d, True).wait_recv()
                early_copy(d, True).wait_recv()
                noise_copy(d, True).wait_recv()

        rows = block_rows(at)
        came = all_slots(routed_ref, at)
        added = [mm(noise_all[at * group + k], fold, TN) for k in range(group)]
        added = added[0] if group == 1 else jnp.concatenate(added, axis=0)
        logits = jnp.where(expert_lane < experts, mm(came, w_router_ref[...]) + added, -1e30)
        power = jnp.exp(logits - jnp.max(logits, -1, keepdims=True))
        router_ref[rows, :] = power / jnp.sum(power, -1, keepdims=True)
        for f in range(parts):
            pre = mm(came, w_in_all[f])
            normal, density = gelu_parts(pre)
            hidden_ref[f, rows, :] = (pre * normal).astype(BF)
            slope_ref[f, rows, :] = (normal + pre * density).astype(BF)
        return 0

    lax.fori_loop(0, groups, hidden_units, 0)

    line_back.arrive(tensor - 2)
    keep[2].wait()

    def early_sent(d):
        early_copy(d, False).wait_send()
        route_copy(d, False).wait_send()

    each(experts, early_sent)

    small_ref[...] = jnp.zeros_like(small_ref)

    def expert_rows(turn, _):
        at = lax.rem(me_e // group + groups - turn, groups)
        rows = block_rows(at)
        came = all_slots(routed_ref, at)
        router = router_ref[rows, :]
        own_lane = expert_lane == me_e
        gate = jnp.sum(jnp.where(own_lane, router, 0.0), -1, keepdims=True)
        cot = all_slots(early_ref, at).astype(F32)
        d_exp = (gate * cot).astype(BF)
        out = jnp.zeros((chunk, D), F32)
        back = jnp.zeros((chunk, D), F32)
        for f in range(parts):
            w_b = w_back_all[f]
            out = out + mm(hidden_ref[f, rows, :], w_b)
            d_pre = (mm(d_exp, w_b, NT) * slope_ref[f, rows, :].astype(F32)).astype(BF)
            slope_ref[f, rows, :] = d_pre
            back = back + mm(d_pre, w_in_all[f], NT)
        out = out.astype(BF).astype(F32)
        d_gate = jnp.sum(cot * out, -1, keepdims=True)
        d_logits = (d_gate * gate * (own_lane.astype(F32) - router)).astype(BF)
        back = (back + mm(d_logits, w_router_ref[...], NT)).astype(BF)
        out = (gate * out).astype(BF)
        small_ref[0:experts, :] += mm(d_logits, came, TN)[0:experts]
        for k in range(group):
            e = at * group + k
            part = slice(k * slots, (k + 1) * slots)
            early_ref[e] = d_exp[part]
            d = lax.rem(e + experts - me_e, experts)

            @pl.when(d > 0)
            def _(d=d, e=e, part=part):
                send_ref[e] = out[part]
                early_send[e] = back[part]
                back_copy(d, False).start()

            @pl.when(d == 0)
            def _(e=e, part=part):
                out_ref[e] = out[part]
                back_ref[e] = back[part]

        return 0

    lax.fori_loop(0, groups, expert_rows, 0)

    def grads_at(block, part):
        return slope_ref.at[block, part * D : (part + 1) * D]

    sums = Sums(tensor, grads_at, held, sum_send, sum_recv)
    order = []
    for step in range(tensor):
        for f in (tensor - 1 - step, step):
            if f not in order:
                order.append(f)
    for f in order:
        for part, left, right in ((0, routed_ref, slope_ref), (1, early_ref, hidden_ref)):
            in_grad_ref[...] = jnp.zeros_like(in_grad_ref)

            def add_in(at, _, f=f, left=left, right=right):
                in_grad_ref[...] += mm(all_slots(left, at), right[f, block_rows(at), :], TN)
                return 0

            lax.fori_loop(0, groups, add_in, 0)
            grads_at(f, part)[...] = in_grad_ref[...].astype(BF)
        for step in range(tensor - 1):
            for way, block in ((0, tensor - 1 - step), (1, step)):
                if block == f:
                    sums.start_first(way, step)
    each(experts, lambda d: out_copy(d, False).start())

    each(experts, lambda d: back_copy(d, True).wait_recv())
    slots_of = rows_ref[:, 0:experts]
    d_normed2 = take_rows(slots_of, back_ref, experts)
    unit2, inverse2 = unit_norm(residual_ref[...])
    d_rows, norm2 = norm_back(d_normed2, unit2, inverse2, gain2_ref[...])
    small_ref[experts + 1 : experts + 2, :] = norm2
    d_residual = cot_ref[...] + d_rows
    cot_ref[...] = d_residual
    d_attention = d_residual.astype(BF)
    scaling = HD ** (-0.5)
    line_steps = [(step, part) for step in range(1, tensor - 1) for part in (0, 1)]
    unit1, inverse1 = unit_norm(x_ref[...])
    normed1 = (unit1 * gain1_ref[...]).astype(BF)
    for t in range(tensor):
        w_grad_ref[t, :, 3 * width : wide] = mm(d_attention, mixed_ref[t], TN).astype(BF)
        d_mixed = mm(d_attention, w_ref[t, :, 3 * width : wide]).astype(BF)
        for i in range(images):
            rows = slice(i * SP, (i + 1) * SP)
            q = qkv_ref[t, rows, 0:width]
            k = qkv_ref[t, rows, width : 2 * width]
            v = qkv_ref[t, rows, 2 * width : 3 * width]
            do = d_mixed[rows]
            dq = dk = dv = None
            for j in range(heads):
                own = lane == j
                do_j = do if heads == 1 else jnp.where(own, do, jnp.zeros_like(do))
                q_j = q if heads == 1 else jnp.where(own, q, jnp.zeros_like(q))
                attend_low = attend_ref[i, t * heads + j]
                attend = attend_low.astype(F32)
                part_v = mm(attend_low, do_j, TN)
                d_attend = mm(do_j, v, NT)
                inner = jnp.sum(attend * d_attend, -1, keepdims=True)
                ds = (attend * (d_attend - inner)).astype(BF)
                part_q = mm(ds, k) * scaling
                part_k = mm(ds, q_j, TN) * scaling
                dq = part_q if dq is None else jnp.where(own, part_q, dq)
                dk = part_k if dk is None else dk + part_k
                dv = part_v if dv is None else dv + part_v
            d_qkv_ref[t, rows, 0:width] = dq.astype(BF)
            d_qkv_ref[t, rows, width : 2 * width] = dk.astype(BF)
            d_qkv_ref[t, rows, 2 * width : 3 * width] = dv.astype(BF)
        w_grad_ref[t, :, 0 : 3 * width] = mm(normed1, d_qkv_ref[t], TN).astype(BF)
        each(experts, lambda d, t=t: w_copy(t, d, False).start())
        if t in (0, tensor // 2) and line_steps:
            sums.forward(*line_steps.pop(0))
    d_normed1 = None
    for t in range(tensor):
        part = mm(d_qkv_ref[t], w_ref[t, :, 0 : 3 * width], NT)
        d_normed1 = part if d_normed1 is None else d_normed1 + part
    d_rows, norm1 = norm_back(d_normed1, unit1, inverse1, gain1_ref[...])
    small_ref[experts : experts + 1, :] = norm1
    each(experts, lambda d: small_copy(d, False).start())
    small_plane[me_e] = small_ref[...]
    tokens_grad_ref[...] = compact(cot_ref[...] + d_rows)

    each(experts, lambda d: out_copy(d, True).wait_recv())
    output = residual_ref[...] + take_rows(slots_of, out_ref, experts)
    output_ref[...] = compact(output).astype(BF)

    for t in range(tensor):
        pieces[me_e, t] = w_grad_ref[t, mine, :]
    for t in range(tensor):
        each(experts, lambda d, t=t: w_copy(t, d, True).wait_recv())
        total = pieces[0, t].astype(F32)
        for e in range(1, experts):
            total = total + pieces[e, t].astype(F32)
        piece_send[t] = total.astype(BF)
    each(tensor, lambda d: piece_copy(d, False).start())
    piece_line[me_t] = piece_send[me_t]
    each(experts, lambda d: small_copy(d, True).wait_recv())
    total = small_plane[0]
    for e in range(1, experts):
        total = total + small_plane[e]
    small_line_send[...] = total
    each(tensor, lambda d: small_line_copy(d, False).start())
    small_line[me_t] = total
    if line_steps:
        sums.forward(*line_steps.pop(0))
    each(tensor, lambda d: piece_copy(d, True).wait_recv())
    total = piece_line[0].astype(F32)
    for t in range(1, tensor):
        total = total + piece_line[t].astype(F32)
    w_sum_ref[mine, :] = total.astype(BF)
    each(experts, lambda d: final_copy(d, False).start())
    for step, part in line_steps:
        sums.forward(step, part)

    each(tensor, lambda d: small_line_copy(d, True).wait_recv())
    total = small_line[0]
    for t in range(1, tensor):
        total = total + small_line[t]
    small_sum_ref[...] = total
    each(experts, lambda d: final_copy(d, True).wait_recv())

    for part in (0, 1):
        sums.last(part)
        total = grads_at(me_t, part)[...].astype(F32)
        for way in (0, 1):
            came = held[way, tensor - 2, part].astype(F32)
            total = total + jnp.where(sums.hops(way) >= 1, came, jnp.zeros_like(came))
        if part == 0:
            in_grad_ref[...] = total
        else:
            back_grad_ref[...] = total.T

    sums.finish()
    line_in.finish()
    line_back.finish()

    def sent(d):
        noise_copy(d, False).wait_send()
        back_copy(d, False).wait_send()
        out_copy(d, False).wait_send()
        for t in range(tensor):
            w_copy(t, d, False).wait_send()
        final_copy(d, False).wait_send()
        small_copy(d, False).wait_send()

    each(experts, sent)

    def sent_line(d):
        first_copy(d, False).wait_send()
        piece_copy(d, False).wait_send()
        small_line_copy(d, False).wait_send()
        each(experts, lambda k: plane_copy(d, k, False).wait_send())

    each(tensor, sent_line)


def per_device(
    tokens, norm1_gain, w_qkv, w_out, norm2_gain, w_router, noise, routes, w_in, w_back, cotangent
):
    own_rows = tokens.shape[0]
    experts = noise.shape[1]
    tensor = lax.axis_size("tensor")
    images = own_rows // SEQ
    rows = images * SP
    capacity = (2 * own_rows * TOP + experts - 1) // experts
    slots = up(capacity, TILE)
    group = max(1, 128 // slots)
    width = w_out.shape[0]
    hidden = w_in.shape[2]
    heads = tensor * width // HD
    piece = D // experts
    small_rows = up(experts + 2, 8)
    noise_rows = up(3 * experts, TILE)
    pairs = experts * slots
    dma = pltpu.SemaphoreType.DMA
    bf, f32 = (lambda *dims: pltpu.VMEM(dims, BF)), (lambda *dims: pltpu.VMEM(dims, F32))

    w_own = jnp.concatenate([w_qkv.reshape(D, 3 * width), w_out.T], axis=1)
    w_router_wide = jnp.pad(w_router, ((0, 0), (0, LANES - experts)))
    output, grad_tokens, w_sum, small, grad_in, grad_back = call(
        functools.partial(block_kernel, experts, tensor, images, group),
        (
            shape((own_rows, D)),
            shape((own_rows, D), F32),
            shape((D, 4 * width)),
            shape((small_rows, D), F32),
            shape((D, hidden), F32),
            shape((hidden, D), F32),
        ),
        scratch=(
            bf(tensor, D, 4 * width),
            bf(tensor, D, hidden),
            bf(tensor, hidden, D),
            f32(up(own_rows, TILE), D),
            f32(rows, D),
            f32(rows, D),
            f32(rows, LANES),
            f32(experts, rows),
            bf(tensor, rows, 3 * width),
            bf(images, heads, SP, SP),
            bf(tensor, rows, width),
            f32(rows, D),
            bf(tensor, rows, 3 * width),
            bf(experts, slots, D),
            bf(experts, slots, D),
            bf(experts, slots, D),
            bf(experts, slots, D),
            bf(experts, noise_rows, slots),
            bf(experts, noise_rows, slots),
            f32(pairs, LANES),
            bf(tensor, pairs, hidden),
            bf(tensor, max(pairs, 2 * D), hidden),
            bf(experts, slots, D),
            bf(experts, slots, D),
            bf(2, tensor - 1, 2, D, hidden),
            bf(tensor, D, 4 * width),
            bf(experts, tensor, piece, 4 * width),
            bf(tensor, piece, 4 * width),
            bf(tensor, piece, 4 * width),
            f32(small_rows, D),
            f32(experts, small_rows, D),
            f32(small_rows, D),
            f32(tensor, small_rows, D),
            dma((3,)),
            dma((2, tensor)),
            dma((2, tensor, experts)),
            dma((2, 2, tensor - 1)),
            dma((2, 2, tensor - 1)),
            dma((2, experts)),
            dma((2, experts)),
            dma((2, experts)),
            dma((2, experts)),
            dma((2, experts)),
            dma((2, tensor - 1, 2)),
            dma((2, tensor - 1, 2)),
            dma((2, tensor, experts)),
            dma((2, tensor)),
            dma((2, experts)),
            dma((2, experts)),
            dma((2, tensor)),
        ),
        far_in=(7, 8, 9),
        collective_id=0,
        has_side_effects=True,
    )(
        routes, tokens, cotangent, noise, norm1_gain.reshape(1, D), norm2_gain.reshape(1, D),
        w_router_wide, w_own, w_in[0], w_back[0],
    )
    w_sum = w_sum.astype(F32)
    return (
        output,
        grad_tokens,
        small[experts],
        w_sum[:, : 3 * width].reshape(D, 3, width),
        w_sum[:, 3 * width :].T,
        small[experts + 1],
        small[:experts].T,
        grad_in[None],
        grad_back[None],
    )


def solution(mesh):
    rows = P(("expert", "tensor"), None)
    placed = (
        rows,
        P(),
        P(None, None, "tensor"),
        P("tensor", None),
        P(),
        P(),
        rows,
        rows,
        P("expert", None, "tensor"),
        P("expert", "tensor", None),
        rows,
    )
    return jax.shard_map(
        per_device,
        mesh=mesh,
        in_specs=placed,
        out_specs=(
            rows,
            rows,
            P(),
            P(None, None, "tensor"),
            P("tensor", None),
            P(),
            P(),
            P("expert", None, "tensor"),
            P("expert", "tensor", None),
        ),
        check_vma=False,
    )
```

```python
import functools

import jax
import jax.numpy as jnp
from jax import lax
from jax.experimental import pallas as pl
from jax.experimental.pallas import tpu as pltpu
from jax.sharding import PartitionSpec as P

D = 512
HD = 64
CORES = 2
TOP = 2
SEQ = 197
LANES = 128
TILE = 16
EPSILON = 1e-06
BF = jnp.bfloat16
F32 = jnp.float32
VMEM_BYTES = 62 * 1024 * 1024

NN = (((1,), (0,)), ((), ()))
NT = (((1,), (1,)), ((), ()))
TN = (((0,), (0,)), ((), ()))


def up(value, unit):
    return (value + unit - 1) // unit * unit


SP = up(SEQ, TILE)


def mm(a, b, dims=NN):
    return lax.dot_general(a, b, dims, preferred_element_type=F32)


def call(
    body, out_shape, scratch=(), flops=0, moved=0, prefetch=(), far_in=(), far_out=(), **more
):
    params = pltpu.CompilerParams(vmem_limit_bytes=VMEM_BYTES, **more)
    cost = pl.CostEstimate(flops=flops, bytes_accessed=moved, transcendentals=0)

    def spec(place, far, scalar=()):
        if place in scalar:
            return pl.BlockSpec(memory_space=pltpu.SMEM)
        return pl.BlockSpec(memory_space=pl.ANY if place in far else pltpu.VMEM)

    def run(*args):
        return pl.pallas_call(
            body,
            out_shape=out_shape,
            in_specs=[spec(place, far_in, prefetch) for place in range(len(args))],
            out_specs=tuple(spec(place, far_out) for place in range(len(out_shape))),
            scratch_shapes=list(scratch),
            compiler_params=params,
            cost_estimate=cost,
        )(*args)

    return run


def shape(dims, dtype=BF):
    return jax.ShapeDtypeStruct(dims, dtype)


def unit_norm(values):
    center = values - jnp.mean(values, -1, keepdims=True)
    spread = jnp.mean(center * center, -1, keepdims=True)
    inverse = lax.rsqrt(spread + EPSILON)
    return center * inverse, inverse


def norm_back(grad_rows, normed, inverse, gain):
    scaled = grad_rows * gain
    inner = (
        scaled
        - jnp.mean(scaled, -1, keepdims=True)
        - normed * jnp.mean(scaled * normed, -1, keepdims=True)
    )
    return inverse * inner, jnp.sum(grad_rows * normed, axis=0, keepdims=True)


def ids(shape_of, dim):
    return lax.broadcasted_iota(jnp.int32, shape_of, dim)


def slots_by_row(routes, experts):
    rows = routes.shape[0]
    which = ids((rows, experts), 1)
    named = (routes[:, 0:1] == which) | (routes[:, 1:2] == which)
    before = (ids((rows, rows), 1) < ids((rows, rows), 0)).astype(F32).astype(BF)
    rank = mm(before, named.astype(F32).astype(BF))
    return jnp.where(named, rank, -1.0)


def take_rows(slots, in_ref, experts):
    count = in_ref.shape[0] // experts
    rows = slots.shape[0]
    place = ids((rows, count), 1).astype(F32)
    total = None
    for e in range(experts):
        pick = (place == slots[:, e : e + 1]).astype(F32).astype(BF)
        part = mm(pick, in_ref[e * count : (e + 1) * count, :])
        total = part if total is None else total + part
    return total


MESH = pl.DeviceIdType.MESH


def greet(axes):
    barrier = pltpu.get_barrier_semaphore()
    for name, size in axes:
        me = lax.axis_index(name)

        def hello(d, _, name=name, size=size, me=me):
            pl.semaphore_signal(
                barrier, inc=1, device_id={name: lax.rem(me + d, size)}, device_id_type=MESH
            )
            return 0

        lax.fori_loop(1, size, hello, 0)
    pl.semaphore_wait(barrier, sum(size - 1 for _, size in axes))


def remote(src, dst, send_sem, recv_sem, name, to):
    return pltpu.make_async_remote_copy(
        src_ref=src,
        dst_ref=dst,
        send_sem=send_sem,
        recv_sem=recv_sem,
        device_id={name: to},
        device_id_type=MESH,
    )


def each(size, step):
    def body(d, _):
        step(d)
        return 0

    lax.fori_loop(1, size, body, 0)


class Line:
    def __init__(self, size, own, everyone, send_sem, recv_sem):
        self.size, self.own, self.all = size, own, everyone
        self.send_sem, self.recv_sem = send_sem, recv_sem
        self.me = lax.axis_index("tensor")

    def copy(self, way, step, arriving):
        toward = 1 if way == 0 else -1
        owner = self.me - toward * (step + (1 if arriving else 0))
        src = self.own if step == 0 else self.all.at[owner]
        return remote(
            src, self.all.at[owner], self.send_sem.at[way, step], self.recv_sem.at[way, step],
            "tensor", self.me + toward,
        )

    def sends(self, way, step):
        last = self.size - 1
        if way == 0:
            return (self.me >= step) & (self.me < last)
        return (self.me <= last - step) & (self.me > 0)

    def receives(self, way, step):
        if way == 0:
            return self.me >= step + 1
        return self.me <= self.size - 2 - step

    def start(self, step):
        for way in (0, 1):
            pl.when(self.sends(way, step))(lambda way=way: self.copy(way, step, False).start())

    def arrive(self, step):
        for way in (0, 1):
            pl.when(self.receives(way, step))(
                lambda way=way: self.copy(way, step, True).wait_recv()
            )

    def finish(self):
        for step in range(self.size - 1):
            for way in (0, 1):
                pl.when(self.sends(way, step))(
                    lambda way=way, step=step: self.copy(way, step, False).wait_send()
                )


def gelu_parts(pre):
    density = jnp.exp(pre * pre * -0.5)
    size = jnp.abs(pre) * (0.5**0.5)
    t = 1.0 / (1.0 + 0.3275911 * size)
    series = t * (
        0.254829592
        + t * (-0.284496736 + t * (1.421413741 + t * (-1.453152027 + t * 1.061405429)))
    )
    tail = 0.5 * series * density
    return jnp.where(pre < 0, tail, 1.0 - tail), density * 0.3989422804014327


class Sums:
    def __init__(self, size, own, held, send_sem, recv_sem):
        self.size, self.own, self.held = size, own, held
        self.send_sem, self.recv_sem = send_sem, recv_sem
        self.me = lax.axis_index("tensor")

    def hops(self, way):
        return self.me if way == 0 else self.size - 1 - self.me

    def block(self, way, step):
        ahead = self.size - 1 + self.hops(way) - step
        return ahead if way == 0 else self.size - 1 - ahead

    def copy(self, way, step, part, first):
        toward = 1 if way == 0 else -1
        if first:
            src = self.own(self.block(way, step), part)
        else:
            src = self.held.at[way, max(step - 1, 0), part]
        return remote(
            src, self.held.at[way, step, part],
            self.send_sem.at[way, step, part], self.recv_sem.at[way, step, part],
            "tensor", self.me + toward,
        )

    def start_first(self, way, step, part):
        pl.when(self.hops(way) == 0)(lambda: self.copy(way, step, part, True).start())

    def middle(self, way, step):
        hops = self.hops(way)
        return (hops >= 1) & (hops <= step) & (hops < self.size - 1)

    def forward(self, step, part):
        for way in (0, 1):

            def go(way=way):
                self.copy(way, step - 1, part, False).wait_recv()
                held = self.held.at[way, step - 1, part]
                mine = self.own(self.block(way, step), part)
                add_into(held, mine)
                self.copy(way, step, part, False).start()

            pl.when(self.middle(way, step))(go)

    def last(self, part):
        for way in (0, 1):
            pl.when(self.hops(way) >= 1)(
                lambda way=way: self.copy(way, self.size - 2, part, False).wait_recv()
            )

    def finish(self):
        for part in (0, 1):
            for step in range(self.size - 1):
                for way in (0, 1):
                    sends = (self.hops(way) == 0) | self.middle(way, step)
                    pl.when(sends)(
                        lambda way=way, step=step, part=part: self.copy(
                            way, step, part, False
                        ).wait_send()
                    )


def add_into(held, mine):
    rows = held.shape[0]
    block = min(rows, 128)

    def body(r, _):
        at = pl.ds(pl.multiple_of(r * block, block), block)
        held[at, :] = (held[at, :].astype(F32) + mine[at, :].astype(F32)).astype(BF)
        return 0

    lax.fori_loop(0, rows // block, body, 0)


def block_kernel(
    experts, tensor, images, group,
    routes_ref, tokens_ref, cotangent_ref, noise_ref, gain1_ref, gain2_ref, w_router_ref,
    w_own_ref, w_in_own, w_back_own,
    output_ref, tokens_grad_ref, w_sum_ref, small_sum_ref, in_grad_ref, back_grad_ref,
    w_ref, w_in_all, w_back_all, narrow, x_ref, cot_ref, rows_ref, lanes_ref,
    qkv_ref, attend_ref, mixed_ref, residual_ref,
    send_ref, routed_ref, early_send, early_ref, noise_send, noise_all, router_ref,
    hidden_ref, slope_ref, back_ref, held,
    wide_ref, back_grads, pair_ref, pieces, piece_send, piece_line,
    small_ref, small_plane, small_line_send, small_line,
    own_sem, first_sems, plane_sems, pair_sems, in_sems, in_back_sems, route_sems, early_sems, noise_sems,
    back_sems, out_sems, sum_send, sum_recv, w_pair_sems, w_sems, piece_sems, final_sems,
    small_sems, small_line_sems,
):
    own_rows = tokens_ref.shape[0]
    wide = w_own_ref.shape[1]
    width = wide // 4
    heads = width // HD
    slots = noise_send.shape[2]
    pairs = experts * slots
    parts = w_in_all.shape[0]
    chunk = group * slots
    me_e, me_t = lax.axis_index("expert"), lax.axis_index("tensor")
    piece = D // experts

    chips = experts // CORES
    core = lax.rem(me_e, CORES)
    half = chips * piece

    def rows_at(e):
        at = lax.rem(e, CORES) * chips + e // CORES
        return pl.ds(pl.multiple_of(at * piece, piece), piece)

    def half_at(which):
        return pl.ds(pl.multiple_of(which * half, half), half)

    def chip_after(k):
        return lax.rem(me_e + CORES * k, experts)

    def chip_place(k, arriving):
        return lax.rem(me_e + experts - CORES * k, experts) if arriving else me_e

    mine = rows_at(me_e)

    def after(d):
        return lax.rem(me_e + d, experts)

    def place(d, arriving):
        return lax.rem(me_e + experts - d, experts) if arriving else me_e

    def swap_copy(src, dst, sems, d, arriving):
        to = after(d)
        return remote(
            src.at[to], dst.at[place(d, arriving)], sems.at[0, d], sems.at[1, d], "expert", to
        )

    def line_copy(src, dst, sems, d, arriving):
        owner = lax.rem(me_t + tensor - d, tensor) if arriving else me_t
        return remote(
            src, dst(owner), sems.at[0, d], sems.at[1, d],
            "tensor", lax.rem(me_t + d, tensor),
        )

    def first_copy(d, arriving):
        return line_copy(
            w_own_ref.at[mine], lambda owner: w_ref.at[owner, mine], first_sems, d, arriving
        )

    def plane_copy(z, k, arriving):
        owner = lax.rem(me_t + tensor - z, tensor)
        block = w_ref.at[owner, rows_at(chip_place(k, arriving))]
        return remote(
            block, block, plane_sems.at[0, z, k], plane_sems.at[1, z, k], "expert", chip_after(k)
        )

    def pair_copy(z, arriving):
        owner = lax.rem(me_t + tensor - z, tensor)
        block = w_ref.at[owner, half_at(CORES - 1 - core if arriving else core)]
        return remote(
            block, block, pair_sems.at[0, z], pair_sems.at[1, z], "expert",
            me_e + CORES - 1 - 2 * core,
        )

    def slot_rows(e):
        return pl.ds(pl.multiple_of(e * slots, slots), slots)

    def flat_copy(src, dst, sems, d, arriving):
        return remote(
            src.at[slot_rows(after(d))], dst.at[slot_rows(place(d, arriving))],
            sems.at[0, d], sems.at[1, d], "expert", after(d),
        )

    def route_copy(d, arriving):
        return flat_copy(send_ref, routed_ref, route_sems, d, arriving)

    def early_copy(d, arriving):
        return flat_copy(early_send, early_ref, early_sems, d, arriving)

    def noise_copy(d, arriving):
        return swap_copy(noise_send, noise_all, noise_sems, d, arriving)

    def back_copy(d, arriving):
        return flat_copy(early_send, back_ref, back_sems, d, arriving)

    def out_copy(d, arriving):
        return flat_copy(send_ref, routed_ref, out_sems, d, arriving)

    def columns(t):
        return slice(t * wide, (t + 1) * wide)

    def w_pair_copy(t):
        return remote(
            wide_ref.at[half_at(CORES - 1 - core), columns(t)], pair_ref.at[t],
            w_pair_sems.at[0, t], w_pair_sems.at[1, t], "expert", me_e + CORES - 1 - 2 * core,
        )

    def w_copy(t, k, arriving):
        return remote(
            wide_ref.at[rows_at(chip_after(k)), columns(t)],
            pieces.at[chip_place(k, arriving) // CORES, t],
            w_sems.at[0, t, k], w_sems.at[1, t, k], "expert", chip_after(k),
        )

    def share_pair_sum(t):
        w_pair_copy(t).wait_recv()
        ours = half_at(core)
        pair_sum = wide_ref[ours, columns(t)].astype(F32) + pair_ref[t].astype(F32)
        wide_ref[ours, columns(t)] = pair_sum.astype(BF)
        each(chips, lambda k: w_copy(t, k, False).start())

    def piece_copy(d, arriving):
        src = piece_send.at[lax.rem(me_t + d, tensor)]
        return line_copy(src, lambda owner: piece_line.at[owner], piece_sems, d, arriving)

    def final_copy(d, arriving):
        block = w_sum_ref.at[rows_at(place(d, arriving))]
        return remote(block, block, final_sems.at[0, d], final_sems.at[1, d], "expert", after(d))

    def small_copy(d, arriving):
        return remote(
            small_ref, small_plane.at[place(d, arriving)], small_sems.at[0, d],
            small_sems.at[1, d], "expert", after(d),
        )

    def small_line_copy(d, arriving):
        return line_copy(
            small_line_send, lambda owner: small_line.at[owner], small_line_sems, d, arriving
        )

    greet((("expert", experts), ("tensor", tensor)))
    each(tensor, lambda d: first_copy(d, False).start())
    line_in = Line(tensor, w_in_own, w_in_all, in_sems.at[0], in_sems.at[1])
    line_back = Line(tensor, w_back_own, w_back_all, in_back_sems.at[0], in_back_sems.at[1])
    line_in.start(0)
    keep = [
        pltpu.make_async_copy(w_own_ref, w_ref.at[me_t], own_sem.at[0]),
        pltpu.make_async_copy(w_in_own, w_in_all.at[me_t], own_sem.at[1]),
        pltpu.make_async_copy(w_back_own, w_back_all.at[me_t], own_sem.at[2]),
    ]
    for copy in keep:
        copy.start()

    def spread(compact, to_ref, fill=0.0):
        columns = compact.shape[1]
        narrow[0:own_rows, 0:columns] = compact
        to_ref[...] = jnp.full(to_ref.shape, fill, F32)
        for i in range(images):
            to_ref[i * SP : i * SP + SEQ, 0:columns] = narrow[
                i * SEQ : (i + 1) * SEQ, 0:columns
            ]

    def compact(padded):
        for i in range(images):
            narrow[i * SEQ : (i + 1) * SEQ, :] = padded[i * SP : i * SP + SEQ, :]
        return narrow[0:own_rows, :]

    spread(noise_ref[...], rows_ref)
    noise = rows_ref[...].T[0:experts, :]
    high = noise.astype(BF).astype(F32)
    middle = (noise - high).astype(BF).astype(F32)
    low = noise - high - middle
    noise_parts = [high, middle, low]
    if noise_send.shape[1] > 3 * experts:
        noise_parts.append(jnp.zeros((noise_send.shape[1] - 3 * experts, noise.shape[1]), F32))
    noise = jnp.concatenate(noise_parts, axis=0).astype(BF)
    spread(slots_by_row(routes_ref[...], experts), rows_ref, -1.0)
    lanes_ref[...] = rows_ref[...].T[0:experts, :]
    spread(cotangent_ref[...].astype(F32), cot_ref)
    cot_low = cot_ref[...].astype(BF)
    spot = ids((slots, lanes_ref.shape[1]), 0).astype(F32)

    def pick_of(e):
        return (spot == lanes_ref[pl.ds(e, 1), :]).astype(F32).astype(BF)

    def forward_piece(z):
        first_copy(z, True).wait_recv()
        each(chips, lambda k: plane_copy(z, k, False).start())

    each(tensor, forward_piece)
    for d in range(1, experts + 1):
        e = after(d)
        pick = pick_of(e)
        rows_of_e = mm(pick, cot_low).astype(BF)
        noise_of_e = mm(noise, pick, NT).astype(BF)
        if d < experts:
            early_send[slot_rows(e), :] = rows_of_e
            noise_send[e] = noise_of_e
            early_copy(d, False).start()
            noise_copy(d, False).start()
        else:
            early_ref[slot_rows(e), :] = rows_of_e
            noise_all[e] = noise_of_e
    spread(tokens_ref[...].astype(F32), x_ref)
    x = x_ref[...]
    unit1, inverse1 = unit_norm(x)
    normed1 = (unit1 * gain1_ref[...]).astype(BF)
    line_in.arrive(0)
    if tensor > 2:
        line_in.start(1)

    def forward_half(z):
        each(chips, lambda k: plane_copy(z, k, True).wait_recv())
        pair_copy(z, False).start()

    each(tensor, forward_half)
    keep[0].wait()
    each(tensor, lambda z: pair_copy(z, True).wait_recv())

    lane = ids((SP, width), 1) // HD
    live = ids((SP, SP), 1) < SEQ
    for t in range(tensor):
        qkv_ref[t] = mm(normed1, w_ref[t, :, 0 : 3 * width]).astype(BF)
        for i in range(images):
            rows = slice(i * SP, (i + 1) * SP)
            q = qkv_ref[t, rows, 0:width]
            k = qkv_ref[t, rows, width : 2 * width]
            v = qkv_ref[t, rows, 2 * width : 3 * width]
            mixed = None
            for j in range(heads):
                q_j = q if heads == 1 else jnp.where(lane == j, q, jnp.zeros_like(q))
                scores = mm(q_j, k, NT) * HD ** (-0.5)
                scores = jnp.where(live, scores, -1e30)
                power = jnp.exp(scores - jnp.max(scores, -1, keepdims=True))
                attend = (power / jnp.sum(power, -1, keepdims=True)).astype(BF)
                attend_ref[i, t * heads + j] = attend
                part = mm(attend, v)
                mixed = part if mixed is None else jnp.where(lane == j, part, mixed)
            mixed_ref[t, rows, :] = mixed.astype(BF)
    residual = x
    for t in range(tensor):
        residual = residual + mm(mixed_ref[t], w_ref[t, :, 3 * width : wide], NT)
    residual_ref[...] = residual
    unit2, inverse2 = unit_norm(residual)
    normed2 = (unit2 * gain2_ref[...]).astype(BF)
    for d in range(1, experts + 1):
        e = after(d)
        rows_of_e = mm(pick_of(e), normed2).astype(BF)
        if d < experts:
            send_ref[slot_rows(e), :] = rows_of_e
            route_copy(d, False).start()
        else:
            routed_ref[slot_rows(e), :] = rows_of_e
    for step in range(1, tensor - 1):
        line_in.arrive(step)
        if step + 1 < tensor - 1:
            line_in.start(step + 1)
        if step == max(1, tensor - 3):
            line_back.start(0)
    if tensor == 2:
        line_back.start(0)
    keep[1].wait()

    fold_from, fold_to = ids((noise_all.shape[1], LANES), 0), ids((noise_all.shape[1], LANES), 1)
    fold = (
        (fold_from < 3 * experts) & (lax.rem(fold_from, experts) == fold_to)
    ).astype(F32).astype(BF)
    expert_lane = ids((chunk, LANES), 1)
    groups = experts // group

    def block_rows(at):
        return pl.ds(pl.multiple_of(at * chunk, chunk), chunk)

    def hidden_units(turn, _):
        at = lax.rem(me_e // group + groups - turn, groups)
        for k in range(group):
            d = lax.rem(me_e + experts - (at * group + k), experts)

            @pl.when(d > 0)
            def _(d=d):
                route_copy(d, True).wait_recv()
                early_copy(d, True).wait_recv()
                noise_copy(d, True).wait_recv()

        @pl.when(turn == groups // 2)
        def _():
            for step in range(0, tensor - 3):
                line_back.arrive(step)
                line_back.start(step + 1)

        rows = block_rows(at)
        came = routed_ref[rows, :]
        added = [mm(noise_all[at * group + k], fold, TN) for k in range(group)]
        added = added[0] if group == 1 else jnp.concatenate(added, axis=0)
        logits = jnp.where(expert_lane < experts, mm(came, w_router_ref[...]) + added, -1e30)
        power = jnp.exp(logits - jnp.max(logits, -1, keepdims=True))
        router = power / jnp.sum(power, -1, keepdims=True)
        router_ref[rows, :] = router
        gate = jnp.sum(jnp.where(expert_lane == me_e, router, 0.0), -1, keepdims=True)
        early_ref[rows, :] = (gate * early_ref[rows, :].astype(F32)).astype(BF)
        for f in range(parts):
            pre = mm(came, w_in_all[f])
            normal, density = gelu_parts(pre)
            hidden_ref[f, rows, :] = (pre * normal).astype(BF)
            slope_ref[f, rows, :] = (normal + pre * density).astype(BF)
        return 0

    lax.fori_loop(0, groups, hidden_units, 0)

    def grads_at(block, part):
        return back_grads.at[block] if part else slope_ref.at[block, 0:D]

    sums = Sums(tensor, grads_at, held, sum_send, sum_recv)
    order = []
    for step in range(tensor):
        for f in (tensor - 1 - step, step):
            if f not in order:
                order.append(f)

    def turn_rows(ref):
        def body(at, _):
            rows = pl.ds(pl.multiple_of(at * LANES, LANES), LANES)
            wide_ref[:, rows] = ref[rows, :].T
            return 0

        lax.fori_loop(0, pairs // LANES, body, 0)

    def weight_grads(part, right):
        for f in order:
            block = mm(wide_ref[:, 0:pairs], right[f, 0:pairs, :]).astype(BF)
            grads_at(f, part)[...] = block
            for step in range(tensor - 1):
                for way, to in ((0, tensor - 1 - step), (1, step)):
                    if to == f:
                        sums.start_first(way, step, part)

    turn_rows(early_ref)
    weight_grads(1, hidden_ref)
    turn_rows(routed_ref)

    for step in range(max(tensor - 3, 0), tensor - 2):
        line_back.arrive(step)
        line_back.start(step + 1)
    keep[2].wait()

    def early_sent(d):
        early_copy(d, False).wait_send()
        route_copy(d, False).wait_send()

    each(experts, early_sent)

    small_ref[...] = jnp.zeros_like(small_ref)

    def near(k):
        def from_low(me):
            below = (me - k + tensor) // tensor
            return below * (me - k) + (1 - below) * k

        low = 1 - (2 * me_t) // tensor
        mirrored = tensor - 1 - from_low(tensor - 1 - me_t)
        return low * from_low(me_t) + (1 - low) * mirrored

    def unit_part(k, rows):
        f = near(k)
        w_b = w_back_all[f]
        out = mm(hidden_ref[f, rows, :], w_b)
        d_pre = (mm(early_ref[rows, :], w_b, NT) * slope_ref[f, rows, :].astype(F32)).astype(BF)
        slope_ref[f, rows, :] = d_pre
        return out, mm(d_pre, w_in_all[f], NT)

    def near_rows(at, _):
        rows = block_rows(at)
        out, back = unit_part(0, rows)
        for k in range(1, tensor - 1):
            more_out, more_back = unit_part(k, rows)
            out, back = out + more_out, back + more_back
        send_ref[rows, :] = out.astype(BF)
        early_send[rows, :] = back.astype(BF)
        return 0

    lax.fori_loop(0, groups, near_rows, 0)
    line_steps = [(step, part) for part in (1, 0) for step in range(1, tensor - 1)]

    def next_sum():
        if line_steps:
            sums.forward(*line_steps.pop(0))

    next_sum()
    line_back.arrive(tensor - 2)

    def far_rows(turn, _):
        at = lax.rem(me_e // group + groups - turn, groups)
        rows = block_rows(at)
        router = router_ref[rows, :]
        own_lane = expert_lane == me_e
        gate = jnp.sum(jnp.where(own_lane, router, 0.0), -1, keepdims=True)
        out, back = unit_part(tensor - 1, rows)
        out = (out + send_ref[rows, :].astype(F32)).astype(BF).astype(F32)
        back = back + early_send[rows, :].astype(F32)
        d_gate = jnp.sum(early_ref[rows, :].astype(F32) * out, -1, keepdims=True)
        d_logits = (d_gate * (own_lane.astype(F32) - router)).astype(BF)
        early_send[rows, :] = (back + mm(d_logits, w_router_ref[...], NT)).astype(BF)
        send_ref[rows, :] = (gate * out).astype(BF)
        small_ref[0:experts, :] += mm(d_logits, routed_ref[rows, :], TN)[0:experts]
        for k in range(group):
            e = at * group + k
            d = lax.rem(e + experts - me_e, experts)

            @pl.when(d > 0)
            def _(d=d):
                back_copy(d, False).start()

            @pl.when(d == 0)
            def _(e=e):
                back_ref[slot_rows(e), :] = early_send[slot_rows(e), :]
                routed_ref[slot_rows(e), :] = send_ref[slot_rows(e), :]

        return 0

    lax.fori_loop(0, groups, far_rows, 0)

    weight_grads(0, slope_ref)
    next_sum()

    each(experts, lambda d: back_copy(d, True).wait_recv())
    slots_of = rows_ref[:, 0:experts]
    d_normed2 = take_rows(slots_of, back_ref, experts)
    unit2, inverse2 = unit_norm(residual_ref[...])
    d_rows, norm2 = norm_back(d_normed2, unit2, inverse2, gain2_ref[...])
    small_ref[experts + 1 : experts + 2, :] = norm2
    d_residual = cot_ref[...] + d_rows
    cot_ref[...] = d_residual
    d_attention = d_residual.astype(BF)
    scaling = HD ** (-0.5)
    unit1, inverse1 = unit_norm(x_ref[...])
    normed1 = (unit1 * gain1_ref[...]).astype(BF)
    for t in range(tensor):
        wide_ref[:, t * wide + 3 * width : (t + 1) * wide] = mm(d_attention, mixed_ref[t], TN).astype(BF)
        d_mixed = mm(d_attention, w_ref[t, :, 3 * width : wide]).astype(BF)
        for i in range(images):
            rows = slice(i * SP, (i + 1) * SP)
            q = qkv_ref[t, rows, 0:width]
            k = qkv_ref[t, rows, width : 2 * width]
            v = qkv_ref[t, rows, 2 * width : 3 * width]
            do = d_mixed[rows]
            dq = dk = dv = None
            for j in range(heads):
                own = lane == j
                do_j = do if heads == 1 else jnp.where(own, do, jnp.zeros_like(do))
                q_j = q if heads == 1 else jnp.where(own, q, jnp.zeros_like(q))
                attend_low = attend_ref[i, t * heads + j]
                attend = attend_low.astype(F32)
                part_v = mm(attend_low, do_j, TN)
                d_attend = mm(do_j, v, NT)
                inner = jnp.sum(attend * d_attend, -1, keepdims=True)
                ds = (attend * (d_attend - inner)).astype(BF)
                part_q = mm(ds, k) * scaling
                part_k = mm(ds, q_j, TN) * scaling
                dq = part_q if dq is None else jnp.where(own, part_q, dq)
                dk = part_k if dk is None else dk + part_k
                dv = part_v if dv is None else dv + part_v
            qkv_ref[t, rows, 0:width] = dq.astype(BF)
            qkv_ref[t, rows, width : 2 * width] = dk.astype(BF)
            qkv_ref[t, rows, 2 * width : 3 * width] = dv.astype(BF)
        wide_ref[:, t * wide : t * wide + 3 * width] = mm(normed1, qkv_ref[t], TN).astype(BF)
        w_pair_copy(t).start()
        if t > 0:
            share_pair_sum(t - 1)
    share_pair_sum(tensor - 1)
    next_sum()
    d_normed1 = None
    for t in range(tensor):
        part = mm(qkv_ref[t], w_ref[t, :, 0 : 3 * width], NT)
        d_normed1 = part if d_normed1 is None else d_normed1 + part
    d_rows, norm1 = norm_back(d_normed1, unit1, inverse1, gain1_ref[...])
    small_ref[experts : experts + 1, :] = norm1
    each(experts, lambda d: small_copy(d, False).start())
    each(experts, lambda d: out_copy(d, False).start())
    small_plane[me_e] = small_ref[...]
    tokens_grad_ref[...] = compact(cot_ref[...] + d_rows)

    for t in range(tensor):
        pieces[me_e // CORES, t] = wide_ref[mine, columns(t)]
    for t in range(tensor):
        each(chips, lambda k, t=t: w_copy(t, k, True).wait_recv())
        total = pieces[0, t].astype(F32)
        for e in range(1, chips):
            total = total + pieces[e, t].astype(F32)
        piece_send[t] = total.astype(BF)
    each(tensor, lambda d: piece_copy(d, False).start())
    piece_line[me_t] = piece_send[me_t]
    each(experts, lambda d: small_copy(d, True).wait_recv())
    total = small_plane[0]
    for e in range(1, experts):
        total = total + small_plane[e]
    small_line_send[...] = total
    each(tensor, lambda d: small_line_copy(d, False).start())
    small_line[me_t] = total
    each(tensor, lambda d: piece_copy(d, True).wait_recv())
    total = piece_line[0].astype(F32)
    for t in range(1, tensor):
        total = total + piece_line[t].astype(F32)
    w_sum_ref[mine, :] = total.astype(BF)
    each(experts, lambda d: final_copy(d, False).start())
    while line_steps:
        next_sum()

    each(experts, lambda d: out_copy(d, True).wait_recv())
    output = residual_ref[...] + take_rows(slots_of, routed_ref, experts)
    output_ref[...] = compact(output).astype(BF)

    each(tensor, lambda d: small_line_copy(d, True).wait_recv())
    total = small_line[0]
    for t in range(1, tensor):
        total = total + small_line[t]
    small_sum_ref[...] = total
    each(experts, lambda d: final_copy(d, True).wait_recv())

    for part in (0, 1):
        sums.last(part)
        total = grads_at(me_t, part)[...].astype(F32)
        for way in (0, 1):
            came = held[way, tensor - 2, part].astype(F32)
            total = total + jnp.where(sums.hops(way) >= 1, came, jnp.zeros_like(came))
        if part == 0:
            in_grad_ref[...] = total.astype(BF)
        else:
            back_grad_ref[...] = total.T.astype(BF)

    sums.finish()
    line_in.finish()
    line_back.finish()

    def sent(d):
        noise_copy(d, False).wait_send()
        back_copy(d, False).wait_send()
        out_copy(d, False).wait_send()
        final_copy(d, False).wait_send()
        small_copy(d, False).wait_send()

    each(experts, sent)

    def sent_line(d):
        first_copy(d, False).wait_send()
        piece_copy(d, False).wait_send()
        small_line_copy(d, False).wait_send()
        pair_copy(d, False).wait_send()
        each(chips, lambda k: plane_copy(d, k, False).wait_send())

    each(tensor, sent_line)
    for t in range(tensor):
        w_pair_copy(t).wait_send()
        each(chips, lambda k, t=t: w_copy(t, k, False).wait_send())


def per_device(
    tokens, norm1_gain, w_qkv, w_out, norm2_gain, w_router, noise, routes, w_in, w_back, cotangent
):
    own_rows = tokens.shape[0]
    experts = noise.shape[1]
    tensor = lax.axis_size("tensor")
    images = own_rows // SEQ
    rows = images * SP
    capacity = (2 * own_rows * TOP + experts - 1) // experts
    slots = up(capacity, TILE)
    group = max(g for g in range(1, experts + 1) if experts % g == 0 and g * slots <= 2 * SP)
    width = w_out.shape[0]
    hidden = w_in.shape[2]
    heads = tensor * width // HD
    piece = D // experts
    small_rows = up(experts + 2, 8)
    noise_rows = up(3 * experts, TILE)
    pairs = experts * slots
    dma = pltpu.SemaphoreType.DMA
    bf, f32 = (lambda *dims: pltpu.VMEM(dims, BF)), (lambda *dims: pltpu.VMEM(dims, F32))

    w_own = jnp.concatenate([w_qkv.reshape(D, 3 * width), w_out.T], axis=1)
    w_router_wide = jnp.pad(w_router, ((0, 0), (0, LANES - experts)))
    output, grad_tokens, w_sum, small, grad_in, grad_back = call(
        functools.partial(block_kernel, experts, tensor, images, group),
        (
            shape((own_rows, D)),
            shape((own_rows, D), F32),
            shape((D, 4 * width)),
            shape((small_rows, D), F32),
            shape((D, hidden)),
            shape((hidden, D)),
        ),
        scratch=(
            bf(tensor, D, 4 * width),
            bf(tensor, D, hidden),
            bf(tensor, hidden, D),
            f32(up(own_rows, TILE), D),
            f32(rows, D),
            f32(rows, D),
            f32(rows, LANES),
            f32(experts, rows),
            bf(tensor, rows, 3 * width),
            bf(images, heads, SP, SP),
            bf(tensor, rows, width),
            f32(rows, D),
            bf(pairs, D),
            bf(pairs, D),
            bf(pairs, D),
            bf(pairs, D),
            bf(experts, noise_rows, slots),
            bf(experts, noise_rows, slots),
            f32(pairs, LANES),
            bf(tensor, pairs, hidden),
            bf(tensor, max(pairs, D), hidden),
            bf(pairs, D),
            bf(2, tensor - 1, 2, D, hidden),
            bf(D, max(pairs, tensor * 4 * width)),
            bf(tensor, D, hidden),
            bf(tensor, D // CORES, 4 * width),
            bf(experts // CORES, tensor, piece, 4 * width),
            bf(tensor, piece, 4 * width),
            bf(tensor, piece, 4 * width),
            f32(small_rows, D),
            f32(experts, small_rows, D),
            f32(small_rows, D),
            f32(tensor, small_rows, D),
            dma((3,)),
            dma((2, tensor)),
            dma((2, tensor, experts // CORES)),
            dma((2, tensor)),
            dma((2, 2, tensor - 1)),
            dma((2, 2, tensor - 1)),
            dma((2, experts)),
            dma((2, experts)),
            dma((2, experts)),
            dma((2, experts)),
            dma((2, experts)),
            dma((2, tensor - 1, 2)),
            dma((2, tensor - 1, 2)),
            dma((2, tensor)),
            dma((2, tensor, experts // CORES)),
            dma((2, tensor)),
            dma((2, experts)),
            dma((2, experts)),
            dma((2, tensor)),
        ),
        far_in=(7, 8, 9),
        collective_id=0,
        has_side_effects=True,
    )(
        routes, tokens, cotangent, noise, norm1_gain.reshape(1, D), norm2_gain.reshape(1, D),
        w_router_wide, w_own, w_in[0], w_back[0],
    )
    w_sum = w_sum.astype(F32)
    return (
        output,
        grad_tokens,
        small[experts],
        w_sum[:, : 3 * width].reshape(D, 3, width),
        w_sum[:, 3 * width :].T,
        small[experts + 1],
        small[:experts].T,
        grad_in.astype(F32)[None],
        grad_back.astype(F32)[None],
    )


def solution(mesh):
    rows = P(("expert", "tensor"), None)
    placed = (
        rows,
        P(),
        P(None, None, "tensor"),
        P("tensor", None),
        P(),
        P(),
        rows,
        rows,
        P("expert", None, "tensor"),
        P("expert", "tensor", None),
        rows,
    )
    return jax.shard_map(
        per_device,
        mesh=mesh,
        in_specs=placed,
        out_specs=(
            rows,
            rows,
            P(),
            P(None, None, "tensor"),
            P("tensor", None),
            P(),
            P(),
            P("expert", None, "tensor"),
            P("expert", "tensor", None),
        ),
        check_vma=False,
    )
```

```python
import functools

import jax
import jax.numpy as jnp
from jax import lax
from jax.experimental import pallas as pl
from jax.experimental.pallas import tpu as pltpu
from jax.sharding import PartitionSpec as P

D = 512
HD = 64
CORES = 2
TOP = 2
SEQ = 197
LANES = 128
TILE = 16
EPSILON = 1e-06
BF = jnp.bfloat16
F32 = jnp.float32
VMEM_BYTES = 62 * 1024 * 1024

NN = (((1,), (0,)), ((), ()))
NT = (((1,), (1,)), ((), ()))
TN = (((0,), (0,)), ((), ()))


def up(value, unit):
    return (value + unit - 1) // unit * unit


SP = up(SEQ, TILE)


def mm(a, b, dims=NN):
    return lax.dot_general(a, b, dims, preferred_element_type=F32)


def call(
    body, out_shape, scratch=(), flops=0, moved=0, prefetch=(), far_in=(), far_out=(), **more
):
    params = pltpu.CompilerParams(vmem_limit_bytes=VMEM_BYTES, **more)
    cost = pl.CostEstimate(flops=flops, bytes_accessed=moved, transcendentals=0)

    def spec(place, far, scalar=()):
        if place in scalar:
            return pl.BlockSpec(memory_space=pltpu.SMEM)
        return pl.BlockSpec(memory_space=pl.ANY if place in far else pltpu.VMEM)

    def run(*args):
        return pl.pallas_call(
            body,
            out_shape=out_shape,
            in_specs=[spec(place, far_in, prefetch) for place in range(len(args))],
            out_specs=tuple(spec(place, far_out) for place in range(len(out_shape))),
            scratch_shapes=list(scratch),
            compiler_params=params,
            cost_estimate=cost,
        )(*args)

    return run


def shape(dims, dtype=BF):
    return jax.ShapeDtypeStruct(dims, dtype)


def unit_norm(values):
    center = values - jnp.mean(values, -1, keepdims=True)
    spread = jnp.mean(center * center, -1, keepdims=True)
    inverse = lax.rsqrt(spread + EPSILON)
    return center * inverse, inverse


def norm_back(grad_rows, normed, inverse, gain):
    scaled = grad_rows * gain
    inner = (
        scaled
        - jnp.mean(scaled, -1, keepdims=True)
        - normed * jnp.mean(scaled * normed, -1, keepdims=True)
    )
    return inverse * inner, jnp.sum(grad_rows * normed, axis=0, keepdims=True)


def ids(shape_of, dim):
    return lax.broadcasted_iota(jnp.int32, shape_of, dim)


def slots_by_lane(routes, experts):
    rows = routes.shape[1]
    which = ids((experts, rows), 0).astype(F32)
    named = (routes[0:1] == which) | (routes[1:2] == which)
    before = (ids((rows, rows), 0) < ids((rows, rows), 1)).astype(F32).astype(BF)
    rank = mm(named.astype(F32).astype(BF), before)
    return jnp.where(named, rank, -1.0)


def take_rows(slots, in_ref, experts):
    count = in_ref.shape[0] // experts
    rows = slots.shape[0]
    place = ids((rows, count), 1).astype(F32)
    total = None
    for e in range(experts):
        pick = (place == slots[:, e : e + 1]).astype(F32).astype(BF)
        part = mm(pick, in_ref[e * count : (e + 1) * count, :])
        total = part if total is None else total + part
    return total


MESH = pl.DeviceIdType.MESH


def greet(axes):
    barrier = pltpu.get_barrier_semaphore()
    for name, size in axes:
        me = lax.axis_index(name)

        def hello(d, _, name=name, size=size, me=me):
            pl.semaphore_signal(
                barrier, inc=1, device_id={name: lax.rem(me + d, size)}, device_id_type=MESH
            )
            return 0

        lax.fori_loop(1, size, hello, 0)
    pl.semaphore_wait(barrier, sum(size - 1 for _, size in axes))


def remote(src, dst, send_sem, recv_sem, name, to):
    return pltpu.make_async_remote_copy(
        src_ref=src,
        dst_ref=dst,
        send_sem=send_sem,
        recv_sem=recv_sem,
        device_id={name: to},
        device_id_type=MESH,
    )


def each(size, step):
    def body(d, _):
        step(d)
        return 0

    lax.fori_loop(1, size, body, 0)


class Line:
    def __init__(self, size, own, everyone, send_sem, recv_sem):
        self.size, self.own, self.all = size, own, everyone
        self.send_sem, self.recv_sem = send_sem, recv_sem
        self.me = lax.axis_index("tensor")

    def copy(self, way, step, arriving):
        toward = 1 if way == 0 else -1
        owner = self.me - toward * (step + (1 if arriving else 0))
        src = self.own if step == 0 else self.all.at[owner]
        return remote(
            src, self.all.at[owner], self.send_sem.at[way, step], self.recv_sem.at[way, step],
            "tensor", self.me + toward,
        )

    def sends(self, way, step):
        last = self.size - 1
        if way == 0:
            return (self.me >= step) & (self.me < last)
        return (self.me <= last - step) & (self.me > 0)

    def receives(self, way, step):
        if way == 0:
            return self.me >= step + 1
        return self.me <= self.size - 2 - step

    def start(self, step):
        for way in (0, 1):
            pl.when(self.sends(way, step))(lambda way=way: self.copy(way, step, False).start())

    def arrive(self, step):
        for way in (0, 1):
            pl.when(self.receives(way, step))(
                lambda way=way: self.copy(way, step, True).wait_recv()
            )

    def finish(self):
        for step in range(self.size - 1):
            for way in (0, 1):
                pl.when(self.sends(way, step))(
                    lambda way=way, step=step: self.copy(way, step, False).wait_send()
                )


def gelu_parts(pre):
    density = jnp.exp(pre * pre * -0.5)
    size = jnp.abs(pre) * (0.5**0.5)
    t = 1.0 / (1.0 + 0.3275911 * size)
    series = t * (
        0.254829592
        + t * (-0.284496736 + t * (1.421413741 + t * (-1.453152027 + t * 1.061405429)))
    )
    tail = 0.5 * series * density
    return jnp.where(pre < 0, tail, 1.0 - tail), density * 0.3989422804014327


class Sums:
    def __init__(self, size, own, held, send_sem, recv_sem):
        self.size, self.own, self.held = size, own, held
        self.send_sem, self.recv_sem = send_sem, recv_sem
        self.me = lax.axis_index("tensor")

    def hops(self, way):
        return self.me if way == 0 else self.size - 1 - self.me

    def block(self, way, step):
        ahead = self.size - 1 + self.hops(way) - step
        return ahead if way == 0 else self.size - 1 - ahead

    def copy(self, way, step, part, first):
        toward = 1 if way == 0 else -1
        if first:
            src = self.own(self.block(way, step), part)
        else:
            src = self.held.at[way, max(step - 1, 0), part]
        return remote(
            src, self.held.at[way, step, part],
            self.send_sem.at[way, step, part], self.recv_sem.at[way, step, part],
            "tensor", self.me + toward,
        )

    def start_first(self, way, step, part):
        pl.when(self.hops(way) == 0)(lambda: self.copy(way, step, part, True).start())

    def middle(self, way, step):
        hops = self.hops(way)
        return (hops >= 1) & (hops <= step) & (hops < self.size - 1)

    def forward(self, step, part):
        for way in (0, 1):

            def go(way=way):
                self.copy(way, step - 1, part, False).wait_recv()
                held = self.held.at[way, step - 1, part]
                mine = self.own(self.block(way, step), part)
                add_into(held, mine)
                self.copy(way, step, part, False).start()

            pl.when(self.middle(way, step))(go)

    def last(self, part):
        for way in (0, 1):
            pl.when(self.hops(way) >= 1)(
                lambda way=way: self.copy(way, self.size - 2, part, False).wait_recv()
            )

    def finish(self):
        for part in (0, 1):
            for step in range(self.size - 1):
                for way in (0, 1):
                    sends = (self.hops(way) == 0) | self.middle(way, step)
                    pl.when(sends)(
                        lambda way=way, step=step, part=part: self.copy(
                            way, step, part, False
                        ).wait_send()
                    )


def add_into(held, mine):
    rows = held.shape[0]
    block = min(rows, 128)

    def body(r, _):
        at = pl.ds(pl.multiple_of(r * block, block), block)
        held[at, :] = (held[at, :].astype(F32) + mine[at, :].astype(F32)).astype(BF)
        return 0

    lax.fori_loop(0, rows // block, body, 0)


def block_kernel(
    experts, tensor, images, group,
    routes_ref, tokens_ref, cotangent_ref, noise_ref, gain1_ref, gain2_ref, router_own,
    w_out_own, w_qkv_own, w_in_own, w_back_own,
    output_ref, tokens_grad_ref, w_sum_ref, small_sum_ref, in_grad_ref, back_grad_ref,
    w_ref, w_router_ref, w_in_all, w_back_all, narrow, x_ref, cot_ref, rows_ref, lanes_ref,
    qkv_ref, attend_ref, mixed_ref, residual_ref,
    send_ref, routed_ref, early_send, early_ref, noise_send, noise_all, router_ref,
    hidden_ref, slope_ref, back_ref, held,
    wide_ref, back_grads, pair_ref, pieces, piece_send, piece_line,
    small_ref, small_plane, small_line_send, small_line,
    own_sem, first_sems, plane_sems, pair_sems, in_sems, in_back_sems, route_sems, early_sems, noise_sems,
    back_sems, out_sems, sum_send, sum_recv, w_pair_sems, w_sems, piece_sems, final_sems,
    small_sems, small_line_sems,
):
    own_rows = tokens_ref.shape[0]
    width = w_out_own.shape[0]
    wide = 4 * width
    heads = width // HD
    slots = noise_send.shape[2]
    pairs = experts * slots
    parts = w_in_all.shape[0]
    chunk = group * slots
    me_e, me_t = lax.axis_index("expert"), lax.axis_index("tensor")
    piece = D // experts

    chips = experts // CORES
    core = lax.rem(me_e, CORES)
    half = chips * piece

    def rows_at(e):
        at = lax.rem(e, CORES) * chips + e // CORES
        return pl.ds(pl.multiple_of(at * piece, piece), piece)

    def half_at(which):
        return pl.ds(pl.multiple_of(which * half, half), half)

    def chip_after(k):
        return lax.rem(me_e + CORES * k, experts)

    def chip_place(k, arriving):
        return lax.rem(me_e + experts - CORES * k, experts) if arriving else me_e

    mine = rows_at(me_e)

    def after(d):
        return lax.rem(me_e + d, experts)

    def place(d, arriving):
        return lax.rem(me_e + experts - d, experts) if arriving else me_e

    def swap_copy(src, dst, sems, d, arriving):
        to = after(d)
        return remote(
            src.at[to], dst.at[place(d, arriving)], sems.at[0, d], sems.at[1, d], "expert", to
        )

    def line_copy(src, dst, sems, d, arriving):
        owner = lax.rem(me_t + tensor - d, tensor) if arriving else me_t
        return remote(
            src, dst(owner), sems.at[0, d], sems.at[1, d],
            "tensor", lax.rem(me_t + d, tensor),
        )

    def first_copy(which, d, arriving):
        parts_of = (slice(0, 3), slice(3, 4))[which]
        src = w_ref.at[me_t, parts_of, mine] if which else w_qkv_own.at[:, mine]
        return line_copy(
            src, lambda owner: w_ref.at[owner, parts_of, mine], first_sems.at[which], d, arriving
        )

    def plane_copy(z, k, arriving):
        owner = lax.rem(me_t + tensor - z, tensor)
        block = w_ref.at[owner, :, rows_at(chip_place(k, arriving))]
        return remote(
            block, block, plane_sems.at[0, z, k], plane_sems.at[1, z, k], "expert", chip_after(k)
        )

    def pair_copy(z, arriving):
        owner = lax.rem(me_t + tensor - z, tensor)
        block = w_ref.at[owner, :, half_at(CORES - 1 - core if arriving else core)]
        return remote(
            block, block, pair_sems.at[0, z], pair_sems.at[1, z], "expert",
            me_e + CORES - 1 - 2 * core,
        )

    def slot_rows(e):
        return pl.ds(pl.multiple_of(e * slots, slots), slots)

    def flat_copy(src, dst, sems, d, arriving):
        return remote(
            src.at[slot_rows(after(d))], dst.at[slot_rows(place(d, arriving))],
            sems.at[0, d], sems.at[1, d], "expert", after(d),
        )

    def route_copy(d, arriving):
        return flat_copy(send_ref, routed_ref, route_sems, d, arriving)

    def early_copy(d, arriving):
        return flat_copy(early_send, early_ref, early_sems, d, arriving)

    def noise_copy(d, arriving):
        return swap_copy(noise_send, noise_all, noise_sems, d, arriving)

    def back_copy(d, arriving):
        return flat_copy(early_send, back_ref, back_sems, d, arriving)

    def out_copy(d, arriving):
        return flat_copy(send_ref, routed_ref, out_sems, d, arriving)

    def columns(t):
        return slice(t * wide, (t + 1) * wide)

    def w_pair_copy(t):
        return remote(
            wide_ref.at[half_at(CORES - 1 - core), columns(t)], pair_ref.at[t],
            w_pair_sems.at[0, t], w_pair_sems.at[1, t], "expert", me_e + CORES - 1 - 2 * core,
        )

    def w_copy(t, k, arriving):
        return remote(
            wide_ref.at[rows_at(chip_after(k)), columns(t)],
            pieces.at[chip_place(k, arriving) // CORES, t],
            w_sems.at[0, t, k], w_sems.at[1, t, k], "expert", chip_after(k),
        )

    def share_pair_sum(t):
        w_pair_copy(t).wait_recv()
        ours = half_at(core)
        pair_sum = wide_ref[ours, columns(t)].astype(F32) + pair_ref[t].astype(F32)
        wide_ref[ours, columns(t)] = pair_sum.astype(BF)
        each(chips, lambda k: w_copy(t, k, False).start())

    def piece_copy(d, arriving):
        src = piece_send.at[lax.rem(me_t + d, tensor)]
        return line_copy(src, lambda owner: piece_line.at[owner], piece_sems, d, arriving)

    def final_copy(d, arriving):
        block = w_sum_ref.at[rows_at(place(d, arriving))]
        return remote(block, block, final_sems.at[0, d], final_sems.at[1, d], "expert", after(d))

    def small_copy(d, arriving):
        return remote(
            small_ref, small_plane.at[place(d, arriving)], small_sems.at[0, d],
            small_sems.at[1, d], "expert", after(d),
        )

    def small_line_copy(d, arriving):
        return line_copy(
            small_line_send, lambda owner: small_line.at[owner], small_line_sems, d, arriving
        )

    greet((("expert", experts), ("tensor", tensor)))
    each(tensor, lambda d: first_copy(0, d, False).start())
    line_in = Line(tensor, w_in_own, w_in_all, in_sems.at[0], in_sems.at[1])
    line_back = Line(tensor, w_back_own, w_back_all, in_back_sems.at[0], in_back_sems.at[1])
    w_ref[me_t, 3] = w_out_own[...].T
    each(tensor, lambda d: first_copy(1, d, False).start())
    line_in.start(0)
    keep = [
        pltpu.make_async_copy(w_qkv_own, w_ref.at[me_t, 0:3], own_sem.at[0]),
        pltpu.make_async_copy(w_in_own, w_in_all.at[me_t], own_sem.at[1]),
        pltpu.make_async_copy(w_back_own, w_back_all.at[me_t], own_sem.at[2]),
    ]
    for copy in keep:
        copy.start()

    def spread(compact, to_ref, fill=0.0):
        columns = compact.shape[1]
        narrow[0:own_rows, 0:columns] = compact
        to_ref[...] = jnp.full(to_ref.shape, fill, F32)
        for i in range(images):
            to_ref[i * SP : i * SP + SEQ, 0:columns] = narrow[
                i * SEQ : (i + 1) * SEQ, 0:columns
            ]

    def compact(padded):
        for i in range(images):
            narrow[i * SEQ : (i + 1) * SEQ, :] = padded[i * SP : i * SP + SEQ, :]
        return narrow[0:own_rows, :]

    def spread_lanes(packed, fill):
        gap = jnp.full((packed.shape[0], SP - SEQ), fill, F32)
        blocks = []
        for i in range(images):
            blocks += [packed[:, i * SEQ : (i + 1) * SEQ], gap]
        return jnp.concatenate(blocks, axis=1)

    noise = spread_lanes(noise_ref[...], 0.0)
    high = noise.astype(BF).astype(F32)
    middle = (noise - high).astype(BF).astype(F32)
    low = noise - high - middle
    noise_parts = [high, middle, low]
    if noise_send.shape[1] > 3 * experts:
        noise_parts.append(jnp.zeros((noise_send.shape[1] - 3 * experts, noise.shape[1]), F32))
    noise = jnp.concatenate(noise_parts, axis=0).astype(BF)
    slots_by = slots_by_lane(spread_lanes(routes_ref[...].astype(F32), -1.0), experts)
    lanes_ref[...] = slots_by
    no_slots = jnp.zeros((LANES - experts, slots_by.shape[1]), F32)
    rows_ref[...] = jnp.concatenate([slots_by, no_slots], axis=0).T
    no_router = jnp.zeros((LANES - experts, D), F32)
    w_router_ref[...] = jnp.concatenate(
        [router_own[...].astype(F32), no_router], axis=0
    ).astype(BF)
    spread(cotangent_ref[...].astype(F32), cot_ref)
    cot_low = cot_ref[...].astype(BF)
    spot = ids((slots, lanes_ref.shape[1]), 0).astype(F32)

    def pick_of(e):
        return (spot == lanes_ref[pl.ds(e, 1), :]).astype(F32).astype(BF)

    def forward_piece(z):
        first_copy(0, z, True).wait_recv()
        first_copy(1, z, True).wait_recv()
        each(chips, lambda k: plane_copy(z, k, False).start())

    each(tensor, forward_piece)
    for d in range(1, experts + 1):
        e = after(d)
        pick = pick_of(e)
        rows_of_e = mm(pick, cot_low).astype(BF)
        noise_of_e = mm(noise, pick, NT).astype(BF)
        if d < experts:
            early_send[slot_rows(e), :] = rows_of_e
            noise_send[e] = noise_of_e
            early_copy(d, False).start()
            noise_copy(d, False).start()
        else:
            early_ref[slot_rows(e), :] = rows_of_e
            noise_all[e] = noise_of_e
    spread(tokens_ref[...].astype(F32), x_ref)
    x = x_ref[...]
    unit1, inverse1 = unit_norm(x)
    normed1 = (unit1 * gain1_ref[...]).astype(BF)
    line_in.arrive(0)
    if tensor > 2:
        line_in.start(1)

    def forward_half(z):
        each(chips, lambda k: plane_copy(z, k, True).wait_recv())
        pair_copy(z, False).start()

    each(tensor, forward_half)
    keep[0].wait()
    each(tensor, lambda z: pair_copy(z, True).wait_recv())

    def qkv_weights(t):
        return jnp.concatenate([w_ref[t, c] for c in range(3)], axis=1)

    lane = ids((SP, width), 1) // HD
    live = ids((SP, SP), 1) < SEQ
    for t in range(tensor):
        qkv_ref[t] = mm(normed1, qkv_weights(t)).astype(BF)
        for i in range(images):
            rows = slice(i * SP, (i + 1) * SP)
            q = qkv_ref[t, rows, 0:width]
            k = qkv_ref[t, rows, width : 2 * width]
            v = qkv_ref[t, rows, 2 * width : 3 * width]
            mixed = None
            for j in range(heads):
                q_j = q if heads == 1 else jnp.where(lane == j, q, jnp.zeros_like(q))
                scores = mm(q_j, k, NT) * HD ** (-0.5)
                scores = jnp.where(live, scores, -1e30)
                power = jnp.exp(scores - jnp.max(scores, -1, keepdims=True))
                attend = (power / jnp.sum(power, -1, keepdims=True)).astype(BF)
                attend_ref[i, t * heads + j] = attend
                part = mm(attend, v)
                mixed = part if mixed is None else jnp.where(lane == j, part, mixed)
            mixed_ref[t, rows, :] = mixed.astype(BF)
    residual = x
    for t in range(tensor):
        residual = residual + mm(mixed_ref[t], w_ref[t, 3], NT)
    residual_ref[...] = residual
    unit2, inverse2 = unit_norm(residual)
    normed2 = (unit2 * gain2_ref[...]).astype(BF)
    for d in range(1, experts + 1):
        e = after(d)
        rows_of_e = mm(pick_of(e), normed2).astype(BF)
        if d < experts:
            send_ref[slot_rows(e), :] = rows_of_e
            route_copy(d, False).start()
        else:
            routed_ref[slot_rows(e), :] = rows_of_e
    for step in range(1, tensor - 1):
        line_in.arrive(step)
        if step + 1 < tensor - 1:
            line_in.start(step + 1)
        if step == max(1, tensor - 3):
            line_back.start(0)
    if tensor == 2:
        line_back.start(0)
    keep[1].wait()

    fold_from, fold_to = ids((noise_all.shape[1], LANES), 0), ids((noise_all.shape[1], LANES), 1)
    fold = (
        (fold_from < 3 * experts) & (lax.rem(fold_from, experts) == fold_to)
    ).astype(F32).astype(BF)
    expert_lane = ids((chunk, LANES), 1)
    groups = experts // group

    def block_rows(at):
        return pl.ds(pl.multiple_of(at * chunk, chunk), chunk)

    def hidden_units(turn, _):
        at = lax.rem(me_e // group + groups - turn, groups)
        for k in range(group):
            d = lax.rem(me_e + experts - (at * group + k), experts)

            @pl.when(d > 0)
            def _(d=d):
                route_copy(d, True).wait_recv()
                early_copy(d, True).wait_recv()
                noise_copy(d, True).wait_recv()

        @pl.when(turn == groups // 2)
        def _():
            for step in range(0, tensor - 3):
                line_back.arrive(step)
                line_back.start(step + 1)

        rows = block_rows(at)
        came = routed_ref[rows, :]
        added = [mm(noise_all[at * group + k], fold, TN) for k in range(group)]
        added = added[0] if group == 1 else jnp.concatenate(added, axis=0)
        logits = jnp.where(expert_lane < experts, mm(came, w_router_ref[...], NT) + added, -1e30)
        power = jnp.exp(logits - jnp.max(logits, -1, keepdims=True))
        router = power / jnp.sum(power, -1, keepdims=True)
        router_ref[rows, :] = router
        gate = jnp.sum(jnp.where(expert_lane == me_e, router, 0.0), -1, keepdims=True)
        early_ref[rows, :] = (gate * early_ref[rows, :].astype(F32)).astype(BF)
        for f in range(parts):
            pre = mm(came, w_in_all[f])
            normal, density = gelu_parts(pre)
            hidden_ref[f, rows, :] = (pre * normal).astype(BF)
            slope_ref[f, rows, :] = (normal + pre * density).astype(BF)
        return 0

    lax.fori_loop(0, groups, hidden_units, 0)

    def grads_at(block, part):
        return back_grads.at[block] if part else slope_ref.at[block, 0:D]

    sums = Sums(tensor, grads_at, held, sum_send, sum_recv)
    order = []
    for step in range(tensor):
        for f in (tensor - 1 - step, step):
            if f not in order:
                order.append(f)

    def turn_rows(ref):
        def body(at, _):
            rows = pl.ds(pl.multiple_of(at * LANES, LANES), LANES)
            wide_ref[:, rows] = ref[rows, :].T
            return 0

        lax.fori_loop(0, pairs // LANES, body, 0)

    def weight_grads(part, right):
        for f in order:
            block = mm(wide_ref[:, 0:pairs], right[f, 0:pairs, :]).astype(BF)
            grads_at(f, part)[...] = block
            for step in range(tensor - 1):
                for way, to in ((0, tensor - 1 - step), (1, step)):
                    if to == f:
                        sums.start_first(way, step, part)

    turn_rows(early_ref)
    weight_grads(1, hidden_ref)
    turn_rows(routed_ref)

    for step in range(max(tensor - 3, 0), tensor - 2):
        line_back.arrive(step)
        line_back.start(step + 1)
    keep[2].wait()

    def early_sent(d):
        early_copy(d, False).wait_send()
        route_copy(d, False).wait_send()

    each(experts, early_sent)

    small_ref[...] = jnp.zeros_like(small_ref)

    def near(k):
        def from_low(me):
            below = (me - k + tensor) // tensor
            return below * (me - k) + (1 - below) * k

        low = 1 - (2 * me_t) // tensor
        mirrored = tensor - 1 - from_low(tensor - 1 - me_t)
        return low * from_low(me_t) + (1 - low) * mirrored

    def unit_part(k, rows):
        f = near(k)
        w_b = w_back_all[f]
        out = mm(hidden_ref[f, rows, :], w_b)
        d_pre = (mm(early_ref[rows, :], w_b, NT) * slope_ref[f, rows, :].astype(F32)).astype(BF)
        slope_ref[f, rows, :] = d_pre
        return out, mm(d_pre, w_in_all[f], NT)

    def near_rows(at, _):
        rows = block_rows(at)
        out, back = unit_part(0, rows)
        for k in range(1, tensor - 1):
            more_out, more_back = unit_part(k, rows)
            out, back = out + more_out, back + more_back
        send_ref[rows, :] = out.astype(BF)
        early_send[rows, :] = back.astype(BF)
        return 0

    lax.fori_loop(0, groups, near_rows, 0)
    line_steps = [(step, part) for part in (1, 0) for step in range(1, tensor - 1)]

    def next_sum():
        if line_steps:
            sums.forward(*line_steps.pop(0))

    next_sum()
    line_back.arrive(tensor - 2)

    def far_rows(turn, _):
        at = lax.rem(me_e // group + groups - turn, groups)
        rows = block_rows(at)
        router = router_ref[rows, :]
        own_lane = expert_lane == me_e
        gate = jnp.sum(jnp.where(own_lane, router, 0.0), -1, keepdims=True)
        out, back = unit_part(tensor - 1, rows)
        out = (out + send_ref[rows, :].astype(F32)).astype(BF).astype(F32)
        back = back + early_send[rows, :].astype(F32)
        d_gate = jnp.sum(early_ref[rows, :].astype(F32) * out, -1, keepdims=True)
        d_logits = (d_gate * (own_lane.astype(F32) - router)).astype(BF)
        early_send[rows, :] = (back + mm(d_logits, w_router_ref[...])).astype(BF)
        send_ref[rows, :] = (gate * out).astype(BF)
        small_ref[0:experts, :] += mm(d_logits, routed_ref[rows, :], TN)[0:experts]
        for k in range(group):
            e = at * group + k
            d = lax.rem(e + experts - me_e, experts)

            @pl.when(d > 0)
            def _(d=d):
                back_copy(d, False).start()

            @pl.when(d == 0)
            def _(e=e):
                back_ref[slot_rows(e), :] = early_send[slot_rows(e), :]
                routed_ref[slot_rows(e), :] = send_ref[slot_rows(e), :]

        return 0

    lax.fori_loop(0, groups, far_rows, 0)

    weight_grads(0, slope_ref)
    next_sum()

    each(experts, lambda d: back_copy(d, True).wait_recv())
    slots_of = rows_ref[:, 0:experts]
    d_normed2 = take_rows(slots_of, back_ref, experts)
    unit2, inverse2 = unit_norm(residual_ref[...])
    d_rows, norm2 = norm_back(d_normed2, unit2, inverse2, gain2_ref[...])
    small_ref[experts + 1 : experts + 2, :] = norm2
    d_residual = cot_ref[...] + d_rows
    cot_ref[...] = d_residual
    d_attention = d_residual.astype(BF)
    scaling = HD ** (-0.5)
    unit1, inverse1 = unit_norm(x_ref[...])
    normed1 = (unit1 * gain1_ref[...]).astype(BF)
    for t in range(tensor):
        wide_ref[:, t * wide + 3 * width : (t + 1) * wide] = mm(d_attention, mixed_ref[t], TN).astype(BF)
        d_mixed = mm(d_attention, w_ref[t, 3]).astype(BF)
        for i in range(images):
            rows = slice(i * SP, (i + 1) * SP)
            q = qkv_ref[t, rows, 0:width]
            k = qkv_ref[t, rows, width : 2 * width]
            v = qkv_ref[t, rows, 2 * width : 3 * width]
            do = d_mixed[rows]
            dq = dk = dv = None
            for j in range(heads):
                own = lane == j
                do_j = do if heads == 1 else jnp.where(own, do, jnp.zeros_like(do))
                q_j = q if heads == 1 else jnp.where(own, q, jnp.zeros_like(q))
                attend_low = attend_ref[i, t * heads + j]
                attend = attend_low.astype(F32)
                part_v = mm(attend_low, do_j, TN)
                d_attend = mm(do_j, v, NT)
                inner = jnp.sum(attend * d_attend, -1, keepdims=True)
                ds = (attend * (d_attend - inner)).astype(BF)
                part_q = mm(ds, k) * scaling
                part_k = mm(ds, q_j, TN) * scaling
                dq = part_q if dq is None else jnp.where(own, part_q, dq)
                dk = part_k if dk is None else dk + part_k
                dv = part_v if dv is None else dv + part_v
            qkv_ref[t, rows, 0:width] = dq.astype(BF)
            qkv_ref[t, rows, width : 2 * width] = dk.astype(BF)
            qkv_ref[t, rows, 2 * width : 3 * width] = dv.astype(BF)
        wide_ref[:, t * wide : t * wide + 3 * width] = mm(normed1, qkv_ref[t], TN).astype(BF)
        w_pair_copy(t).start()
        if t > 0:
            share_pair_sum(t - 1)
    share_pair_sum(tensor - 1)
    next_sum()
    d_normed1 = None
    for t in range(tensor):
        part = mm(qkv_ref[t], qkv_weights(t), NT)
        d_normed1 = part if d_normed1 is None else d_normed1 + part
    d_rows, norm1 = norm_back(d_normed1, unit1, inverse1, gain1_ref[...])
    small_ref[experts : experts + 1, :] = norm1
    each(experts, lambda d: small_copy(d, False).start())
    each(experts, lambda d: out_copy(d, False).start())
    small_plane[me_e] = small_ref[...]
    tokens_grad_ref[...] = compact(cot_ref[...] + d_rows)

    for t in range(tensor):
        pieces[me_e // CORES, t] = wide_ref[mine, columns(t)]
    for t in range(tensor):
        each(chips, lambda k, t=t: w_copy(t, k, True).wait_recv())
        total = pieces[0, t].astype(F32)
        for e in range(1, chips):
            total = total + pieces[e, t].astype(F32)
        piece_send[t] = total.astype(BF)
    each(tensor, lambda d: piece_copy(d, False).start())
    piece_line[me_t] = piece_send[me_t]
    each(experts, lambda d: small_copy(d, True).wait_recv())
    total = small_plane[0]
    for e in range(1, experts):
        total = total + small_plane[e]
    small_line_send[...] = total
    each(tensor, lambda d: small_line_copy(d, False).start())
    small_line[me_t] = total
    each(tensor, lambda d: piece_copy(d, True).wait_recv())
    total = piece_line[0].astype(F32)
    for t in range(1, tensor):
        total = total + piece_line[t].astype(F32)
    w_sum_ref[mine, :] = total.astype(BF)
    each(experts, lambda d: final_copy(d, False).start())
    while line_steps:
        next_sum()

    each(experts, lambda d: out_copy(d, True).wait_recv())
    output = residual_ref[...] + take_rows(slots_of, routed_ref, experts)
    output_ref[...] = compact(output).astype(BF)

    each(tensor, lambda d: small_line_copy(d, True).wait_recv())
    total = small_line[0]
    for t in range(1, tensor):
        total = total + small_line[t]
    small_sum_ref[...] = total
    each(experts, lambda d: final_copy(d, True).wait_recv())

    for part in (0, 1):
        sums.last(part)
        total = grads_at(me_t, part)[...].astype(F32)
        for way in (0, 1):
            came = held[way, tensor - 2, part].astype(F32)
            total = total + jnp.where(sums.hops(way) >= 1, came, jnp.zeros_like(came))
        if part == 0:
            in_grad_ref[...] = total.astype(BF)
        else:
            back_grad_ref[...] = total.T.astype(BF)

    sums.finish()
    line_in.finish()
    line_back.finish()

    def sent(d):
        noise_copy(d, False).wait_send()
        back_copy(d, False).wait_send()
        out_copy(d, False).wait_send()
        final_copy(d, False).wait_send()
        small_copy(d, False).wait_send()

    each(experts, sent)

    def sent_line(d):
        first_copy(0, d, False).wait_send()
        first_copy(1, d, False).wait_send()
        piece_copy(d, False).wait_send()
        small_line_copy(d, False).wait_send()
        pair_copy(d, False).wait_send()
        each(chips, lambda k: plane_copy(d, k, False).wait_send())

    each(tensor, sent_line)
    for t in range(tensor):
        w_pair_copy(t).wait_send()
        each(chips, lambda k, t=t: w_copy(t, k, False).wait_send())


def finish_kernel(
    experts, output_in, tokens_in, w_sum_ref, small_ref, in_ref, back_ref,
    output_ref, tokens_ref, norm1_ref, qkv_ref, out_ref, norm2_ref, router_ref,
    in_grad_ref, back_grad_ref,
):
    output_ref[...] = output_in[...]
    tokens_ref[...] = tokens_in[...]
    width = out_ref.shape[0]
    for c in range(3):
        qkv_ref[c] = w_sum_ref[:, c * width : (c + 1) * width].astype(F32)
    out_ref[...] = w_sum_ref[:, 3 * width : 4 * width].T.astype(F32)
    router_ref[...] = small_ref[0:experts, :]
    norm1_ref[...] = small_ref[experts : experts + 1, :]
    norm2_ref[...] = small_ref[experts + 1 : experts + 2, :]
    in_grad_ref[...] = in_ref[...].astype(F32)
    back_grad_ref[...] = back_ref[...].astype(F32)


def per_device(
    tokens, norm1_gain, w_qkv, w_out, norm2_gain, w_router, noise, routes, w_in, w_back, cotangent
):
    own_rows = tokens.shape[0]
    experts = noise.shape[1]
    tensor = lax.axis_size("tensor")
    images = own_rows // SEQ
    rows = images * SP
    capacity = (2 * own_rows * TOP + experts - 1) // experts
    slots = up(capacity, TILE)
    group = max(g for g in range(1, experts + 1) if experts % g == 0 and g * slots <= 2 * SP)
    width = w_out.shape[0]
    hidden = w_in.shape[2]
    heads = tensor * width // HD
    piece = D // experts
    small_rows = up(experts + 2, 8)
    noise_rows = up(3 * experts, TILE)
    pairs = experts * slots
    dma = pltpu.SemaphoreType.DMA
    bf, f32 = (lambda *dims: pltpu.VMEM(dims, BF)), (lambda *dims: pltpu.VMEM(dims, F32))

    output, grad_tokens, w_sum, small, grad_in, grad_back = call(
        functools.partial(block_kernel, experts, tensor, images, group),
        (
            shape((own_rows, D)),
            shape((own_rows, D), F32),
            shape((D, 4 * width)),
            shape((small_rows, D), F32),
            shape((D, hidden)),
            shape((hidden, D)),
        ),
        scratch=(
            bf(tensor, 4, D, width),
            bf(LANES, D),
            bf(tensor, D, hidden),
            bf(tensor, hidden, D),
            f32(up(own_rows, TILE), D),
            f32(rows, D),
            f32(rows, D),
            f32(rows, LANES),
            f32(experts, rows),
            bf(tensor, rows, 3 * width),
            bf(images, heads, SP, SP),
            bf(tensor, rows, width),
            f32(rows, D),
            bf(pairs, D),
            bf(pairs, D),
            bf(pairs, D),
            bf(pairs, D),
            bf(experts, noise_rows, slots),
            bf(experts, noise_rows, slots),
            f32(pairs, LANES),
            bf(tensor, pairs, hidden),
            bf(tensor, max(pairs, D), hidden),
            bf(pairs, D),
            bf(2, tensor - 1, 2, D, hidden),
            bf(D, max(pairs, tensor * 4 * width)),
            bf(tensor, D, hidden),
            bf(tensor, D // CORES, 4 * width),
            bf(experts // CORES, tensor, piece, 4 * width),
            bf(tensor, piece, 4 * width),
            bf(tensor, piece, 4 * width),
            f32(small_rows, D),
            f32(experts, small_rows, D),
            f32(small_rows, D),
            f32(tensor, small_rows, D),
            dma((3,)),
            dma((2, 2, tensor)),
            dma((2, tensor, experts // CORES)),
            dma((2, tensor)),
            dma((2, 2, tensor - 1)),
            dma((2, 2, tensor - 1)),
            dma((2, experts)),
            dma((2, experts)),
            dma((2, experts)),
            dma((2, experts)),
            dma((2, experts)),
            dma((2, tensor - 1, 2)),
            dma((2, tensor - 1, 2)),
            dma((2, tensor)),
            dma((2, tensor, experts // CORES)),
            dma((2, tensor)),
            dma((2, experts)),
            dma((2, experts)),
            dma((2, tensor)),
        ),
        far_in=(8, 9, 10),
        collective_id=0,
        has_side_effects=True,
    )(
        routes.T, tokens, cotangent, noise.T, norm1_gain.reshape(1, D), norm2_gain.reshape(1, D),
        w_router.T, w_out, w_qkv.transpose(1, 0, 2), w_in[0], w_back[0],
    )
    output, grad_tokens, norm1, grad_qkv, grad_out, norm2, router, grad_in, grad_back = call(
        functools.partial(finish_kernel, experts),
        (
            shape((own_rows, D)),
            shape((own_rows, D), F32),
            shape((1, D), F32),
            shape((3, D, width), F32),
            shape((width, D), F32),
            shape((1, D), F32),
            shape((experts, D), F32),
            shape((D, hidden), F32),
            shape((hidden, D), F32),
        ),
    )(output, grad_tokens, w_sum, small, grad_in, grad_back)
    return (
        output,
        grad_tokens,
        norm1.reshape(D),
        grad_qkv.transpose(1, 0, 2),
        grad_out,
        norm2.reshape(D),
        router.T,
        grad_in[None],
        grad_back[None],
    )


def solution(mesh):
    rows = P(("expert", "tensor"), None)
    placed = (
        rows,
        P(),
        P(None, None, "tensor"),
        P("tensor", None),
        P(),
        P(),
        rows,
        rows,
        P("expert", None, "tensor"),
        P("expert", "tensor", None),
        rows,
    )
    return jax.shard_map(
        per_device,
        mesh=mesh,
        in_specs=placed,
        out_specs=(
            rows,
            rows,
            P(),
            P(None, None, "tensor"),
            P("tensor", None),
            P(),
            P(),
            P("expert", None, "tensor"),
            P("expert", "tensor", None),
        ),
        check_vma=False,
    )
```

```python
import functools

import jax
import jax.numpy as jnp
from jax import lax
from jax.experimental import pallas as pl
from jax.experimental.pallas import tpu as pltpu
from jax.sharding import PartitionSpec as P

D = 512
HD = 64
CORES = 2
TOP = 2
SEQ = 197
LANES = 128
TILE = 16
EPSILON = 1e-06
DENSITY = 0.3989422804014327
TAIL = 0.5 / DENSITY
BF = jnp.bfloat16
F32 = jnp.float32
VMEM_BYTES = 62 * 1024 * 1024

NN = (((1,), (0,)), ((), ()))
NT = (((1,), (1,)), ((), ()))
TN = (((0,), (0,)), ((), ()))


def up(value, unit):
    return (value + unit - 1) // unit * unit


SP = up(SEQ, TILE)


def mm(a, b, dims=NN):
    return lax.dot_general(a, b, dims, preferred_element_type=F32)


def call(
    body, out_shape, scratch=(), flops=0, moved=0, prefetch=(), far_in=(), far_out=(), **more
):
    params = pltpu.CompilerParams(vmem_limit_bytes=VMEM_BYTES, **more)
    cost = pl.CostEstimate(flops=flops, bytes_accessed=moved, transcendentals=0)

    def spec(place, far, scalar=()):
        if place in scalar:
            return pl.BlockSpec(memory_space=pltpu.SMEM)
        return pl.BlockSpec(memory_space=pl.ANY if place in far else pltpu.VMEM)

    def run(*args):
        return pl.pallas_call(
            body,
            out_shape=out_shape,
            in_specs=[spec(place, far_in, prefetch) for place in range(len(args))],
            out_specs=tuple(spec(place, far_out) for place in range(len(out_shape))),
            scratch_shapes=list(scratch),
            compiler_params=params,
            cost_estimate=cost,
        )(*args)

    return run


def shape(dims, dtype=BF):
    return jax.ShapeDtypeStruct(dims, dtype)


def unit_norm(values):
    center = values - jnp.mean(values, -1, keepdims=True)
    spread = jnp.mean(center * center, -1, keepdims=True)
    inverse = lax.rsqrt(spread + EPSILON)
    return center * inverse, inverse


def norm_back(grad_rows, normed, inverse, gain):
    scaled = grad_rows * gain
    inner = (
        scaled
        - jnp.mean(scaled, -1, keepdims=True)
        - normed * jnp.mean(scaled * normed, -1, keepdims=True)
    )
    return inverse * inner, jnp.sum(grad_rows * normed, axis=0, keepdims=True)


def ids(shape_of, dim):
    return lax.broadcasted_iota(jnp.int32, shape_of, dim)


def slots_by_lane(routes, experts):
    rows = routes.shape[1]
    which = ids((experts, rows), 0).astype(F32)
    named = (routes[0:1] == which) | (routes[1:2] == which)
    before = (ids((rows, rows), 0) < ids((rows, rows), 1)).astype(F32).astype(BF)
    rank = mm(named.astype(F32).astype(BF), before)
    return jnp.where(named, rank, -1.0)


def take_rows(slots, in_ref, experts):
    count = in_ref.shape[0] // experts
    rows = slots.shape[0]
    place = ids((rows, count), 1).astype(F32)
    total = None
    for e in range(experts):
        pick = (place == slots[:, e : e + 1]).astype(F32).astype(BF)
        part = mm(pick, in_ref[e * count : (e + 1) * count, :])
        total = part if total is None else total + part
    return total


MESH = pl.DeviceIdType.MESH


def greet(axes):
    barrier = pltpu.get_barrier_semaphore()
    for name, size in axes:
        me = lax.axis_index(name)

        def hello(d, _, name=name, size=size, me=me):
            pl.semaphore_signal(
                barrier, inc=1, device_id={name: lax.rem(me + d, size)}, device_id_type=MESH
            )
            return 0

        lax.fori_loop(1, size, hello, 0)
    pl.semaphore_wait(barrier, sum(size - 1 for _, size in axes))


def remote(src, dst, send_sem, recv_sem, name, to):
    return pltpu.make_async_remote_copy(
        src_ref=src,
        dst_ref=dst,
        send_sem=send_sem,
        recv_sem=recv_sem,
        device_id={name: to},
        device_id_type=MESH,
    )


def each(size, step):
    def body(d, _):
        step(d)
        return 0

    lax.fori_loop(1, size, body, 0)


class Line:
    def __init__(self, size, own, everyone, send_sem, recv_sem):
        self.size, self.own, self.all = size, own, everyone
        self.send_sem, self.recv_sem = send_sem, recv_sem
        self.me = lax.axis_index("tensor")

    def copy(self, way, step, arriving):
        toward = 1 if way == 0 else -1
        owner = self.me - toward * (step + (1 if arriving else 0))
        src = self.own if step == 0 else self.all.at[owner]
        return remote(
            src, self.all.at[owner], self.send_sem.at[way, step], self.recv_sem.at[way, step],
            "tensor", self.me + toward,
        )

    def sends(self, way, step):
        last = self.size - 1
        if way == 0:
            return (self.me >= step) & (self.me < last)
        return (self.me <= last - step) & (self.me > 0)

    def receives(self, way, step):
        if way == 0:
            return self.me >= step + 1
        return self.me <= self.size - 2 - step

    def start(self, step):
        for way in (0, 1):
            pl.when(self.sends(way, step))(lambda way=way: self.copy(way, step, False).start())

    def arrive(self, step):
        for way in (0, 1):
            pl.when(self.receives(way, step))(
                lambda way=way: self.copy(way, step, True).wait_recv()
            )

    def finish(self):
        for step in range(self.size - 1):
            for way in (0, 1):
                pl.when(self.sends(way, step))(
                    lambda way=way, step=step: self.copy(way, step, False).wait_send()
                )


def gelu_parts(pre):
    density = jnp.exp2(pre * pre * (-0.5 * 1.4426950408889634)) * DENSITY
    t = pl.reciprocal(1.0 + jnp.abs(pre * (0.3275911 * 0.5**0.5)), approx=True)
    series = t * (
        0.254829592 * TAIL
        + t
        * (
            -0.284496736 * TAIL
            + t * (1.421413741 * TAIL + t * (-1.453152027 * TAIL + t * (1.061405429 * TAIL)))
        )
    )
    tail = series * density
    return jnp.where(pre < 0, tail, 1.0 - tail), density


class Sums:
    def __init__(self, size, own, held, send_sem, recv_sem):
        self.size, self.own, self.held = size, own, held
        self.send_sem, self.recv_sem = send_sem, recv_sem
        self.me = lax.axis_index("tensor")

    def hops(self, way):
        return self.me if way == 0 else self.size - 1 - self.me

    def block(self, way, step):
        ahead = self.size - 1 + self.hops(way) - step
        return ahead if way == 0 else self.size - 1 - ahead

    def copy(self, way, step, part, first):
        toward = 1 if way == 0 else -1
        if first:
            src = self.own(self.block(way, step), part)
        else:
            src = self.held.at[way, max(step - 1, 0), part]
        return remote(
            src, self.held.at[way, step, part],
            self.send_sem.at[way, step, part], self.recv_sem.at[way, step, part],
            "tensor", self.me + toward,
        )

    def start_first(self, way, step, part):
        pl.when(self.hops(way) == 0)(lambda: self.copy(way, step, part, True).start())

    def middle(self, way, step):
        hops = self.hops(way)
        return (hops >= 1) & (hops <= step) & (hops < self.size - 1)

    def forward(self, step, part):
        for way in (0, 1):

            def go(way=way):
                self.copy(way, step - 1, part, False).wait_recv()
                held = self.held.at[way, step - 1, part]
                mine = self.own(self.block(way, step), part)
                add_into(held, mine)
                self.copy(way, step, part, False).start()

            pl.when(self.middle(way, step))(go)

    def last(self, part):
        for way in (0, 1):
            pl.when(self.hops(way) >= 1)(
                lambda way=way: self.copy(way, self.size - 2, part, False).wait_recv()
            )

    def finish(self):
        for part in (0, 1):
            for step in range(self.size - 1):
                for way in (0, 1):
                    sends = (self.hops(way) == 0) | self.middle(way, step)
                    pl.when(sends)(
                        lambda way=way, step=step, part=part: self.copy(
                            way, step, part, False
                        ).wait_send()
                    )


def add_into(held, mine):
    rows = held.shape[0]
    block = min(rows, 128)

    def body(r, _):
        at = pl.ds(pl.multiple_of(r * block, block), block)
        held[at, :] = (held[at, :].astype(F32) + mine[at, :].astype(F32)).astype(BF)
        return 0

    lax.fori_loop(0, rows // block, body, 0)


def block_kernel(
    experts, tensor, images, group,
    routes_ref, tokens_ref, cotangent_ref, noise_ref, gain1_ref, gain2_ref, router_own,
    w_out_own, w_qkv_own, w_in_own, w_back_own,
    output_ref, tokens_grad_ref, w_sum_ref, small_sum_ref, in_grad_ref, back_grad_ref,
    w_ref, w_router_ref, w_in_all, w_back_all, narrow, x_ref, cot_ref, rows_ref, lanes_ref,
    qkv_ref, attend_ref, mixed_ref, residual_ref,
    send_ref, routed_ref, early_send, early_ref, noise_send, noise_all, router_ref,
    hidden_ref, slope_ref, back_ref, held,
    wide_ref, back_grads, pair_ref, pieces, piece_send, piece_line,
    small_ref, small_plane, small_line_send, small_line,
    own_sem, first_sems, plane_sems, pair_sems, in_sems, in_back_sems, route_sems, early_sems, noise_sems,
    back_sems, out_sems, sum_send, sum_recv, w_pair_sems, w_sems, piece_sems, final_sems,
    small_sems, small_line_sems,
):
    own_rows = tokens_ref.shape[0]
    width = w_out_own.shape[0]
    wide = 4 * width
    heads = width // HD
    slots = noise_send.shape[2]
    pairs = experts * slots
    parts = w_in_all.shape[0]
    chunk = group * slots
    me_e, me_t = lax.axis_index("expert"), lax.axis_index("tensor")
    piece = D // experts

    chips = experts // CORES
    core = lax.rem(me_e, CORES)
    half = chips * piece

    def rows_at(e):
        at = lax.rem(e, CORES) * chips + e // CORES
        return pl.ds(pl.multiple_of(at * piece, piece), piece)

    def half_at(which):
        return pl.ds(pl.multiple_of(which * half, half), half)

    def chip_after(k):
        return lax.rem(me_e + CORES * k, experts)

    def chip_place(k, arriving):
        return lax.rem(me_e + experts - CORES * k, experts) if arriving else me_e

    mine = rows_at(me_e)

    def after(d):
        return lax.rem(me_e + d, experts)

    def place(d, arriving):
        return lax.rem(me_e + experts - d, experts) if arriving else me_e

    def swap_copy(src, dst, sems, d, arriving):
        to = after(d)
        return remote(
            src.at[to], dst.at[place(d, arriving)], sems.at[0, d], sems.at[1, d], "expert", to
        )

    def line_copy(src, dst, sems, d, arriving):
        owner = lax.rem(me_t + tensor - d, tensor) if arriving else me_t
        return remote(
            src, dst(owner), sems.at[0, d], sems.at[1, d],
            "tensor", lax.rem(me_t + d, tensor),
        )

    def first_copy(which, d, arriving):
        parts_of = (slice(0, 3), slice(3, 4))[which]
        src = w_ref.at[me_t, parts_of, mine] if which else w_qkv_own.at[:, mine]
        return line_copy(
            src, lambda owner: w_ref.at[owner, parts_of, mine], first_sems.at[which], d, arriving
        )

    def plane_copy(z, k, arriving):
        owner = lax.rem(me_t + tensor - z, tensor)
        block = w_ref.at[owner, :, rows_at(chip_place(k, arriving))]
        return remote(
            block, block, plane_sems.at[0, z, k], plane_sems.at[1, z, k], "expert", chip_after(k)
        )

    def pair_copy(z, arriving):
        owner = lax.rem(me_t + tensor - z, tensor)
        block = w_ref.at[owner, :, half_at(CORES - 1 - core if arriving else core)]
        return remote(
            block, block, pair_sems.at[0, z], pair_sems.at[1, z], "expert",
            me_e + CORES - 1 - 2 * core,
        )

    def slot_rows(e):
        return pl.ds(pl.multiple_of(e * slots, slots), slots)

    def flat_copy(src, dst, sems, d, arriving):
        return remote(
            src.at[slot_rows(after(d))], dst.at[slot_rows(place(d, arriving))],
            sems.at[0, d], sems.at[1, d], "expert", after(d),
        )

    def route_copy(d, arriving):
        return flat_copy(send_ref, routed_ref, route_sems, d, arriving)

    def early_copy(d, arriving):
        return flat_copy(early_send, early_ref, early_sems, d, arriving)

    def noise_copy(d, arriving):
        return swap_copy(noise_send, noise_all, noise_sems, d, arriving)

    def back_copy(d, arriving):
        return flat_copy(early_send, back_ref, back_sems, d, arriving)

    def out_copy(d, arriving):
        return flat_copy(send_ref, routed_ref, out_sems, d, arriving)

    def columns(t):
        return slice(t * wide, (t + 1) * wide)

    def w_pair_copy(t):
        return remote(
            wide_ref.at[half_at(CORES - 1 - core), columns(t)], pair_ref.at[t],
            w_pair_sems.at[0, t], w_pair_sems.at[1, t], "expert", me_e + CORES - 1 - 2 * core,
        )

    def w_copy(t, k, arriving):
        return remote(
            wide_ref.at[rows_at(chip_after(k)), columns(t)],
            pieces.at[chip_place(k, arriving) // CORES, t],
            w_sems.at[0, t, k], w_sems.at[1, t, k], "expert", chip_after(k),
        )

    def share_pair_sum(t):
        w_pair_copy(t).wait_recv()
        ours = half_at(core)
        pair_sum = wide_ref[ours, columns(t)].astype(F32) + pair_ref[t].astype(F32)
        wide_ref[ours, columns(t)] = pair_sum.astype(BF)
        each(chips, lambda k: w_copy(t, k, False).start())
        pieces[me_e // CORES, t] = wide_ref[mine, columns(t)]

    def plane_sum(t):
        each(chips, lambda k: w_copy(t, k, True).wait_recv())
        total = pieces[0, t].astype(F32)
        for e in range(1, chips):
            total = total + pieces[e, t].astype(F32)
        return total.astype(BF)

    def send_piece(t):
        piece_send[t] = plane_sum(t)
        piece_copy(t + 1, False).start()

    def piece_copy(d, arriving):
        return line_copy(piece_send.at[d - 1], lambda owner: piece_line.at[owner], piece_sems, d, arriving)

    def final_copy(d, arriving):
        block = w_sum_ref.at[rows_at(place(d, arriving))]
        return remote(block, block, final_sems.at[0, d], final_sems.at[1, d], "expert", after(d))

    def small_copy(d, arriving):
        return remote(
            small_ref, small_plane.at[place(d, arriving)], small_sems.at[0, d],
            small_sems.at[1, d], "expert", after(d),
        )

    def small_line_copy(d, arriving):
        return line_copy(
            small_line_send, lambda owner: small_line.at[owner], small_line_sems, d, arriving
        )

    greet((("expert", experts), ("tensor", tensor)))
    each(tensor, lambda d: first_copy(0, d, False).start())
    line_in = Line(tensor, w_in_own, w_in_all, in_sems.at[0], in_sems.at[1])
    line_back = Line(tensor, w_back_own, w_back_all, in_back_sems.at[0], in_back_sems.at[1])
    w_ref[me_t, 3] = w_out_own[...].T
    each(tensor, lambda d: first_copy(1, d, False).start())
    line_in.start(0)
    keep = [
        pltpu.make_async_copy(w_qkv_own, w_ref.at[me_t, 0:3], own_sem.at[0]),
        pltpu.make_async_copy(w_in_own, w_in_all.at[me_t], own_sem.at[1]),
        pltpu.make_async_copy(w_back_own, w_back_all.at[me_t], own_sem.at[2]),
    ]
    for copy in keep:
        copy.start()

    def spread(compact, to_ref, fill=0.0):
        columns = compact.shape[1]
        narrow[0:own_rows, 0:columns] = compact
        to_ref[...] = jnp.full(to_ref.shape, fill, F32)
        for i in range(images):
            to_ref[i * SP : i * SP + SEQ, 0:columns] = narrow[
                i * SEQ : (i + 1) * SEQ, 0:columns
            ]

    def compact(padded):
        for i in range(images):
            narrow[i * SEQ : (i + 1) * SEQ, :] = padded[i * SP : i * SP + SEQ, :]
        return narrow[0:own_rows, :]

    def spread_lanes(packed, fill):
        gap = jnp.full((packed.shape[0], SP - SEQ), fill, F32)
        blocks = []
        for i in range(images):
            blocks += [packed[:, i * SEQ : (i + 1) * SEQ], gap]
        return jnp.concatenate(blocks, axis=1)

    noise = spread_lanes(noise_ref[...], 0.0)
    high = noise.astype(BF).astype(F32)
    middle = (noise - high).astype(BF).astype(F32)
    low = noise - high - middle
    noise_parts = [high, middle, low]
    if noise_send.shape[1] > 3 * experts:
        noise_parts.append(jnp.zeros((noise_send.shape[1] - 3 * experts, noise.shape[1]), F32))
    noise = jnp.concatenate(noise_parts, axis=0).astype(BF)
    slots_by = slots_by_lane(spread_lanes(routes_ref[...].astype(F32), -1.0), experts)
    lanes_ref[...] = slots_by
    no_slots = jnp.zeros((LANES - experts, slots_by.shape[1]), F32)
    rows_ref[...] = jnp.concatenate([slots_by, no_slots], axis=0).T
    no_router = jnp.zeros((LANES - experts, D), F32)
    w_router_ref[...] = jnp.concatenate(
        [router_own[...].astype(F32), no_router], axis=0
    ).astype(BF)
    spread(cotangent_ref[...].astype(F32), cot_ref)
    cot_low = cot_ref[...].astype(BF)
    spot = ids((slots, lanes_ref.shape[1]), 0).astype(F32)

    def pick_of(e):
        return (spot == lanes_ref[pl.ds(e, 1), :]).astype(F32).astype(BF)

    def forward_piece(z):
        first_copy(0, z, True).wait_recv()
        first_copy(1, z, True).wait_recv()
        each(chips, lambda k: plane_copy(z, k, False).start())

    each(tensor, forward_piece)
    for d in range(1, experts + 1):
        e = after(d)
        pick = pick_of(e)
        rows_of_e = mm(pick, cot_low).astype(BF)
        noise_of_e = mm(noise, pick, NT).astype(BF)
        if d < experts:
            early_send[slot_rows(e), :] = rows_of_e
            noise_send[e] = noise_of_e
            early_copy(d, False).start()
            noise_copy(d, False).start()
        else:
            early_ref[slot_rows(e), :] = rows_of_e
            noise_all[e] = noise_of_e
    spread(tokens_ref[...].astype(F32), x_ref)
    x = x_ref[...]
    unit1, inverse1 = unit_norm(x)
    normed1 = (unit1 * gain1_ref[...]).astype(BF)
    line_in.arrive(0)
    if tensor > 2:
        line_in.start(1)

    def forward_half(z):
        each(chips, lambda k: plane_copy(z, k, True).wait_recv())
        pair_copy(z, False).start()

    each(tensor, forward_half)
    keep[0].wait()
    each(tensor, lambda z: pair_copy(z, True).wait_recv())

    def qkv_weights(t):
        return jnp.concatenate([w_ref[t, c] for c in range(3)], axis=1)

    lane = ids((SP, width), 1) // HD
    live = ids((SP, SP), 1) < SEQ
    for t in range(tensor):
        qkv_ref[t] = mm(normed1, qkv_weights(t)).astype(BF)
        for i in range(images):
            rows = slice(i * SP, (i + 1) * SP)
            q = qkv_ref[t, rows, 0:width]
            k = qkv_ref[t, rows, width : 2 * width]
            v = qkv_ref[t, rows, 2 * width : 3 * width]
            mixed = None
            for j in range(heads):
                q_j = q if heads == 1 else jnp.where(lane == j, q, jnp.zeros_like(q))
                scores = mm(q_j, k, NT) * HD ** (-0.5)
                scores = jnp.where(live, scores, -1e30)
                power = jnp.exp(scores - jnp.max(scores, -1, keepdims=True))
                attend = (power / jnp.sum(power, -1, keepdims=True)).astype(BF)
                attend_ref[i, t * heads + j] = attend
                part = mm(attend, v)
                mixed = part if mixed is None else jnp.where(lane == j, part, mixed)
            mixed_ref[t, rows, :] = mixed.astype(BF)
    residual = x
    for t in range(tensor):
        residual = residual + mm(mixed_ref[t], w_ref[t, 3], NT)
    residual_ref[...] = residual
    unit2, inverse2 = unit_norm(residual)
    normed2 = (unit2 * gain2_ref[...]).astype(BF)
    for d in range(1, experts + 1):
        e = after(d)
        rows_of_e = mm(pick_of(e), normed2).astype(BF)
        if d < experts:
            send_ref[slot_rows(e), :] = rows_of_e
            route_copy(d, False).start()
        else:
            routed_ref[slot_rows(e), :] = rows_of_e
    for step in range(1, tensor - 1):
        line_in.arrive(step)
        if step + 1 < tensor - 1:
            line_in.start(step + 1)
        if step == max(1, tensor - 3):
            line_back.start(0)
    if tensor == 2:
        line_back.start(0)
    keep[1].wait()

    fold_from, fold_to = ids((noise_all.shape[1], LANES), 0), ids((noise_all.shape[1], LANES), 1)
    fold = (
        (fold_from < 3 * experts) & (lax.rem(fold_from, experts) == fold_to)
    ).astype(F32).astype(BF)
    expert_lane = ids((chunk, LANES), 1)
    groups = experts // group

    def block_rows(at):
        return pl.ds(pl.multiple_of(at * chunk, chunk), chunk)

    def hidden_units(turn, _):
        at = lax.rem(me_e // group + groups - turn, groups)
        for k in range(group):
            d = lax.rem(me_e + experts - (at * group + k), experts)

            @pl.when(d > 0)
            def _(d=d):
                route_copy(d, True).wait_recv()
                early_copy(d, True).wait_recv()
                noise_copy(d, True).wait_recv()

        @pl.when(turn == groups // 2)
        def _():
            for step in range(0, tensor - 3):
                line_back.arrive(step)
                line_back.start(step + 1)

        rows = block_rows(at)
        came = routed_ref[rows, :]
        added = [mm(noise_all[at * group + k], fold, TN) for k in range(group)]
        added = added[0] if group == 1 else jnp.concatenate(added, axis=0)
        logits = jnp.where(expert_lane < experts, mm(came, w_router_ref[...], NT) + added, -1e30)
        power = jnp.exp(logits - jnp.max(logits, -1, keepdims=True))
        router = power / jnp.sum(power, -1, keepdims=True)
        router_ref[rows, :] = router
        gate = jnp.sum(jnp.where(expert_lane == me_e, router, 0.0), -1, keepdims=True)
        early_ref[rows, :] = (gate * early_ref[rows, :].astype(F32)).astype(BF)
        half_rows, block = chunk // 2, min(256, w_in_all.shape[2])

        def spot_of(r):
            return pl.ds(pl.multiple_of(at * chunk + r * half_rows, TILE), half_rows)

        cuts = [
            (f, n, r)
            for f in range(parts)
            for n in range(0, w_in_all.shape[2], block)
            for r in range(2)
        ]

        def pre_of(f, n, r):
            return mm(routed_ref[spot_of(r), :], w_in_all[f, :, n : n + block])

        ahead = pre_of(*cuts[0])
        for number, (f, n, r) in enumerate(cuts):
            pre = ahead
            if number + 1 < len(cuts):
                ahead = pre_of(*cuts[number + 1])
            normal, density = gelu_parts(pre)
            hidden_ref[f, spot_of(r), n : n + block] = (pre * normal).astype(BF)
            slope_ref[f, spot_of(r), n : n + block] = (normal + pre * density).astype(BF)
        return 0

    lax.fori_loop(0, groups, hidden_units, 0)

    def grads_at(block, part):
        return back_grads.at[block] if part else slope_ref.at[block, 0:D]

    sums = Sums(tensor, grads_at, held, sum_send, sum_recv)
    order = []
    for step in range(tensor):
        for f in (tensor - 1 - step, step):
            if f not in order:
                order.append(f)

    def turn_rows(ref):
        def body(at, _):
            rows = pl.ds(pl.multiple_of(at * LANES, LANES), LANES)
            wide_ref[:, rows] = ref[rows, :].T
            return 0

        lax.fori_loop(0, pairs // LANES, body, 0)

    def weight_grads(part, right):
        for f in order:
            block = mm(wide_ref[:, 0:pairs], right[f, 0:pairs, :]).astype(BF)
            grads_at(f, part)[...] = block
            for step in range(tensor - 1 if part else 1):
                for way, to in ((0, tensor - 1 - step), (1, step)):
                    if to == f:
                        sums.start_first(way, step, part)

    turn_rows(early_ref)
    weight_grads(1, hidden_ref)
    turn_rows(routed_ref)

    for step in range(max(tensor - 3, 0), tensor - 2):
        line_back.arrive(step)
        line_back.start(step + 1)
    keep[2].wait()

    def early_sent(d):
        early_copy(d, False).wait_send()
        route_copy(d, False).wait_send()

    each(experts, early_sent)

    small_ref[...] = jnp.zeros_like(small_ref)

    def near(k):
        def from_low(me):
            below = (me - k + tensor) // tensor
            return below * (me - k) + (1 - below) * k

        low = 1 - (2 * me_t) // tensor
        mirrored = tensor - 1 - from_low(tensor - 1 - me_t)
        return low * from_low(me_t) + (1 - low) * mirrored

    def unit_part(k, rows):
        f = near(k)
        w_b = w_back_all[f]
        out = mm(hidden_ref[f, rows, :], w_b)
        d_pre = (mm(early_ref[rows, :], w_b, NT) * slope_ref[f, rows, :].astype(F32)).astype(BF)
        slope_ref[f, rows, :] = d_pre
        return out, mm(d_pre, w_in_all[f], NT)

    def near_rows(at, _):
        rows = block_rows(at)
        out, back = unit_part(0, rows)
        for k in range(1, tensor - 1):
            more_out, more_back = unit_part(k, rows)
            out, back = out + more_out, back + more_back
        send_ref[rows, :] = out.astype(BF)
        early_send[rows, :] = back.astype(BF)
        return 0

    lax.fori_loop(0, groups, near_rows, 0)
    line_steps = [(step, part) for part in (1, 0) for step in range(1, tensor - 1)]

    def next_sum():
        if line_steps:
            sums.forward(*line_steps.pop(0))

    next_sum()
    line_back.arrive(tensor - 2)

    def far_rows(turn, _):
        at = lax.rem(me_e // group + 1 + turn, groups)
        rows = block_rows(at)
        router = router_ref[rows, :]
        own_lane = expert_lane == me_e
        gate = jnp.sum(jnp.where(own_lane, router, 0.0), -1, keepdims=True)
        out, back = unit_part(tensor - 1, rows)
        out = (out + send_ref[rows, :].astype(F32)).astype(BF).astype(F32)
        back = back + early_send[rows, :].astype(F32)
        d_gate = jnp.sum(early_ref[rows, :].astype(F32) * out, -1, keepdims=True)
        d_logits = (d_gate * (own_lane.astype(F32) - router)).astype(BF)
        early_send[rows, :] = (back + mm(d_logits, w_router_ref[...])).astype(BF)
        send_ref[rows, :] = (gate * out).astype(BF)
        small_ref[0:experts, :] += mm(d_logits, routed_ref[rows, :], TN)[0:experts]
        for k in range(group):
            e = at * group + k
            d = lax.rem(e + experts - me_e, experts)

            @pl.when(d > 0)
            def _(d=d):
                back_copy(d, False).start()

            @pl.when(d == 0)
            def _(e=e):
                back_ref[slot_rows(e), :] = early_send[slot_rows(e), :]
                routed_ref[slot_rows(e), :] = send_ref[slot_rows(e), :]

        return 0

    lax.fori_loop(0, groups, far_rows, 0)

    weight_grads(0, slope_ref)
    next_sum()

    each(experts, lambda d: back_copy(d, True).wait_recv())
    slots_of = rows_ref[:, 0:experts]
    d_normed2 = take_rows(slots_of, back_ref, experts)
    unit2, inverse2 = unit_norm(residual_ref[...])
    d_rows, norm2 = norm_back(d_normed2, unit2, inverse2, gain2_ref[...])
    small_ref[experts + 1 : experts + 2, :] = norm2
    d_residual = cot_ref[...] + d_rows
    cot_ref[...] = d_residual
    d_attention = d_residual.astype(BF)
    scaling = HD ** (-0.5)
    unit1, inverse1 = unit_norm(x_ref[...])
    normed1 = (unit1 * gain1_ref[...]).astype(BF)
    for turn in range(tensor):
        t = lax.rem(me_t + 1 + turn, tensor)
        first = turn * wide
        wide_ref[:, first + 3 * width : first + wide] = mm(d_attention, mixed_ref[t], TN).astype(BF)
        d_mixed = mm(d_attention, w_ref[t, 3]).astype(BF)
        for i in range(images):
            rows = slice(i * SP, (i + 1) * SP)
            q = qkv_ref[t, rows, 0:width]
            k = qkv_ref[t, rows, width : 2 * width]
            v = qkv_ref[t, rows, 2 * width : 3 * width]
            do = d_mixed[rows]
            dq = dk = dv = None
            for j in range(heads):
                own = lane == j
                do_j = do if heads == 1 else jnp.where(own, do, jnp.zeros_like(do))
                q_j = q if heads == 1 else jnp.where(own, q, jnp.zeros_like(q))
                attend_low = attend_ref[i, t * heads + j]
                attend = attend_low.astype(F32)
                part_v = mm(attend_low, do_j, TN)
                d_attend = mm(do_j, v, NT)
                inner = jnp.sum(attend * d_attend, -1, keepdims=True)
                ds = (attend * (d_attend - inner)).astype(BF)
                part_q = mm(ds, k) * scaling
                part_k = mm(ds, q_j, TN) * scaling
                dq = part_q if dq is None else jnp.where(own, part_q, dq)
                dk = part_k if dk is None else dk + part_k
                dv = part_v if dv is None else dv + part_v
            qkv_ref[t, rows, 0:width] = dq.astype(BF)
            qkv_ref[t, rows, width : 2 * width] = dk.astype(BF)
            qkv_ref[t, rows, 2 * width : 3 * width] = dv.astype(BF)
        wide_ref[:, first : first + 3 * width] = mm(normed1, qkv_ref[t], TN).astype(BF)
        w_pair_copy(turn).start()
        if turn > 0:
            share_pair_sum(turn - 1)
        if turn > 2:
            send_piece(turn - 3)
    share_pair_sum(tensor - 1)
    next_sum()
    sent = max(tensor - 3, 0)
    for turn in range(sent, tensor - 2):
        send_piece(turn)
    for step in range(1, tensor - 2):
        for way in (0, 1):
            sums.start_first(way, step, 0)
    d_normed1 = None
    for t in range(tensor):
        part = mm(qkv_ref[t], qkv_weights(t), NT)
        d_normed1 = part if d_normed1 is None else d_normed1 + part
    d_rows, norm1 = norm_back(d_normed1, unit1, inverse1, gain1_ref[...])
    small_ref[experts : experts + 1, :] = norm1
    send_piece(tensor - 2)
    each(experts, lambda d: small_copy(d, False).start())
    each(experts, lambda d: out_copy(d, False).start())
    for way in (0, 1):
        sums.start_first(way, tensor - 2, 0)
    small_plane[me_e] = small_ref[...]
    tokens_grad_ref[...] = compact(cot_ref[...] + d_rows)

    piece_line[me_t] = plane_sum(tensor - 1)
    each(tensor, lambda d: piece_copy(d, True).wait_recv())
    total = piece_line[0].astype(F32)
    for t in range(1, tensor):
        total = total + piece_line[t].astype(F32)
    w_sum_ref[mine, :] = total.astype(BF)
    each(experts, lambda d: final_copy(d, False).start())
    each(experts, lambda d: small_copy(d, True).wait_recv())
    total = small_plane[0]
    for e in range(1, experts):
        total = total + small_plane[e]
    small_line_send[...] = total
    each(tensor, lambda d: small_line_copy(d, False).start())
    small_line[me_t] = total
    while line_steps:
        next_sum()

    each(experts, lambda d: out_copy(d, True).wait_recv())
    output = residual_ref[...] + take_rows(slots_of, routed_ref, experts)
    output_ref[...] = compact(output).astype(BF)

    each(tensor, lambda d: small_line_copy(d, True).wait_recv())
    total = small_line[0]
    for t in range(1, tensor):
        total = total + small_line[t]
    small_sum_ref[...] = total
    each(experts, lambda d: final_copy(d, True).wait_recv())

    for part in (1, 0):
        sums.last(part)
        total = grads_at(me_t, part)[...].astype(F32)
        for way in (0, 1):
            came = held[way, tensor - 2, part].astype(F32)
            total = total + jnp.where(sums.hops(way) >= 1, came, jnp.zeros_like(came))
        if part == 0:
            in_grad_ref[...] = total.astype(BF)
        else:
            back_grad_ref[...] = total.T.astype(BF)

    sums.finish()
    line_in.finish()
    line_back.finish()

    def sent(d):
        noise_copy(d, False).wait_send()
        back_copy(d, False).wait_send()
        out_copy(d, False).wait_send()
        final_copy(d, False).wait_send()
        small_copy(d, False).wait_send()

    each(experts, sent)

    def sent_line(d):
        first_copy(0, d, False).wait_send()
        first_copy(1, d, False).wait_send()
        piece_copy(d, False).wait_send()
        small_line_copy(d, False).wait_send()
        pair_copy(d, False).wait_send()
        each(chips, lambda k: plane_copy(d, k, False).wait_send())

    each(tensor, sent_line)
    for t in range(tensor):
        w_pair_copy(t).wait_send()
        each(chips, lambda k, t=t: w_copy(t, k, False).wait_send())


def finish_kernel(
    experts, output_in, tokens_in, w_sum_ref, small_ref, in_ref, back_ref,
    output_ref, tokens_ref, norm1_ref, qkv_ref, out_ref, norm2_ref, router_ref,
    in_grad_ref, back_grad_ref,
):
    output_ref[...] = output_in[...]
    tokens_ref[...] = tokens_in[...]
    width = out_ref.shape[0]
    for c in range(3):
        qkv_ref[c] = w_sum_ref[:, c * width : (c + 1) * width].astype(F32)
    out_ref[...] = w_sum_ref[:, 3 * width : 4 * width].T.astype(F32)
    router_ref[...] = small_ref[0:experts, :]
    norm1_ref[...] = small_ref[experts : experts + 1, :]
    norm2_ref[...] = small_ref[experts + 1 : experts + 2, :]
    in_grad_ref[...] = in_ref[...].astype(F32)
    back_grad_ref[...] = back_ref[...].astype(F32)


def per_device(
    tokens, norm1_gain, w_qkv, w_out, norm2_gain, w_router, noise, routes, w_in, w_back, cotangent
):
    own_rows = tokens.shape[0]
    experts = noise.shape[1]
    tensor = lax.axis_size("tensor")
    images = own_rows // SEQ
    rows = images * SP
    capacity = (2 * own_rows * TOP + experts - 1) // experts
    slots = up(capacity, TILE)
    group = max(g for g in range(1, experts + 1) if experts % g == 0 and g * slots <= 2 * SP)
    width = w_out.shape[0]
    hidden = w_in.shape[2]
    heads = tensor * width // HD
    piece = D // experts
    small_rows = up(experts + 2, 8)
    noise_rows = up(3 * experts, TILE)
    pairs = experts * slots
    dma = pltpu.SemaphoreType.DMA
    bf, f32 = (lambda *dims: pltpu.VMEM(dims, BF)), (lambda *dims: pltpu.VMEM(dims, F32))

    output, grad_tokens, w_sum, small, grad_in, grad_back = call(
        functools.partial(block_kernel, experts, tensor, images, group),
        (
            shape((own_rows, D)),
            shape((own_rows, D), F32),
            shape((D, 4 * width)),
            shape((small_rows, D), F32),
            shape((D, hidden)),
            shape((hidden, D)),
        ),
        scratch=(
            bf(tensor, 4, D, width),
            bf(LANES, D),
            bf(tensor, D, hidden),
            bf(tensor, hidden, D),
            f32(up(own_rows, TILE), D),
            f32(rows, D),
            f32(rows, D),
            f32(rows, LANES),
            f32(experts, rows),
            bf(tensor, rows, 3 * width),
            bf(images, heads, SP, SP),
            bf(tensor, rows, width),
            f32(rows, D),
            bf(pairs, D),
            bf(pairs, D),
            bf(pairs, D),
            bf(pairs, D),
            bf(experts, noise_rows, slots),
            bf(experts, noise_rows, slots),
            f32(pairs, LANES),
            bf(tensor, pairs, hidden),
            bf(tensor, max(pairs, D), hidden),
            bf(pairs, D),
            bf(2, tensor - 1, 2, D, hidden),
            bf(D, max(pairs, tensor * 4 * width)),
            bf(tensor, D, hidden),
            bf(tensor, D // CORES, 4 * width),
            bf(experts // CORES, tensor, piece, 4 * width),
            bf(tensor, piece, 4 * width),
            bf(tensor, piece, 4 * width),
            f32(small_rows, D),
            f32(experts, small_rows, D),
            f32(small_rows, D),
            f32(tensor, small_rows, D),
            dma((3,)),
            dma((2, 2, tensor)),
            dma((2, tensor, experts // CORES)),
            dma((2, tensor)),
            dma((2, 2, tensor - 1)),
            dma((2, 2, tensor - 1)),
            dma((2, experts)),
            dma((2, experts)),
            dma((2, experts)),
            dma((2, experts)),
            dma((2, experts)),
            dma((2, tensor - 1, 2)),
            dma((2, tensor - 1, 2)),
            dma((2, tensor)),
            dma((2, tensor, experts // CORES)),
            dma((2, tensor)),
            dma((2, experts)),
            dma((2, experts)),
            dma((2, tensor)),
        ),
        far_in=(8, 9, 10),
        collective_id=0,
        has_side_effects=True,
    )(
        routes.T, tokens, cotangent, noise.T, norm1_gain.reshape(1, D), norm2_gain.reshape(1, D),
        w_router.T, w_out, w_qkv.transpose(1, 0, 2), w_in[0], w_back[0],
    )
    output, grad_tokens, norm1, grad_qkv, grad_out, norm2, router, grad_in, grad_back = call(
        functools.partial(finish_kernel, experts),
        (
            shape((own_rows, D)),
            shape((own_rows, D), F32),
            shape((1, D), F32),
            shape((3, D, width), F32),
            shape((width, D), F32),
            shape((1, D), F32),
            shape((experts, D), F32),
            shape((D, hidden), F32),
            shape((hidden, D), F32),
        ),
    )(output, grad_tokens, w_sum, small, grad_in, grad_back)
    return (
        output,
        grad_tokens,
        norm1.reshape(D),
        grad_qkv.transpose(1, 0, 2),
        grad_out,
        norm2.reshape(D),
        router.T,
        grad_in[None],
        grad_back[None],
    )


def solution(mesh):
    rows = P(("expert", "tensor"), None)
    placed = (
        rows,
        P(),
        P(None, None, "tensor"),
        P("tensor", None),
        P(),
        P(),
        rows,
        rows,
        P("expert", None, "tensor"),
        P("expert", "tensor", None),
        rows,
    )
    return jax.shard_map(
        per_device,
        mesh=mesh,
        in_specs=placed,
        out_specs=(
            rows,
            rows,
            P(),
            P(None, None, "tensor"),
            P("tensor", None),
            P(),
            P(),
            P("expert", None, "tensor"),
            P("expert", "tensor", None),
        ),
        check_vma=False,
    )
```

```python
import functools

import jax
import jax.numpy as jnp
from jax import lax
from jax.experimental import pallas as pl
from jax.experimental.pallas import tpu as pltpu
from jax.sharding import PartitionSpec as P

D = 512
HD = 64
CORES = 2
TOP = 2
SEQ = 197
LANES = 128
TILE = 16
EPSILON = 1e-06
DENSITY = 0.3989422804014327
TAIL = 0.5 / DENSITY
BF = jnp.bfloat16
F32 = jnp.float32
VMEM_BYTES = 62 * 1024 * 1024

NN = (((1,), (0,)), ((), ()))
NT = (((1,), (1,)), ((), ()))
TN = (((0,), (0,)), ((), ()))


def up(value, unit):
    return (value + unit - 1) // unit * unit


SP = up(SEQ, TILE)


def mm(a, b, dims=NN):
    return lax.dot_general(a, b, dims, preferred_element_type=F32)


def call(
    body, out_shape, scratch=(), flops=0, moved=0, prefetch=(), far_in=(), far_out=(), **more
):
    params = pltpu.CompilerParams(vmem_limit_bytes=VMEM_BYTES, **more)
    cost = pl.CostEstimate(flops=flops, bytes_accessed=moved, transcendentals=0)

    def spec(place, far, scalar=()):
        if place in scalar:
            return pl.BlockSpec(memory_space=pltpu.SMEM)
        return pl.BlockSpec(memory_space=pl.ANY if place in far else pltpu.VMEM)

    def run(*args):
        return pl.pallas_call(
            body,
            out_shape=out_shape,
            in_specs=[spec(place, far_in, prefetch) for place in range(len(args))],
            out_specs=tuple(spec(place, far_out) for place in range(len(out_shape))),
            scratch_shapes=list(scratch),
            compiler_params=params,
            cost_estimate=cost,
        )(*args)

    return run


def shape(dims, dtype=BF):
    return jax.ShapeDtypeStruct(dims, dtype)


def unit_norm(values):
    center = values - jnp.mean(values, -1, keepdims=True)
    spread = jnp.mean(center * center, -1, keepdims=True)
    inverse = lax.rsqrt(spread + EPSILON)
    return center * inverse, inverse


def norm_back(grad_rows, normed, inverse, gain):
    scaled = grad_rows * gain
    inner = (
        scaled
        - jnp.mean(scaled, -1, keepdims=True)
        - normed * jnp.mean(scaled * normed, -1, keepdims=True)
    )
    return inverse * inner, jnp.sum(grad_rows * normed, axis=0, keepdims=True)


def ids(shape_of, dim):
    return lax.broadcasted_iota(jnp.int32, shape_of, dim)


def slots_by_lane(routes, experts):
    rows = routes.shape[1]
    which = ids((experts, rows), 0).astype(F32)
    named = (routes[0:1] == which) | (routes[1:2] == which)
    before = (ids((rows, rows), 0) < ids((rows, rows), 1)).astype(F32).astype(BF)
    rank = mm(named.astype(F32).astype(BF), before)
    return jnp.where(named, rank, -1.0)


def take_rows(slots, in_ref, experts):
    count = in_ref.shape[0] // experts
    rows = slots.shape[0]
    place = ids((rows, count), 1).astype(F32)
    total = None
    for e in range(experts):
        pick = (place == slots[:, e : e + 1]).astype(F32).astype(BF)
        part = mm(pick, in_ref[e * count : (e + 1) * count, :])
        total = part if total is None else total + part
    return total


MESH = pl.DeviceIdType.MESH


def greet(axes):
    barrier = pltpu.get_barrier_semaphore()
    for name, size in axes:
        me = lax.axis_index(name)

        def hello(d, _, name=name, size=size, me=me):
            pl.semaphore_signal(
                barrier, inc=1, device_id={name: lax.rem(me + d, size)}, device_id_type=MESH
            )
            return 0

        lax.fori_loop(1, size, hello, 0)
    pl.semaphore_wait(barrier, sum(size - 1 for _, size in axes))


def remote(src, dst, send_sem, recv_sem, name, to):
    return pltpu.make_async_remote_copy(
        src_ref=src,
        dst_ref=dst,
        send_sem=send_sem,
        recv_sem=recv_sem,
        device_id={name: to},
        device_id_type=MESH,
    )


def each(size, step, first=1):
    def body(d, _):
        step(d)
        return 0

    lax.fori_loop(first, size, body, 0)


class Line:
    def __init__(self, size, own, everyone, send_sem, recv_sem):
        self.size, self.own, self.all = size, own, everyone
        self.send_sem, self.recv_sem = send_sem, recv_sem
        self.me = lax.axis_index("tensor")

    def copy(self, way, step, arriving):
        toward = 1 if way == 0 else -1
        owner = self.me - toward * (step + (1 if arriving else 0))
        src = self.own if step == 0 else self.all.at[owner]
        return remote(
            src, self.all.at[owner], self.send_sem.at[way, step], self.recv_sem.at[way, step],
            "tensor", self.me + toward,
        )

    def sends(self, way, step):
        last = self.size - 1
        if way == 0:
            return (self.me >= step) & (self.me < last)
        return (self.me <= last - step) & (self.me > 0)

    def receives(self, way, step):
        if way == 0:
            return self.me >= step + 1
        return self.me <= self.size - 2 - step

    def start(self, step):
        for way in (0, 1):
            pl.when(self.sends(way, step))(lambda way=way: self.copy(way, step, False).start())

    def arrive(self, step):
        for way in (0, 1):
            pl.when(self.receives(way, step))(
                lambda way=way: self.copy(way, step, True).wait_recv()
            )

    def finish(self):
        for step in range(self.size - 1):
            for way in (0, 1):
                pl.when(self.sends(way, step))(
                    lambda way=way, step=step: self.copy(way, step, False).wait_send()
                )


def gelu_parts(pre):
    density = jnp.exp2(pre * pre * (-0.5 * 1.4426950408889634)) * DENSITY
    t = pl.reciprocal(1.0 + jnp.abs(pre * (0.3275911 * 0.5**0.5)), approx=True)
    series = t * (
        0.254829592 * TAIL
        + t
        * (
            -0.284496736 * TAIL
            + t * (1.421413741 * TAIL + t * (-1.453152027 * TAIL + t * (1.061405429 * TAIL)))
        )
    )
    tail = series * density
    return jnp.where(pre < 0, tail, 1.0 - tail), density


class Sums:
    def __init__(self, size, own, held, send_sem, recv_sem):
        self.size, self.own, self.held = size, own, held
        self.send_sem, self.recv_sem = send_sem, recv_sem
        self.me = lax.axis_index("tensor")

    def hops(self, way):
        return self.me if way == 0 else self.size - 1 - self.me

    def block(self, way, step):
        ahead = self.size - 1 + self.hops(way) - step
        return ahead if way == 0 else self.size - 1 - ahead

    def copy(self, way, step, part, first):
        toward = 1 if way == 0 else -1
        if first:
            src = self.own(self.block(way, step), part)
        else:
            src = self.held.at[way, max(step - 1, 0), part]
        return remote(
            src, self.held.at[way, step, part],
            self.send_sem.at[way, step, part], self.recv_sem.at[way, step, part],
            "tensor", self.me + toward,
        )

    def start_first(self, way, step, part):
        pl.when(self.hops(way) == 0)(lambda: self.copy(way, step, part, True).start())

    def middle(self, way, step):
        hops = self.hops(way)
        return (hops >= 1) & (hops <= step) & (hops < self.size - 1)

    def forward(self, step, part):
        for way in (0, 1):

            def go(way=way):
                self.copy(way, step - 1, part, False).wait_recv()
                held = self.held.at[way, step - 1, part]
                mine = self.own(self.block(way, step), part)
                add_into(held, mine)
                self.copy(way, step, part, False).start()

            pl.when(self.middle(way, step))(go)

    def last(self, part):
        for way in (0, 1):
            pl.when(self.hops(way) >= 1)(
                lambda way=way: self.copy(way, self.size - 2, part, False).wait_recv()
            )

    def finish(self):
        for part in (0, 1):
            for step in range(self.size - 1):
                for way in (0, 1):
                    sends = (self.hops(way) == 0) | self.middle(way, step)
                    pl.when(sends)(
                        lambda way=way, step=step, part=part: self.copy(
                            way, step, part, False
                        ).wait_send()
                    )


def add_into(held, mine):
    rows = held.shape[0]
    block = min(rows, 128)

    def body(r, _):
        at = pl.ds(pl.multiple_of(r * block, block), block)
        held[at, :] = (held[at, :].astype(F32) + mine[at, :].astype(F32)).astype(BF)
        return 0

    lax.fori_loop(0, rows // block, body, 0)


def block_kernel(
    experts, tensor, images, group,
    routes_ref, tokens_ref, cotangent_ref, noise_ref, gain1_ref, gain2_ref, router_own,
    w_out_own, w_qkv_own, w_in_own, w_back_own,
    output_ref, tokens_grad_ref, w_sum_ref, small_sum_ref, in_grad_ref, back_grad_ref,
    w_ref, w_router_ref, w_in_all, w_back_all, narrow, x_ref, cot_ref, rows_ref, lanes_ref,
    qkv_ref, attend_ref, mixed_ref, residual_ref,
    send_ref, routed_ref, early_send, early_ref, noise_send, noise_all, router_ref,
    hidden_ref, slope_ref, back_ref, held,
    wide_ref, back_grads, pair_ref, pieces, piece_send, piece_line,
    small_ref, small_plane, small_line_send, small_line,
    own_sem, first_sems, plane_sems, pair_sems, in_sems, in_back_sems, route_sems, early_sems, noise_sems,
    back_sems, out_sems, sum_send, sum_recv, w_pair_sems, w_sems, piece_sems, final_sems,
    small_sems, small_line_sems,
):
    own_rows = tokens_ref.shape[0]
    width = w_out_own.shape[0]
    wide = 4 * width
    heads = width // HD
    slots = noise_send.shape[2]
    pairs = experts * slots
    parts = w_in_all.shape[0]
    chunk = group * slots
    me_e, me_t = lax.axis_index("expert"), lax.axis_index("tensor")
    piece = D // experts

    chips = experts // CORES
    core = lax.rem(me_e, CORES)
    half = chips * piece

    def rows_at(e):
        at = lax.rem(e, CORES) * chips + e // CORES
        return pl.ds(pl.multiple_of(at * piece, piece), piece)

    def half_at(which):
        return pl.ds(pl.multiple_of(which * half, half), half)

    def chip_after(k):
        return lax.rem(me_e + CORES * k, experts)

    def chip_place(k, arriving):
        return lax.rem(me_e + experts - CORES * k, experts) if arriving else me_e

    mine = rows_at(me_e)

    def after(d):
        return lax.rem(me_e + d, experts)

    def place(d, arriving):
        return lax.rem(me_e + experts - d, experts) if arriving else me_e

    def swap_copy(src, dst, sems, d, arriving):
        to = after(d)
        return remote(
            src.at[to], dst.at[place(d, arriving)], sems.at[0, d], sems.at[1, d], "expert", to
        )

    def line_copy(src, dst, sems, d, arriving):
        owner = lax.rem(me_t + tensor - d, tensor) if arriving else me_t
        return remote(
            src, dst(owner), sems.at[0, d], sems.at[1, d],
            "tensor", lax.rem(me_t + d, tensor),
        )

    def first_copy(which, d, arriving):
        parts_of = (slice(0, 3), slice(3, 4))[which]
        src = w_ref.at[me_t, parts_of, mine] if which else w_qkv_own.at[:, mine]
        return line_copy(
            src, lambda owner: w_ref.at[owner, parts_of, mine], first_sems.at[which], d, arriving
        )

    def plane_copy(z, k, arriving):
        owner = lax.rem(me_t + tensor - z, tensor)
        block = w_ref.at[owner, :, rows_at(chip_place(k, arriving))]
        return remote(
            block, block, plane_sems.at[0, z, k], plane_sems.at[1, z, k], "expert", chip_after(k)
        )

    def pair_copy(z, arriving):
        owner = lax.rem(me_t + tensor - z, tensor)
        block = w_ref.at[owner, :, half_at(CORES - 1 - core if arriving else core)]
        return remote(
            block, block, pair_sems.at[0, z], pair_sems.at[1, z], "expert",
            me_e + CORES - 1 - 2 * core,
        )

    def slot_rows(e):
        return pl.ds(pl.multiple_of(e * slots, slots), slots)

    def flat_copy(src, dst, sems, d, arriving):
        return remote(
            src.at[slot_rows(after(d))], dst.at[slot_rows(place(d, arriving))],
            sems.at[0, d], sems.at[1, d], "expert", after(d),
        )

    def route_copy(d, arriving):
        return flat_copy(send_ref, routed_ref, route_sems, d, arriving)

    def early_copy(d, arriving):
        return flat_copy(early_send, early_ref, early_sems, d, arriving)

    def noise_copy(d, arriving):
        return swap_copy(noise_send, noise_all, noise_sems, d, arriving)

    def back_copy(d, arriving):
        return flat_copy(early_send, back_ref, back_sems, d, arriving)

    def out_copy(d, arriving):
        return flat_copy(send_ref, routed_ref, out_sems, d, arriving)

    def columns(t):
        return slice(t * wide, (t + 1) * wide)

    def w_pair_copy(t):
        return remote(
            wide_ref.at[half_at(CORES - 1 - core), columns(t)], pair_ref.at[t],
            w_pair_sems.at[0, t], w_pair_sems.at[1, t], "expert", me_e + CORES - 1 - 2 * core,
        )

    def w_copy(t, k, arriving):
        return remote(
            wide_ref.at[rows_at(chip_after(k)), columns(t)],
            pieces.at[chip_place(k, arriving) // CORES, t],
            w_sems.at[0, t, k], w_sems.at[1, t, k], "expert", chip_after(k),
        )

    def share_pair_sum(t):
        w_pair_copy(t).wait_recv()
        ours = half_at(core)
        pair_sum = wide_ref[ours, columns(t)].astype(F32) + pair_ref[t].astype(F32)
        wide_ref[ours, columns(t)] = pair_sum.astype(BF)
        each(chips, lambda k: w_copy(t, k, False).start())
        pieces[me_e // CORES, t] = wide_ref[mine, columns(t)]

    def plane_sum(t):
        each(chips, lambda k: w_copy(t, k, True).wait_recv())
        total = pieces[0, t].astype(F32)
        for e in range(1, chips):
            total = total + pieces[e, t].astype(F32)
        return total.astype(BF)

    def send_piece(t):
        piece_send[t] = plane_sum(t)
        piece_copy(t + 1, False).start()

    def piece_copy(d, arriving):
        return line_copy(piece_send.at[d - 1], lambda owner: piece_line.at[owner], piece_sems, d, arriving)

    def final_copy(k, arriving):
        block = w_sum_ref.at[rows_at(chip_place(k, arriving))]
        return remote(
            block, block, final_sems.at[0, k], final_sems.at[1, k], "expert", chip_after(k)
        )

    def final_pair_copy(arriving):
        block = w_sum_ref.at[half_at(CORES - 1 - core if arriving else core)]
        return remote(
            block, block, final_sems.at[0, 0], final_sems.at[1, 0], "expert",
            me_e + CORES - 1 - 2 * core,
        )

    def small_copy(d, arriving):
        return remote(
            small_ref, small_plane.at[place(d, arriving)], small_sems.at[0, d],
            small_sems.at[1, d], "expert", after(d),
        )

    def small_line_copy(d, arriving):
        return line_copy(
            small_line_send, lambda owner: small_line.at[owner], small_line_sems, d, arriving
        )

    greet((("expert", experts), ("tensor", tensor)))
    each(tensor, lambda d: first_copy(0, d, False).start())
    line_in = Line(tensor, w_in_own, w_in_all, in_sems.at[0], in_sems.at[1])
    line_back = Line(tensor, w_back_own, w_back_all, in_back_sems.at[0], in_back_sems.at[1])
    w_ref[me_t, 3] = w_out_own[...].T
    each(tensor, lambda d: first_copy(1, d, False).start())
    line_in.start(0)
    keep = [
        pltpu.make_async_copy(w_qkv_own, w_ref.at[me_t, 0:3], own_sem.at[0]),
        pltpu.make_async_copy(w_in_own, w_in_all.at[me_t], own_sem.at[1]),
        pltpu.make_async_copy(w_back_own, w_back_all.at[me_t], own_sem.at[2]),
    ]
    for copy in keep:
        copy.start()

    def spread(compact, to_ref, fill=0.0):
        columns = compact.shape[1]
        narrow[0:own_rows, 0:columns] = compact
        to_ref[...] = jnp.full(to_ref.shape, fill, F32)
        for i in range(images):
            to_ref[i * SP : i * SP + SEQ, 0:columns] = narrow[
                i * SEQ : (i + 1) * SEQ, 0:columns
            ]

    def compact(padded):
        for i in range(images):
            narrow[i * SEQ : (i + 1) * SEQ, :] = padded[i * SP : i * SP + SEQ, :]
        return narrow[0:own_rows, :]

    def spread_lanes(packed, fill):
        gap = jnp.full((packed.shape[0], SP - SEQ), fill, F32)
        blocks = []
        for i in range(images):
            blocks += [packed[:, i * SEQ : (i + 1) * SEQ], gap]
        return jnp.concatenate(blocks, axis=1)

    noise = spread_lanes(noise_ref[...], 0.0)
    high = noise.astype(BF).astype(F32)
    middle = (noise - high).astype(BF).astype(F32)
    low = noise - high - middle
    noise_parts = [high, middle, low]
    if noise_send.shape[1] > 3 * experts:
        noise_parts.append(jnp.zeros((noise_send.shape[1] - 3 * experts, noise.shape[1]), F32))
    noise = jnp.concatenate(noise_parts, axis=0).astype(BF)
    slots_by = slots_by_lane(spread_lanes(routes_ref[...].astype(F32), -1.0), experts)
    lanes_ref[...] = slots_by
    no_slots = jnp.zeros((LANES - experts, slots_by.shape[1]), F32)
    rows_ref[...] = jnp.concatenate([slots_by, no_slots], axis=0).T
    no_router = jnp.zeros((LANES - experts, D), F32)
    w_router_ref[...] = jnp.concatenate(
        [router_own[...].astype(F32), no_router], axis=0
    ).astype(BF)
    spread(cotangent_ref[...].astype(F32), cot_ref)
    cot_low = cot_ref[...].astype(BF)
    spot = ids((slots, lanes_ref.shape[1]), 0).astype(F32)

    def pick_of(e):
        return (spot == lanes_ref[pl.ds(e, 1), :]).astype(F32).astype(BF)

    def forward_piece(z):
        first_copy(0, z, True).wait_recv()
        first_copy(1, z, True).wait_recv()
        each(chips, lambda k: plane_copy(z, k, False).start())

    each(tensor, forward_piece)
    for d in range(1, experts + 1):
        e = after(d)
        pick = pick_of(e)
        rows_of_e = mm(pick, cot_low).astype(BF)
        noise_of_e = mm(noise, pick, NT).astype(BF)
        if d < experts:
            early_send[slot_rows(e), :] = rows_of_e
            noise_send[e] = noise_of_e
            early_copy(d, False).start()
            noise_copy(d, False).start()
        else:
            early_ref[slot_rows(e), :] = rows_of_e
            noise_all[e] = noise_of_e
    spread(tokens_ref[...].astype(F32), x_ref)
    x = x_ref[...]
    unit1, inverse1 = unit_norm(x)
    normed1 = (unit1 * gain1_ref[...]).astype(BF)
    line_in.arrive(0)
    if tensor > 2:
        line_in.start(1)

    def forward_half(z):
        each(chips, lambda k: plane_copy(z, k, True).wait_recv())
        pair_copy(z, False).start()

    each(tensor, forward_half)
    keep[0].wait()
    each(tensor, lambda z: pair_copy(z, True).wait_recv())

    def qkv_weights(t):
        return jnp.concatenate([w_ref[t, c] for c in range(3)], axis=1)

    lane = ids((SP, width), 1) // HD
    live = ids((SP, SP), 1) < SEQ
    for t in range(tensor):
        qkv_ref[t] = mm(normed1, qkv_weights(t)).astype(BF)
        for i in range(images):
            rows = slice(i * SP, (i + 1) * SP)
            q = qkv_ref[t, rows, 0:width]
            k = qkv_ref[t, rows, width : 2 * width]
            v = qkv_ref[t, rows, 2 * width : 3 * width]
            mixed = None
            for j in range(heads):
                q_j = q if heads == 1 else jnp.where(lane == j, q, jnp.zeros_like(q))
                scores = mm(q_j, k, NT) * HD ** (-0.5)
                scores = jnp.where(live, scores, -1e30)
                power = jnp.exp(scores - jnp.max(scores, -1, keepdims=True))
                attend = (power / jnp.sum(power, -1, keepdims=True)).astype(BF)
                attend_ref[i, t * heads + j] = attend
                part = mm(attend, v)
                mixed = part if mixed is None else jnp.where(lane == j, part, mixed)
            mixed_ref[t, rows, :] = mixed.astype(BF)
    residual = x
    for t in range(tensor):
        residual = residual + mm(mixed_ref[t], w_ref[t, 3], NT)
    residual_ref[...] = residual
    unit2, inverse2 = unit_norm(residual)
    normed2 = (unit2 * gain2_ref[...]).astype(BF)
    for d in range(1, experts + 1):
        e = after(d)
        rows_of_e = mm(pick_of(e), normed2).astype(BF)
        if d < experts:
            send_ref[slot_rows(e), :] = rows_of_e
            route_copy(d, False).start()
        else:
            routed_ref[slot_rows(e), :] = rows_of_e
    for step in range(1, tensor - 1):
        line_in.arrive(step)
        if step + 1 < tensor - 1:
            line_in.start(step + 1)
        if step == max(1, tensor - 3):
            line_back.start(0)
    if tensor == 2:
        line_back.start(0)
    keep[1].wait()

    fold_from, fold_to = ids((noise_all.shape[1], LANES), 0), ids((noise_all.shape[1], LANES), 1)
    fold = (
        (fold_from < 3 * experts) & (lax.rem(fold_from, experts) == fold_to)
    ).astype(F32).astype(BF)
    expert_lane = ids((chunk, LANES), 1)
    groups = experts // group

    def block_rows(at):
        return pl.ds(pl.multiple_of(at * chunk, chunk), chunk)

    def hidden_units(turn, _):
        at = lax.rem(me_e // group + groups - turn, groups)
        for k in range(group):
            d = lax.rem(me_e + experts - (at * group + k), experts)

            @pl.when(d > 0)
            def _(d=d):
                route_copy(d, True).wait_recv()
                early_copy(d, True).wait_recv()
                noise_copy(d, True).wait_recv()

        @pl.when(turn == groups // 2)
        def _():
            for step in range(0, tensor - 3):
                line_back.arrive(step)
                line_back.start(step + 1)

        rows = block_rows(at)
        came = routed_ref[rows, :]
        added = [mm(noise_all[at * group + k], fold, TN) for k in range(group)]
        added = added[0] if group == 1 else jnp.concatenate(added, axis=0)
        logits = jnp.where(expert_lane < experts, mm(came, w_router_ref[...], NT) + added, -1e30)
        power = jnp.exp(logits - jnp.max(logits, -1, keepdims=True))
        router = power / jnp.sum(power, -1, keepdims=True)
        router_ref[rows, :] = router
        gate = jnp.sum(jnp.where(expert_lane == me_e, router, 0.0), -1, keepdims=True)
        early_ref[rows, :] = (gate * early_ref[rows, :].astype(F32)).astype(BF)
        half_rows, block = chunk // 2, min(256, w_in_all.shape[2])

        def spot_of(r):
            return pl.ds(pl.multiple_of(at * chunk + r * half_rows, TILE), half_rows)

        cuts = [
            (f, n, r)
            for f in range(parts)
            for n in range(0, w_in_all.shape[2], block)
            for r in range(2)
        ]

        def pre_of(f, n, r):
            return mm(routed_ref[spot_of(r), :], w_in_all[f, :, n : n + block])

        ahead = pre_of(*cuts[0])
        for number, (f, n, r) in enumerate(cuts):
            pre = ahead
            if number + 1 < len(cuts):
                ahead = pre_of(*cuts[number + 1])
            normal, density = gelu_parts(pre)
            hidden_ref[f, spot_of(r), n : n + block] = (pre * normal).astype(BF)
            slope_ref[f, spot_of(r), n : n + block] = (normal + pre * density).astype(BF)
        return 0

    lax.fori_loop(0, groups, hidden_units, 0)

    def grads_at(block, part):
        return back_grads.at[block] if part else slope_ref.at[block, 0:D]

    sums = Sums(tensor, grads_at, held, sum_send, sum_recv)
    order = []
    for step in range(tensor):
        for f in (tensor - 1 - step, step):
            if f not in order:
                order.append(f)

    def turn_rows(ref):
        def body(at, _):
            rows = pl.ds(pl.multiple_of(at * LANES, LANES), LANES)
            wide_ref[:, rows] = ref[rows, :].T
            return 0

        lax.fori_loop(0, pairs // LANES, body, 0)

    def weight_grads(part, right):
        for f in order:
            block = mm(wide_ref[:, 0:pairs], right[f, 0:pairs, :]).astype(BF)
            grads_at(f, part)[...] = block
            for step in range(tensor - 1 if part else 1):
                for way, to in ((0, tensor - 1 - step), (1, step)):
                    if to == f:
                        sums.start_first(way, step, part)

    turn_rows(early_ref)
    weight_grads(1, hidden_ref)
    turn_rows(routed_ref)

    for step in range(max(tensor - 3, 0), tensor - 2):
        line_back.arrive(step)
        line_back.start(step + 1)
    keep[2].wait()

    def early_sent(d):
        early_copy(d, False).wait_send()
        route_copy(d, False).wait_send()

    each(experts, early_sent)

    small_ref[...] = jnp.zeros_like(small_ref)

    def near(k):
        def from_low(me):
            below = (me - k + tensor) // tensor
            return below * (me - k) + (1 - below) * k

        low = 1 - (2 * me_t) // tensor
        mirrored = tensor - 1 - from_low(tensor - 1 - me_t)
        return low * from_low(me_t) + (1 - low) * mirrored

    def unit_part(k, rows):
        f = near(k)
        w_b = w_back_all[f]
        out = mm(hidden_ref[f, rows, :], w_b)
        d_pre = (mm(early_ref[rows, :], w_b, NT) * slope_ref[f, rows, :].astype(F32)).astype(BF)
        slope_ref[f, rows, :] = d_pre
        return out, mm(d_pre, w_in_all[f], NT)

    def near_rows(at, _):
        rows = block_rows(at)
        out, back = unit_part(0, rows)
        for k in range(1, tensor - 1):
            more_out, more_back = unit_part(k, rows)
            out, back = out + more_out, back + more_back
        send_ref[rows, :] = out.astype(BF)
        early_send[rows, :] = back.astype(BF)
        return 0

    lax.fori_loop(0, groups, near_rows, 0)
    line_steps = [(step, part) for part in (1, 0) for step in range(1, tensor - 1)]

    def next_sum():
        if line_steps:
            sums.forward(*line_steps.pop(0))

    next_sum()
    line_back.arrive(tensor - 2)

    def far_rows(turn, _):
        at = lax.rem(me_e // group + 1 + turn, groups)
        rows = block_rows(at)
        router = router_ref[rows, :]
        own_lane = expert_lane == me_e
        gate = jnp.sum(jnp.where(own_lane, router, 0.0), -1, keepdims=True)
        out, back = unit_part(tensor - 1, rows)
        out = (out + send_ref[rows, :].astype(F32)).astype(BF).astype(F32)
        back = back + early_send[rows, :].astype(F32)
        d_gate = jnp.sum(early_ref[rows, :].astype(F32) * out, -1, keepdims=True)
        d_logits = (d_gate * (own_lane.astype(F32) - router)).astype(BF)
        early_send[rows, :] = (back + mm(d_logits, w_router_ref[...])).astype(BF)
        send_ref[rows, :] = (gate * out).astype(BF)
        small_ref[0:experts, :] += mm(d_logits, routed_ref[rows, :], TN)[0:experts]
        for k in range(group):
            e = at * group + k
            d = lax.rem(e + experts - me_e, experts)

            @pl.when(d > 0)
            def _(d=d):
                back_copy(d, False).start()

            @pl.when(d == 0)
            def _(e=e):
                back_ref[slot_rows(e), :] = early_send[slot_rows(e), :]
                routed_ref[slot_rows(e), :] = send_ref[slot_rows(e), :]

        return 0

    lax.fori_loop(0, groups, far_rows, 0)

    weight_grads(0, slope_ref)
    next_sum()

    each(experts, lambda d: back_copy(d, True).wait_recv())
    out_copy(experts // 2, False).start()
    slots_of = rows_ref[:, 0:experts]
    d_normed2 = take_rows(slots_of, back_ref, experts)
    unit2, inverse2 = unit_norm(residual_ref[...])
    d_rows, norm2 = norm_back(d_normed2, unit2, inverse2, gain2_ref[...])
    small_ref[experts + 1 : experts + 2, :] = norm2
    d_residual = cot_ref[...] + d_rows
    cot_ref[...] = d_residual
    d_attention = d_residual.astype(BF)
    scaling = HD ** (-0.5)
    unit1, inverse1 = unit_norm(x_ref[...])
    normed1 = (unit1 * gain1_ref[...]).astype(BF)
    for turn in range(tensor):
        t = lax.rem(me_t + 1 + turn, tensor)
        first = turn * wide
        wide_ref[:, first + 3 * width : first + wide] = mm(d_attention, mixed_ref[t], TN).astype(BF)
        d_mixed = mm(d_attention, w_ref[t, 3]).astype(BF)
        for i in range(images):
            rows = slice(i * SP, (i + 1) * SP)
            q = qkv_ref[t, rows, 0:width]
            k = qkv_ref[t, rows, width : 2 * width]
            v = qkv_ref[t, rows, 2 * width : 3 * width]
            do = d_mixed[rows]
            dq = dk = dv = None
            for j in range(heads):
                own = lane == j
                do_j = do if heads == 1 else jnp.where(own, do, jnp.zeros_like(do))
                q_j = q if heads == 1 else jnp.where(own, q, jnp.zeros_like(q))
                attend_low = attend_ref[i, t * heads + j]
                attend = attend_low.astype(F32)
                part_v = mm(attend_low, do_j, TN)
                d_attend = mm(do_j, v, NT)
                inner = jnp.sum(attend * d_attend, -1, keepdims=True)
                ds = (attend * (d_attend - inner)).astype(BF)
                part_q = mm(ds, k) * scaling
                part_k = mm(ds, q_j, TN) * scaling
                dq = part_q if dq is None else jnp.where(own, part_q, dq)
                dk = part_k if dk is None else dk + part_k
                dv = part_v if dv is None else dv + part_v
            qkv_ref[t, rows, 0:width] = dq.astype(BF)
            qkv_ref[t, rows, width : 2 * width] = dk.astype(BF)
            qkv_ref[t, rows, 2 * width : 3 * width] = dv.astype(BF)
        wide_ref[:, first : first + 3 * width] = mm(normed1, qkv_ref[t], TN).astype(BF)
        w_pair_copy(turn).start()
        if turn > 0:
            share_pair_sum(turn - 1)
        if turn > 2:
            send_piece(turn - 3)
    share_pair_sum(tensor - 1)
    sent = max(tensor - 3, 0)
    for turn in range(sent, tensor - 2):
        send_piece(turn)
    d_normed1 = None
    for t in range(tensor):
        part = mm(qkv_ref[t], qkv_weights(t), NT)
        d_normed1 = part if d_normed1 is None else d_normed1 + part
    d_rows, norm1 = norm_back(d_normed1, unit1, inverse1, gain1_ref[...])
    small_ref[experts : experts + 1, :] = norm1
    send_piece(tensor - 2)
    for step in range(1, tensor - 2):
        for way in (0, 1):
            sums.start_first(way, step, 0)
    each(experts, lambda d: small_copy(d, False).start())
    each(experts // 2, lambda d: out_copy(d, False).start())
    each(experts, lambda d: out_copy(d, False).start(), experts // 2 + 1)
    for way in (0, 1):
        sums.start_first(way, tensor - 2, 0)
    next_sum()
    small_plane[me_e] = small_ref[...]
    tokens_grad_ref[...] = compact(cot_ref[...] + d_rows)

    piece_line[me_t] = plane_sum(tensor - 1)
    each(tensor, lambda d: piece_copy(d, True).wait_recv())
    total = piece_line[0].astype(F32)
    for t in range(1, tensor):
        total = total + piece_line[t].astype(F32)
    w_sum_ref[mine, :] = total.astype(BF)
    each(chips, lambda k: final_copy(k, False).start())
    each(experts, lambda d: small_copy(d, True).wait_recv())
    total = small_plane[0]
    for e in range(1, experts):
        total = total + small_plane[e]
    small_line_send[...] = total
    each(tensor, lambda d: small_line_copy(d, False).start())
    small_line[me_t] = total
    while line_steps:
        next_sum()

    each(experts, lambda d: out_copy(d, True).wait_recv())
    each(chips, lambda k: final_copy(k, True).wait_recv())
    final_pair_copy(False).start()
    output = residual_ref[...] + take_rows(slots_of, routed_ref, experts)
    output_ref[...] = compact(output).astype(BF)

    each(tensor, lambda d: small_line_copy(d, True).wait_recv())
    total = small_line[0]
    for t in range(1, tensor):
        total = total + small_line[t]
    small_sum_ref[...] = total
    final_pair_copy(True).wait_recv()

    for part in (1, 0):
        sums.last(part)
        total = grads_at(me_t, part)[...].astype(F32)
        for way in (0, 1):
            came = held[way, tensor - 2, part].astype(F32)
            total = total + jnp.where(sums.hops(way) >= 1, came, jnp.zeros_like(came))
        if part == 0:
            in_grad_ref[...] = total.astype(BF)
        else:
            back_grad_ref[...] = total.T.astype(BF)

    sums.finish()
    line_in.finish()
    line_back.finish()

    def sent(d):
        noise_copy(d, False).wait_send()
        back_copy(d, False).wait_send()
        out_copy(d, False).wait_send()
        small_copy(d, False).wait_send()

    each(experts, sent)

    def sent_line(d):
        first_copy(0, d, False).wait_send()
        first_copy(1, d, False).wait_send()
        piece_copy(d, False).wait_send()
        small_line_copy(d, False).wait_send()
        pair_copy(d, False).wait_send()
        each(chips, lambda k: plane_copy(d, k, False).wait_send())

    each(tensor, sent_line)
    each(chips, lambda k: final_copy(k, False).wait_send())
    final_pair_copy(False).wait_send()
    for t in range(tensor):
        w_pair_copy(t).wait_send()
        each(chips, lambda k, t=t: w_copy(t, k, False).wait_send())


def finish_kernel(
    experts, output_in, tokens_in, w_sum_ref, small_ref, in_ref, back_ref,
    output_ref, tokens_ref, norm1_ref, qkv_ref, out_ref, norm2_ref, router_ref,
    in_grad_ref, back_grad_ref,
):
    output_ref[...] = output_in[...]
    tokens_ref[...] = tokens_in[...]
    width = out_ref.shape[0]
    for c in range(3):
        qkv_ref[c] = w_sum_ref[:, c * width : (c + 1) * width].astype(F32)
    out_ref[...] = w_sum_ref[:, 3 * width : 4 * width].T.astype(F32)
    router_ref[...] = small_ref[0:experts, :]
    norm1_ref[...] = small_ref[experts : experts + 1, :]
    norm2_ref[...] = small_ref[experts + 1 : experts + 2, :]
    in_grad_ref[...] = in_ref[...].astype(F32)
    back_grad_ref[...] = back_ref[...].astype(F32)


def per_device(
    tokens, norm1_gain, w_qkv, w_out, norm2_gain, w_router, noise, routes, w_in, w_back, cotangent
):
    own_rows = tokens.shape[0]
    experts = noise.shape[1]
    tensor = lax.axis_size("tensor")
    images = own_rows // SEQ
    rows = images * SP
    capacity = (2 * own_rows * TOP + experts - 1) // experts
    slots = up(capacity, TILE)
    group = max(g for g in range(1, experts + 1) if experts % g == 0 and g * slots <= 2 * SP)
    width = w_out.shape[0]
    hidden = w_in.shape[2]
    heads = tensor * width // HD
    piece = D // experts
    small_rows = up(experts + 2, 8)
    noise_rows = up(3 * experts, TILE)
    pairs = experts * slots
    dma = pltpu.SemaphoreType.DMA
    bf, f32 = (lambda *dims: pltpu.VMEM(dims, BF)), (lambda *dims: pltpu.VMEM(dims, F32))

    output, grad_tokens, w_sum, small, grad_in, grad_back = call(
        functools.partial(block_kernel, experts, tensor, images, group),
        (
            shape((own_rows, D)),
            shape((own_rows, D), F32),
            shape((D, 4 * width)),
            shape((small_rows, D), F32),
            shape((D, hidden)),
            shape((hidden, D)),
        ),
        scratch=(
            bf(tensor, 4, D, width),
            bf(LANES, D),
            bf(tensor, D, hidden),
            bf(tensor, hidden, D),
            f32(up(own_rows, TILE), D),
            f32(rows, D),
            f32(rows, D),
            f32(rows, LANES),
            f32(experts, rows),
            bf(tensor, rows, 3 * width),
            bf(images, heads, SP, SP),
            bf(tensor, rows, width),
            f32(rows, D),
            bf(pairs, D),
            bf(pairs, D),
            bf(pairs, D),
            bf(pairs, D),
            bf(experts, noise_rows, slots),
            bf(experts, noise_rows, slots),
            f32(pairs, LANES),
            bf(tensor, pairs, hidden),
            bf(tensor, max(pairs, D), hidden),
            bf(pairs, D),
            bf(2, tensor - 1, 2, D, hidden),
            bf(D, max(pairs, tensor * 4 * width)),
            bf(tensor, D, hidden),
            bf(tensor, D // CORES, 4 * width),
            bf(experts // CORES, tensor, piece, 4 * width),
            bf(tensor, piece, 4 * width),
            bf(tensor, piece, 4 * width),
            f32(small_rows, D),
            f32(experts, small_rows, D),
            f32(small_rows, D),
            f32(tensor, small_rows, D),
            dma((3,)),
            dma((2, 2, tensor)),
            dma((2, tensor, experts // CORES)),
            dma((2, tensor)),
            dma((2, 2, tensor - 1)),
            dma((2, 2, tensor - 1)),
            dma((2, experts)),
            dma((2, experts)),
            dma((2, experts)),
            dma((2, experts)),
            dma((2, experts)),
            dma((2, tensor - 1, 2)),
            dma((2, tensor - 1, 2)),
            dma((2, tensor)),
            dma((2, tensor, experts // CORES)),
            dma((2, tensor)),
            dma((2, experts // CORES)),
            dma((2, experts)),
            dma((2, tensor)),
        ),
        far_in=(8, 9, 10),
        collective_id=0,
        has_side_effects=True,
    )(
        routes.T, tokens, cotangent, noise.T, norm1_gain.reshape(1, D), norm2_gain.reshape(1, D),
        w_router.T, w_out, w_qkv.transpose(1, 0, 2), w_in[0], w_back[0],
    )
    output, grad_tokens, norm1, grad_qkv, grad_out, norm2, router, grad_in, grad_back = call(
        functools.partial(finish_kernel, experts),
        (
            shape((own_rows, D)),
            shape((own_rows, D), F32),
            shape((1, D), F32),
            shape((3, D, width), F32),
            shape((width, D), F32),
            shape((1, D), F32),
            shape((experts, D), F32),
            shape((D, hidden), F32),
            shape((hidden, D), F32),
        ),
    )(output, grad_tokens, w_sum, small, grad_in, grad_back)
    return (
        output,
        grad_tokens,
        norm1.reshape(D),
        grad_qkv.transpose(1, 0, 2),
        grad_out,
        norm2.reshape(D),
        router.T,
        grad_in[None],
        grad_back[None],
    )


def solution(mesh):
    rows = P(("expert", "tensor"), None)
    placed = (
        rows,
        P(),
        P(None, None, "tensor"),
        P("tensor", None),
        P(),
        P(),
        rows,
        rows,
        P("expert", None, "tensor"),
        P("expert", "tensor", None),
        rows,
    )
    return jax.shard_map(
        per_device,
        mesh=mesh,
        in_specs=placed,
        out_specs=(
            rows,
            rows,
            P(),
            P(None, None, "tensor"),
            P("tensor", None),
            P(),
            P(),
            P("expert", None, "tensor"),
            P("expert", "tensor", None),
        ),
        check_vma=False,
    )
```

```python
import functools

import jax
import jax.numpy as jnp
from jax import lax
from jax.experimental import pallas as pl
from jax.experimental.pallas import tpu as pltpu
from jax.sharding import PartitionSpec as P

D = 512
HD = 64
CORES = 2
TOP = 2
SEQ = 197
LANES = 128
TILE = 16
EPSILON = 1e-06
DENSITY = 0.3989422804014327
TAIL = 0.5 / DENSITY
BF = jnp.bfloat16
F32 = jnp.float32
VMEM_BYTES = 62 * 1024 * 1024

NN = (((1,), (0,)), ((), ()))
NT = (((1,), (1,)), ((), ()))
TN = (((0,), (0,)), ((), ()))


def up(value, unit):
    return (value + unit - 1) // unit * unit


SP = up(SEQ, TILE)


def mm(a, b, dims=NN):
    return lax.dot_general(a, b, dims, preferred_element_type=F32)


def call(
    body, out_shape, scratch=(), flops=0, moved=0, prefetch=(), far_in=(), far_out=(), **more
):
    params = pltpu.CompilerParams(vmem_limit_bytes=VMEM_BYTES, **more)
    cost = pl.CostEstimate(flops=flops, bytes_accessed=moved, transcendentals=0)

    def spec(place, far, scalar=()):
        if place in scalar:
            return pl.BlockSpec(memory_space=pltpu.SMEM)
        return pl.BlockSpec(memory_space=pl.ANY if place in far else pltpu.VMEM)

    def run(*args):
        return pl.pallas_call(
            body,
            out_shape=out_shape,
            in_specs=[spec(place, far_in, prefetch) for place in range(len(args))],
            out_specs=tuple(spec(place, far_out) for place in range(len(out_shape))),
            scratch_shapes=list(scratch),
            compiler_params=params,
            cost_estimate=cost,
        )(*args)

    return run


def shape(dims, dtype=BF):
    return jax.ShapeDtypeStruct(dims, dtype)


def unit_norm(values):
    center = values - jnp.mean(values, -1, keepdims=True)
    spread = jnp.mean(center * center, -1, keepdims=True)
    inverse = lax.rsqrt(spread + EPSILON)
    return center * inverse, inverse


def norm_back(grad_rows, normed, inverse, gain):
    scaled = grad_rows * gain
    inner = (
        scaled
        - jnp.mean(scaled, -1, keepdims=True)
        - normed * jnp.mean(scaled * normed, -1, keepdims=True)
    )
    return inverse * inner, jnp.sum(grad_rows * normed, axis=0, keepdims=True)


def ids(shape_of, dim):
    return lax.broadcasted_iota(jnp.int32, shape_of, dim)


def slots_by_lane(routes, experts):
    rows = routes.shape[1]
    which = ids((experts, rows), 0).astype(F32)
    named = (routes[0:1] == which) | (routes[1:2] == which)
    before = (ids((rows, rows), 0) < ids((rows, rows), 1)).astype(F32).astype(BF)
    rank = mm(named.astype(F32).astype(BF), before)
    return jnp.where(named, rank, -1.0)


def take_rows(slots, in_ref, experts):
    count = in_ref.shape[0] // experts
    rows = slots.shape[0]
    place = ids((rows, count), 1).astype(F32)
    total = None
    for e in range(experts):
        pick = (place == slots[:, e : e + 1]).astype(F32).astype(BF)
        part = mm(pick, in_ref[e * count : (e + 1) * count, :])
        total = part if total is None else total + part
    return total


MESH = pl.DeviceIdType.MESH


def greet(axes):
    barrier = pltpu.get_barrier_semaphore()
    for name, size in axes:
        me = lax.axis_index(name)

        def hello(d, _, name=name, size=size, me=me):
            pl.semaphore_signal(
                barrier, inc=1, device_id={name: lax.rem(me + d, size)}, device_id_type=MESH
            )
            return 0

        lax.fori_loop(1, size, hello, 0)
    pl.semaphore_wait(barrier, sum(size - 1 for _, size in axes))


def remote(src, dst, send_sem, recv_sem, name, to):
    return pltpu.make_async_remote_copy(
        src_ref=src,
        dst_ref=dst,
        send_sem=send_sem,
        recv_sem=recv_sem,
        device_id={name: to},
        device_id_type=MESH,
    )


def each(size, step, first=1):
    def body(d, _):
        step(d)
        return 0

    lax.fori_loop(first, size, body, 0)


class Line:
    def __init__(self, size, own, everyone, send_sem, recv_sem):
        self.size, self.own, self.all = size, own, everyone
        self.send_sem, self.recv_sem = send_sem, recv_sem
        self.me = lax.axis_index("tensor")

    def copy(self, way, step, arriving):
        toward = 1 if way == 0 else -1
        owner = self.me - toward * (step + (1 if arriving else 0))
        src = self.own if step == 0 else self.all.at[owner]
        return remote(
            src, self.all.at[owner], self.send_sem.at[way, step], self.recv_sem.at[way, step],
            "tensor", self.me + toward,
        )

    def sends(self, way, step):
        last = self.size - 1
        if way == 0:
            return (self.me >= step) & (self.me < last)
        return (self.me <= last - step) & (self.me > 0)

    def receives(self, way, step):
        if way == 0:
            return self.me >= step + 1
        return self.me <= self.size - 2 - step

    def start(self, step):
        for way in (0, 1):
            pl.when(self.sends(way, step))(lambda way=way: self.copy(way, step, False).start())

    def arrive(self, step):
        for way in (0, 1):
            pl.when(self.receives(way, step))(
                lambda way=way: self.copy(way, step, True).wait_recv()
            )

    def finish(self):
        for step in range(self.size - 1):
            for way in (0, 1):
                pl.when(self.sends(way, step))(
                    lambda way=way, step=step: self.copy(way, step, False).wait_send()
                )


def gelu_parts(pre):
    density = jnp.exp2(pre * pre * (-0.5 * 1.4426950408889634)) * DENSITY
    t = pl.reciprocal(1.0 + jnp.abs(pre * (0.3275911 * 0.5**0.5)), approx=True)
    series = t * (
        0.254829592 * TAIL
        + t
        * (
            -0.284496736 * TAIL
            + t * (1.421413741 * TAIL + t * (-1.453152027 * TAIL + t * (1.061405429 * TAIL)))
        )
    )
    tail = series * density
    return jnp.where(pre < 0, tail, 1.0 - tail), density


class Sums:
    def __init__(self, size, own, held, send_sem, recv_sem):
        self.size, self.own, self.held = size, own, held
        self.send_sem, self.recv_sem = send_sem, recv_sem
        self.me = lax.axis_index("tensor")

    def hops(self, way):
        return self.me if way == 0 else self.size - 1 - self.me

    def block(self, way, step):
        ahead = self.size - 1 + self.hops(way) - step
        return ahead if way == 0 else self.size - 1 - ahead

    def copy(self, way, step, part, first):
        toward = 1 if way == 0 else -1
        if first:
            src = self.own(self.block(way, step), part)
        else:
            src = self.held.at[way, max(step - 1, 0), part]
        return remote(
            src, self.held.at[way, step, part],
            self.send_sem.at[way, step, part], self.recv_sem.at[way, step, part],
            "tensor", self.me + toward,
        )

    def start_first(self, way, step, part):
        pl.when(self.hops(way) == 0)(lambda: self.copy(way, step, part, True).start())

    def middle(self, way, step):
        hops = self.hops(way)
        return (hops >= 1) & (hops <= step) & (hops < self.size - 1)

    def forward(self, step, part):
        for way in (0, 1):

            def go(way=way):
                self.copy(way, step - 1, part, False).wait_recv()
                held = self.held.at[way, step - 1, part]
                mine = self.own(self.block(way, step), part)
                add_into(held, mine)
                self.copy(way, step, part, False).start()

            pl.when(self.middle(way, step))(go)

    def last(self, part):
        for way in (0, 1):
            pl.when(self.hops(way) >= 1)(
                lambda way=way: self.copy(way, self.size - 2, part, False).wait_recv()
            )

    def finish(self):
        for part in (0, 1):
            for step in range(self.size - 1):
                for way in (0, 1):
                    sends = (self.hops(way) == 0) | self.middle(way, step)
                    pl.when(sends)(
                        lambda way=way, step=step, part=part: self.copy(
                            way, step, part, False
                        ).wait_send()
                    )


def add_into(held, mine):
    rows = held.shape[0]
    block = min(rows, 128)

    def body(r, _):
        at = pl.ds(pl.multiple_of(r * block, block), block)
        held[at, :] = (held[at, :].astype(F32) + mine[at, :].astype(F32)).astype(BF)
        return 0

    lax.fori_loop(0, rows // block, body, 0)


def block_kernel(
    experts, tensor, images, group,
    routes_ref, tokens_ref, cotangent_ref, noise_ref, gain1_ref, gain2_ref, router_own,
    w_out_own, w_qkv_own, w_in_own, w_back_own,
    output_ref, tokens_grad_ref, w_sum_ref, small_sum_ref, in_grad_ref, back_grad_ref,
    w_ref, w_router_ref, w_in_all, w_back_all, narrow, x_ref, cot_ref, rows_ref, lanes_ref,
    qkv_ref, attend_ref, mixed_ref, residual_ref,
    send_ref, routed_ref, early_send, early_ref, noise_send, noise_all, router_ref,
    hidden_ref, slope_ref, back_ref, held,
    wide_ref, back_grads, pair_ref, pieces, piece_send, piece_line,
    small_ref, small_plane, small_line_send, small_line,
    own_sem, first_sems, plane_sems, pair_sems, in_sems, in_back_sems, route_sems, early_sems, noise_sems,
    back_sems, out_sems, sum_send, sum_recv, w_pair_sems, w_sems, piece_sems, final_sems,
    small_sems, small_line_sems,
):
    own_rows = tokens_ref.shape[0]
    width = w_out_own.shape[0]
    wide = 4 * width
    heads = width // HD
    slots = noise_send.shape[2]
    pairs = experts * slots
    parts = w_in_all.shape[0]
    chunk = group * slots
    me_e, me_t = lax.axis_index("expert"), lax.axis_index("tensor")
    piece = D // experts

    chips = experts // CORES
    core = lax.rem(me_e, CORES)
    half = chips * piece

    def rows_at(e):
        at = lax.rem(e, CORES) * chips + e // CORES
        return pl.ds(pl.multiple_of(at * piece, piece), piece)

    def half_at(which):
        return pl.ds(pl.multiple_of(which * half, half), half)

    def chip_after(k):
        return lax.rem(me_e + CORES * k, experts)

    def chip_place(k, arriving):
        return lax.rem(me_e + experts - CORES * k, experts) if arriving else me_e

    mine = rows_at(me_e)

    def after(d):
        return lax.rem(me_e + d, experts)

    def place(d, arriving):
        return lax.rem(me_e + experts - d, experts) if arriving else me_e

    def swap_copy(src, dst, sems, d, arriving):
        to = after(d)
        return remote(
            src.at[to], dst.at[place(d, arriving)], sems.at[0, d], sems.at[1, d], "expert", to
        )

    def line_copy(src, dst, sems, d, arriving):
        owner = lax.rem(me_t + tensor - d, tensor) if arriving else me_t
        return remote(
            src, dst(owner), sems.at[0, d], sems.at[1, d],
            "tensor", lax.rem(me_t + d, tensor),
        )

    def first_copy(which, d, arriving):
        parts_of = (slice(0, 3), slice(3, 4))[which]
        src = w_ref.at[me_t, parts_of, mine] if which else w_qkv_own.at[:, mine]
        return line_copy(
            src, lambda owner: w_ref.at[owner, parts_of, mine], first_sems.at[which], d, arriving
        )

    def plane_copy(z, k, arriving):
        owner = lax.rem(me_t + tensor - z, tensor)
        block = w_ref.at[owner, :, rows_at(chip_place(k, arriving))]
        return remote(
            block, block, plane_sems.at[0, z, k], plane_sems.at[1, z, k], "expert", chip_after(k)
        )

    def pair_copy(z, arriving):
        owner = lax.rem(me_t + tensor - z, tensor)
        block = w_ref.at[owner, :, half_at(CORES - 1 - core if arriving else core)]
        return remote(
            block, block, pair_sems.at[0, z], pair_sems.at[1, z], "expert",
            me_e + CORES - 1 - 2 * core,
        )

    def slot_rows(e):
        return pl.ds(pl.multiple_of(e * slots, slots), slots)

    def flat_copy(src, dst, sems, d, arriving):
        return remote(
            src.at[slot_rows(after(d))], dst.at[slot_rows(place(d, arriving))],
            sems.at[0, d], sems.at[1, d], "expert", after(d),
        )

    def route_copy(d, arriving):
        return flat_copy(send_ref, routed_ref, route_sems, d, arriving)

    def early_copy(d, arriving):
        return flat_copy(early_send, early_ref, early_sems, d, arriving)

    def noise_copy(d, arriving):
        return swap_copy(noise_send, noise_all, noise_sems, d, arriving)

    def back_copy(d, arriving):
        return flat_copy(early_send, back_ref, back_sems, d, arriving)

    def out_copy(d, arriving):
        return flat_copy(send_ref, early_ref, out_sems, d, arriving)

    def columns(t):
        return slice(t * wide, (t + 1) * wide)

    def w_pair_copy(t):
        return remote(
            wide_ref.at[half_at(CORES - 1 - core), columns(t)], pair_ref.at[t],
            w_pair_sems.at[0, t], w_pair_sems.at[1, t], "expert", me_e + CORES - 1 - 2 * core,
        )

    def w_copy(t, k, arriving):
        return remote(
            wide_ref.at[rows_at(chip_after(k)), columns(t)],
            pieces.at[chip_place(k, arriving) // CORES, t],
            w_sems.at[0, t, k], w_sems.at[1, t, k], "expert", chip_after(k),
        )

    def share_pair_sum(t):
        w_pair_copy(t).wait_recv()
        ours = half_at(core)
        pair_sum = wide_ref[ours, columns(t)].astype(F32) + pair_ref[t].astype(F32)
        wide_ref[ours, columns(t)] = pair_sum.astype(BF)
        each(chips, lambda k: w_copy(t, k, False).start())
        pieces[me_e // CORES, t] = wide_ref[mine, columns(t)]

    def plane_sum(t):
        each(chips, lambda k: w_copy(t, k, True).wait_recv())
        total = pieces[0, t].astype(F32)
        for e in range(1, chips):
            total = total + pieces[e, t].astype(F32)
        return total.astype(BF)

    def send_piece(t):
        piece_send[t] = plane_sum(t)
        piece_copy(t + 1, False).start()

    def piece_copy(d, arriving):
        return line_copy(piece_send.at[d - 1], lambda owner: piece_line.at[owner], piece_sems, d, arriving)

    def final_copy(k, arriving):
        block = w_sum_ref.at[rows_at(chip_place(k, arriving))]
        return remote(
            block, block, final_sems.at[0, k], final_sems.at[1, k], "expert", chip_after(k)
        )

    def final_pair_copy(arriving):
        block = w_sum_ref.at[half_at(CORES - 1 - core if arriving else core)]
        return remote(
            block, block, final_sems.at[0, 0], final_sems.at[1, 0], "expert",
            me_e + CORES - 1 - 2 * core,
        )

    def small_copy(d, arriving):
        return remote(
            small_ref, small_plane.at[place(d, arriving)], small_sems.at[0, d],
            small_sems.at[1, d], "expert", after(d),
        )

    def small_line_copy(d, arriving):
        return line_copy(
            small_line_send, lambda owner: small_line.at[owner], small_line_sems, d, arriving
        )

    greet((("expert", experts), ("tensor", tensor)))
    each(tensor, lambda d: first_copy(0, d, False).start())
    line_in = Line(tensor, w_in_own, w_in_all, in_sems.at[0], in_sems.at[1])
    line_back = Line(tensor, w_back_own, w_back_all, in_back_sems.at[0], in_back_sems.at[1])
    w_ref[me_t, 3] = w_out_own[...].T
    each(tensor, lambda d: first_copy(1, d, False).start())
    line_in.start(0)
    keep = [
        pltpu.make_async_copy(w_qkv_own, w_ref.at[me_t, 0:3], own_sem.at[0]),
        pltpu.make_async_copy(w_in_own, w_in_all.at[me_t], own_sem.at[1]),
        pltpu.make_async_copy(w_back_own, w_back_all.at[me_t], own_sem.at[2]),
    ]
    for copy in keep:
        copy.start()

    def spread(compact, to_ref, fill=0.0):
        columns = compact.shape[1]
        narrow[0:own_rows, 0:columns] = compact
        to_ref[...] = jnp.full(to_ref.shape, fill, F32)
        for i in range(images):
            to_ref[i * SP : i * SP + SEQ, 0:columns] = narrow[
                i * SEQ : (i + 1) * SEQ, 0:columns
            ]

    def compact(padded):
        for i in range(images):
            narrow[i * SEQ : (i + 1) * SEQ, :] = padded[i * SP : i * SP + SEQ, :]
        return narrow[0:own_rows, :]

    def spread_lanes(packed, fill):
        gap = jnp.full((packed.shape[0], SP - SEQ), fill, F32)
        blocks = []
        for i in range(images):
            blocks += [packed[:, i * SEQ : (i + 1) * SEQ], gap]
        return jnp.concatenate(blocks, axis=1)

    noise = spread_lanes(noise_ref[...], 0.0)
    high = noise.astype(BF).astype(F32)
    middle = (noise - high).astype(BF).astype(F32)
    low = noise - high - middle
    noise_parts = [high, middle, low]
    if noise_send.shape[1] > 3 * experts:
        noise_parts.append(jnp.zeros((noise_send.shape[1] - 3 * experts, noise.shape[1]), F32))
    noise = jnp.concatenate(noise_parts, axis=0).astype(BF)
    slots_by = slots_by_lane(spread_lanes(routes_ref[...].astype(F32), -1.0), experts)
    lanes_ref[...] = slots_by
    no_slots = jnp.zeros((LANES - experts, slots_by.shape[1]), F32)
    rows_ref[...] = jnp.concatenate([slots_by, no_slots], axis=0).T
    no_router = jnp.zeros((LANES - experts, D), F32)
    w_router_ref[...] = jnp.concatenate(
        [router_own[...].astype(F32), no_router], axis=0
    ).astype(BF)
    spread(cotangent_ref[...].astype(F32), cot_ref)
    cot_low = cot_ref[...].astype(BF)
    spot = ids((slots, lanes_ref.shape[1]), 0).astype(F32)

    def pick_of(e):
        return (spot == lanes_ref[pl.ds(e, 1), :]).astype(F32).astype(BF)

    def forward_piece(z):
        first_copy(0, z, True).wait_recv()
        first_copy(1, z, True).wait_recv()
        each(chips, lambda k: plane_copy(z, k, False).start())

    each(tensor, forward_piece)
    for d in range(1, experts + 1):
        e = after(d)
        pick = pick_of(e)
        rows_of_e = mm(pick, cot_low).astype(BF)
        noise_of_e = mm(noise, pick, NT).astype(BF)
        if d < experts:
            early_send[slot_rows(e), :] = rows_of_e
            noise_send[e] = noise_of_e
            early_copy(d, False).start()
            noise_copy(d, False).start()
        else:
            early_ref[slot_rows(e), :] = rows_of_e
            noise_all[e] = noise_of_e
    spread(tokens_ref[...].astype(F32), x_ref)
    x = x_ref[...]
    unit1, inverse1 = unit_norm(x)
    normed1 = (unit1 * gain1_ref[...]).astype(BF)
    line_in.arrive(0)
    if tensor > 2:
        line_in.start(1)

    def forward_half(z):
        each(chips, lambda k: plane_copy(z, k, True).wait_recv())
        pair_copy(z, False).start()

    each(tensor, forward_half)
    keep[0].wait()
    each(tensor, lambda z: pair_copy(z, True).wait_recv())

    def qkv_weights(t):
        return jnp.concatenate([w_ref[t, c] for c in range(3)], axis=1)

    lane = ids((SP, width), 1) // HD
    live = ids((SP, SP), 1) < SEQ
    for t in range(tensor):
        qkv_ref[t] = mm(normed1, qkv_weights(t)).astype(BF)
        for i in range(images):
            rows = slice(i * SP, (i + 1) * SP)
            q = qkv_ref[t, rows, 0:width]
            k = qkv_ref[t, rows, width : 2 * width]
            v = qkv_ref[t, rows, 2 * width : 3 * width]
            mixed = None
            for j in range(heads):
                q_j = q if heads == 1 else jnp.where(lane == j, q, jnp.zeros_like(q))
                scores = mm(q_j, k, NT) * HD ** (-0.5)
                scores = jnp.where(live, scores, -1e30)
                power = jnp.exp(scores - jnp.max(scores, -1, keepdims=True))
                attend = (power / jnp.sum(power, -1, keepdims=True)).astype(BF)
                attend_ref[i, t * heads + j] = attend
                part = mm(attend, v)
                mixed = part if mixed is None else jnp.where(lane == j, part, mixed)
            mixed_ref[t, rows, :] = mixed.astype(BF)
    residual = x
    for t in range(tensor):
        residual = residual + mm(mixed_ref[t], w_ref[t, 3], NT)
    residual_ref[...] = residual
    unit2, inverse2 = unit_norm(residual)
    normed2 = (unit2 * gain2_ref[...]).astype(BF)
    for d in range(1, experts + 1):
        e = after(d)
        rows_of_e = mm(pick_of(e), normed2).astype(BF)
        if d < experts:
            send_ref[slot_rows(e), :] = rows_of_e
            route_copy(d, False).start()
        else:
            routed_ref[slot_rows(e), :] = rows_of_e
    for step in range(1, tensor - 1):
        line_in.arrive(step)
        if step + 1 < tensor - 1:
            line_in.start(step + 1)
        if step == max(1, tensor - 3):
            line_back.start(0)
    if tensor == 2:
        line_back.start(0)
    keep[1].wait()

    fold_from, fold_to = ids((noise_all.shape[1], LANES), 0), ids((noise_all.shape[1], LANES), 1)
    fold = (
        (fold_from < 3 * experts) & (lax.rem(fold_from, experts) == fold_to)
    ).astype(F32).astype(BF)
    expert_lane = ids((chunk, LANES), 1)
    groups = experts // group

    def block_rows(at):
        return pl.ds(pl.multiple_of(at * chunk, chunk), chunk)

    def hidden_units(turn, _):
        at = lax.rem(me_e // group + groups - turn, groups)
        for k in range(group):
            d = lax.rem(me_e + experts - (at * group + k), experts)

            @pl.when(d > 0)
            def _(d=d):
                route_copy(d, True).wait_recv()
                early_copy(d, True).wait_recv()
                noise_copy(d, True).wait_recv()

        @pl.when(turn == groups // 2)
        def _():
            for step in range(0, tensor - 3):
                line_back.arrive(step)
                line_back.start(step + 1)

        rows = block_rows(at)
        came = routed_ref[rows, :]
        added = [mm(noise_all[at * group + k], fold, TN) for k in range(group)]
        added = added[0] if group == 1 else jnp.concatenate(added, axis=0)
        logits = jnp.where(expert_lane < experts, mm(came, w_router_ref[...], NT) + added, -1e30)
        power = jnp.exp(logits - jnp.max(logits, -1, keepdims=True))
        router = power / jnp.sum(power, -1, keepdims=True)
        router_ref[rows, :] = router
        gate = jnp.sum(jnp.where(expert_lane == me_e, router, 0.0), -1, keepdims=True)
        early_ref[rows, :] = (gate * early_ref[rows, :].astype(F32)).astype(BF)
        half_rows, block = chunk // 2, min(256, w_in_all.shape[2])

        def spot_of(r):
            return pl.ds(pl.multiple_of(at * chunk + r * half_rows, TILE), half_rows)

        cuts = [
            (f, n, r)
            for f in range(parts)
            for n in range(0, w_in_all.shape[2], block)
            for r in range(2)
        ]

        def pre_of(f, n, r):
            return mm(routed_ref[spot_of(r), :], w_in_all[f, :, n : n + block])

        ahead = pre_of(*cuts[0])
        for number, (f, n, r) in enumerate(cuts):
            pre = ahead
            if number + 1 < len(cuts):
                ahead = pre_of(*cuts[number + 1])
            normal, density = gelu_parts(pre)
            hidden_ref[f, spot_of(r), n : n + block] = (pre * normal).astype(BF)
            slope_ref[f, spot_of(r), n : n + block] = (normal + pre * density).astype(BF)
        return 0

    lax.fori_loop(0, groups, hidden_units, 0)

    def grads_at(block, part):
        return back_grads.at[block] if part else slope_ref.at[block, 0:D]

    sums = Sums(tensor, grads_at, held, sum_send, sum_recv)
    order = []
    for step in range(tensor):
        for f in (tensor - 1 - step, step):
            if f not in order:
                order.append(f)

    def turn_rows(ref):
        def body(at, _):
            rows = pl.ds(pl.multiple_of(at * LANES, LANES), LANES)
            wide_ref[:, rows] = ref[rows, :].T
            return 0

        lax.fori_loop(0, pairs // LANES, body, 0)

    def weight_grads(part, right):
        for f in order:
            block = mm(wide_ref[:, 0:pairs], right[f, 0:pairs, :]).astype(BF)
            grads_at(f, part)[...] = block
            for step in range(tensor - 1 if part else 1):
                for way, to in ((0, tensor - 1 - step), (1, step)):
                    if to == f:
                        sums.start_first(way, step, part)

    turn_rows(early_ref)
    weight_grads(1, hidden_ref)
    turn_rows(routed_ref)

    for step in range(max(tensor - 3, 0), tensor - 2):
        line_back.arrive(step)
        line_back.start(step + 1)
    keep[2].wait()

    def early_sent(d):
        early_copy(d, False).wait_send()
        route_copy(d, False).wait_send()

    each(experts, early_sent)

    small_ref[...] = jnp.zeros_like(small_ref)

    def near(k):
        def from_low(me):
            below = (me - k + tensor) // tensor
            return below * (me - k) + (1 - below) * k

        low = 1 - (2 * me_t) // tensor
        mirrored = tensor - 1 - from_low(tensor - 1 - me_t)
        return low * from_low(me_t) + (1 - low) * mirrored

    def unit_part(k, rows):
        f = near(k)
        w_b = w_back_all[f]
        out = mm(hidden_ref[f, rows, :], w_b)
        d_pre = (mm(early_ref[rows, :], w_b, NT) * slope_ref[f, rows, :].astype(F32)).astype(BF)
        slope_ref[f, rows, :] = d_pre
        return out, mm(d_pre, w_in_all[f], NT)

    def near_rows(at, _):
        rows = block_rows(at)
        out, back = unit_part(0, rows)
        for k in range(1, tensor - 1):
            more_out, more_back = unit_part(k, rows)
            out, back = out + more_out, back + more_back
        send_ref[rows, :] = out.astype(BF)
        early_send[rows, :] = back.astype(BF)
        return 0

    lax.fori_loop(0, groups, near_rows, 0)
    line_steps = [(step, part) for part in (1, 0) for step in range(1, tensor - 1)]

    def next_sum():
        if line_steps:
            sums.forward(*line_steps.pop(0))

    next_sum()
    line_back.arrive(tensor - 2)

    def far_rows(turn, _):
        at = lax.rem(me_e // group + 1 + turn, groups)
        rows = block_rows(at)
        router = router_ref[rows, :]
        own_lane = expert_lane == me_e
        gate = jnp.sum(jnp.where(own_lane, router, 0.0), -1, keepdims=True)
        out, back = unit_part(tensor - 1, rows)
        out = (out + send_ref[rows, :].astype(F32)).astype(BF).astype(F32)
        back = back + early_send[rows, :].astype(F32)
        d_gate = jnp.sum(early_ref[rows, :].astype(F32) * out, -1, keepdims=True)
        d_logits = (d_gate * (own_lane.astype(F32) - router)).astype(BF)
        early_send[rows, :] = (back + mm(d_logits, w_router_ref[...])).astype(BF)
        send_ref[rows, :] = (gate * out).astype(BF)
        router_ref[rows, :] = d_logits.astype(F32)
        for k in range(group):
            e = at * group + k
            d = lax.rem(e + experts - me_e, experts)

            @pl.when(d > 0)
            def _(d=d):
                back_copy(d, False).start()

            @pl.when(d == 0)
            def _(e=e):
                back_ref[slot_rows(e), :] = early_send[slot_rows(e), :]
                early_ref[slot_rows(e), :] = send_ref[slot_rows(e), :]

        return 0

    lax.fori_loop(0, groups, far_rows, 0)

    weight_grads(0, slope_ref)

    def router_part(at, _):
        rows = block_rows(at)
        d_logits = router_ref[rows, :].astype(BF)
        small_ref[0:experts, :] += mm(d_logits, routed_ref[rows, :], TN)[0:experts]
        return 0

    lax.fori_loop(0, groups, router_part, 0)
    unit1, inverse1 = unit_norm(x_ref[...])
    normed1 = (unit1 * gain1_ref[...]).astype(BF)
    unit2, inverse2 = unit_norm(residual_ref[...])
    each(experts, lambda d: back_copy(d, True).wait_recv())
    out_copy(experts // 2, False).start()
    slots_of = rows_ref[:, 0:experts]
    d_normed2 = take_rows(slots_of, back_ref, experts)
    d_rows, norm2 = norm_back(d_normed2, unit2, inverse2, gain2_ref[...])
    small_ref[experts + 1 : experts + 2, :] = norm2
    d_residual = cot_ref[...] + d_rows
    cot_ref[...] = d_residual
    d_attention = d_residual.astype(BF)
    scaling = HD ** (-0.5)
    for turn in range(tensor):
        t = lax.rem(me_t + 1 + turn, tensor)
        first = turn * wide
        wide_ref[:, first + 3 * width : first + wide] = mm(d_attention, mixed_ref[t], TN).astype(BF)
        d_mixed = mm(d_attention, w_ref[t, 3]).astype(BF)
        for i in range(images):
            rows = slice(i * SP, (i + 1) * SP)
            q = qkv_ref[t, rows, 0:width]
            k = qkv_ref[t, rows, width : 2 * width]
            v = qkv_ref[t, rows, 2 * width : 3 * width]
            do = d_mixed[rows]
            dq = dk = dv = None
            for j in range(heads):
                own = lane == j
                do_j = do if heads == 1 else jnp.where(own, do, jnp.zeros_like(do))
                q_j = q if heads == 1 else jnp.where(own, q, jnp.zeros_like(q))
                attend_low = attend_ref[i, t * heads + j]
                attend = attend_low.astype(F32)
                part_v = mm(attend_low, do_j, TN)
                d_attend = mm(do_j, v, NT)
                inner = jnp.sum(attend * d_attend, -1, keepdims=True)
                ds = (attend * (d_attend - inner)).astype(BF)
                part_q = mm(ds, k) * scaling
                part_k = mm(ds, q_j, TN) * scaling
                dq = part_q if dq is None else jnp.where(own, part_q, dq)
                dk = part_k if dk is None else dk + part_k
                dv = part_v if dv is None else dv + part_v
            qkv_ref[t, rows, 0:width] = dq.astype(BF)
            qkv_ref[t, rows, width : 2 * width] = dk.astype(BF)
            qkv_ref[t, rows, 2 * width : 3 * width] = dv.astype(BF)
        wide_ref[:, first : first + 3 * width] = mm(normed1, qkv_ref[t], TN).astype(BF)
        w_pair_copy(turn).start()
        if turn > 0:
            share_pair_sum(turn - 1)
        if turn == 0:
            next_sum()
        if turn > 2:
            send_piece(turn - 3)
    share_pair_sum(tensor - 1)
    sent = max(tensor - 3, 0)
    for turn in range(sent, tensor - 2):
        send_piece(turn)
    d_normed1 = None
    for t in range(tensor):
        part = mm(qkv_ref[t], qkv_weights(t), NT)
        d_normed1 = part if d_normed1 is None else d_normed1 + part
    d_rows, norm1 = norm_back(d_normed1, unit1, inverse1, gain1_ref[...])
    small_ref[experts : experts + 1, :] = norm1
    send_piece(tensor - 2)
    for step in range(1, tensor - 2):
        for way in (0, 1):
            sums.start_first(way, step, 0)
    each(experts, lambda d: small_copy(d, False).start())
    each(experts // 2, lambda d: out_copy(d, False).start())
    each(experts, lambda d: out_copy(d, False).start(), experts // 2 + 1)
    for way in (0, 1):
        sums.start_first(way, tensor - 2, 0)
    next_sum()
    small_plane[me_e] = small_ref[...]
    tokens_grad_ref[...] = compact(cot_ref[...] + d_rows)

    piece_line[me_t] = plane_sum(tensor - 1)
    each(tensor, lambda d: piece_copy(d, True).wait_recv())
    total = piece_line[0].astype(F32)
    for t in range(1, tensor):
        total = total + piece_line[t].astype(F32)
    w_sum_ref[mine, :] = total.astype(BF)
    each(chips, lambda k: final_copy(k, False).start())
    each(experts, lambda d: small_copy(d, True).wait_recv())
    total = small_plane[0]
    for e in range(1, experts):
        total = total + small_plane[e]
    small_line_send[...] = total
    each(tensor, lambda d: small_line_copy(d, False).start())
    small_line[me_t] = total
    while line_steps:
        next_sum()

    each(experts, lambda d: out_copy(d, True).wait_recv())
    each(chips, lambda k: final_copy(k, True).wait_recv())
    final_pair_copy(False).start()
    output = residual_ref[...] + take_rows(slots_of, early_ref, experts)
    output_ref[...] = compact(output).astype(BF)

    each(tensor, lambda d: small_line_copy(d, True).wait_recv())
    total = small_line[0]
    for t in range(1, tensor):
        total = total + small_line[t]
    small_sum_ref[...] = total
    final_pair_copy(True).wait_recv()

    for part in (1, 0):
        sums.last(part)
        total = grads_at(me_t, part)[...].astype(F32)
        for way in (0, 1):
            came = held[way, tensor - 2, part].astype(F32)
            total = total + jnp.where(sums.hops(way) >= 1, came, jnp.zeros_like(came))
        if part == 0:
            in_grad_ref[...] = total.astype(BF)
        else:
            back_grad_ref[...] = total.T.astype(BF)

    sums.finish()
    line_in.finish()
    line_back.finish()

    def sent(d):
        noise_copy(d, False).wait_send()
        back_copy(d, False).wait_send()
        out_copy(d, False).wait_send()
        small_copy(d, False).wait_send()

    each(experts, sent)

    def sent_line(d):
        first_copy(0, d, False).wait_send()
        first_copy(1, d, False).wait_send()
        piece_copy(d, False).wait_send()
        small_line_copy(d, False).wait_send()
        pair_copy(d, False).wait_send()
        each(chips, lambda k: plane_copy(d, k, False).wait_send())

    each(tensor, sent_line)
    each(chips, lambda k: final_copy(k, False).wait_send())
    final_pair_copy(False).wait_send()
    for t in range(tensor):
        w_pair_copy(t).wait_send()
        each(chips, lambda k, t=t: w_copy(t, k, False).wait_send())


def finish_kernel(
    experts, output_in, tokens_in, w_sum_ref, small_ref, in_ref, back_ref,
    output_ref, tokens_ref, norm1_ref, qkv_ref, out_ref, norm2_ref, router_ref,
    in_grad_ref, back_grad_ref,
):
    output_ref[...] = output_in[...]
    tokens_ref[...] = tokens_in[...]
    width = out_ref.shape[0]
    for c in range(3):
        qkv_ref[c] = w_sum_ref[:, c * width : (c + 1) * width].astype(F32)
    out_ref[...] = w_sum_ref[:, 3 * width : 4 * width].T.astype(F32)
    router_ref[...] = small_ref[0:experts, :]
    norm1_ref[...] = small_ref[experts : experts + 1, :]
    norm2_ref[...] = small_ref[experts + 1 : experts + 2, :]
    in_grad_ref[...] = in_ref[...].astype(F32)
    back_grad_ref[...] = back_ref[...].astype(F32)


def per_device(
    tokens, norm1_gain, w_qkv, w_out, norm2_gain, w_router, noise, routes, w_in, w_back, cotangent
):
    own_rows = tokens.shape[0]
    experts = noise.shape[1]
    tensor = lax.axis_size("tensor")
    images = own_rows // SEQ
    rows = images * SP
    capacity = (2 * own_rows * TOP + experts - 1) // experts
    slots = up(capacity, TILE)
    group = max(g for g in range(1, experts + 1) if experts % g == 0 and g * slots <= 2 * SP)
    width = w_out.shape[0]
    hidden = w_in.shape[2]
    heads = tensor * width // HD
    piece = D // experts
    small_rows = up(experts + 2, 8)
    noise_rows = up(3 * experts, TILE)
    pairs = experts * slots
    dma = pltpu.SemaphoreType.DMA
    bf, f32 = (lambda *dims: pltpu.VMEM(dims, BF)), (lambda *dims: pltpu.VMEM(dims, F32))

    output, grad_tokens, w_sum, small, grad_in, grad_back = call(
        functools.partial(block_kernel, experts, tensor, images, group),
        (
            shape((own_rows, D)),
            shape((own_rows, D), F32),
            shape((D, 4 * width)),
            shape((small_rows, D), F32),
            shape((D, hidden)),
            shape((hidden, D)),
        ),
        scratch=(
            bf(tensor, 4, D, width),
            bf(LANES, D),
            bf(tensor, D, hidden),
            bf(tensor, hidden, D),
            f32(up(own_rows, TILE), D),
            f32(rows, D),
            f32(rows, D),
            f32(rows, LANES),
            f32(experts, rows),
            bf(tensor, rows, 3 * width),
            bf(images, heads, SP, SP),
            bf(tensor, rows, width),
            f32(rows, D),
            bf(pairs, D),
            bf(pairs, D),
            bf(pairs, D),
            bf(pairs, D),
            bf(experts, noise_rows, slots),
            bf(experts, noise_rows, slots),
            f32(pairs, LANES),
            bf(tensor, pairs, hidden),
            bf(tensor, max(pairs, D), hidden),
            bf(pairs, D),
            bf(2, tensor - 1, 2, D, hidden),
            bf(D, max(pairs, tensor * 4 * width)),
            bf(tensor, D, hidden),
            bf(tensor, D // CORES, 4 * width),
            bf(experts // CORES, tensor, piece, 4 * width),
            bf(tensor, piece, 4 * width),
            bf(tensor, piece, 4 * width),
            f32(small_rows, D),
            f32(experts, small_rows, D),
            f32(small_rows, D),
            f32(tensor, small_rows, D),
            dma((3,)),
            dma((2, 2, tensor)),
            dma((2, tensor, experts // CORES)),
            dma((2, tensor)),
            dma((2, 2, tensor - 1)),
            dma((2, 2, tensor - 1)),
            dma((2, experts)),
            dma((2, experts)),
            dma((2, experts)),
            dma((2, experts)),
            dma((2, experts)),
            dma((2, tensor - 1, 2)),
            dma((2, tensor - 1, 2)),
            dma((2, tensor)),
            dma((2, tensor, experts // CORES)),
            dma((2, tensor)),
            dma((2, experts // CORES)),
            dma((2, experts)),
            dma((2, tensor)),
        ),
        far_in=(8, 9, 10),
        collective_id=0,
        has_side_effects=True,
    )(
        routes.T, tokens, cotangent, noise.T, norm1_gain.reshape(1, D), norm2_gain.reshape(1, D),
        w_router.T, w_out, w_qkv.transpose(1, 0, 2), w_in[0], w_back[0],
    )
    output, grad_tokens, norm1, grad_qkv, grad_out, norm2, router, grad_in, grad_back = call(
        functools.partial(finish_kernel, experts),
        (
            shape((own_rows, D)),
            shape((own_rows, D), F32),
            shape((1, D), F32),
            shape((3, D, width), F32),
            shape((width, D), F32),
            shape((1, D), F32),
            shape((experts, D), F32),
            shape((D, hidden), F32),
            shape((hidden, D), F32),
        ),
    )(output, grad_tokens, w_sum, small, grad_in, grad_back)
    return (
        output,
        grad_tokens,
        norm1.reshape(D),
        grad_qkv.transpose(1, 0, 2),
        grad_out,
        norm2.reshape(D),
        router.T,
        grad_in[None],
        grad_back[None],
    )


def solution(mesh):
    rows = P(("expert", "tensor"), None)
    placed = (
        rows,
        P(),
        P(None, None, "tensor"),
        P("tensor", None),
        P(),
        P(),
        rows,
        rows,
        P("expert", None, "tensor"),
        P("expert", "tensor", None),
        rows,
    )
    return jax.shard_map(
        per_device,
        mesh=mesh,
        in_specs=placed,
        out_specs=(
            rows,
            rows,
            P(),
            P(None, None, "tensor"),
            P("tensor", None),
            P(),
            P(),
            P("expert", None, "tensor"),
            P("expert", "tensor", None),
        ),
        check_vma=False,
    )
```

```python
import functools

import jax
import jax.numpy as jnp
from jax import lax
from jax.experimental import pallas as pl
from jax.experimental.pallas import tpu as pltpu
from jax.sharding import PartitionSpec as P

D = 512
HD = 64
CORES = 2
TOP = 2
SEQ = 197
LANES = 128
TILE = 16
EPSILON = 1e-06
DENSITY = 0.3989422804014327
TAIL = 0.5 / DENSITY
BF = jnp.bfloat16
F32 = jnp.float32
VMEM_BYTES = 62 * 1024 * 1024

NN = (((1,), (0,)), ((), ()))
NT = (((1,), (1,)), ((), ()))
TN = (((0,), (0,)), ((), ()))


def up(value, unit):
    return (value + unit - 1) // unit * unit


SP = up(SEQ, TILE)


def mm(a, b, dims=NN):
    return lax.dot_general(a, b, dims, preferred_element_type=F32)


def call(
    body, out_shape, scratch=(), flops=0, moved=0, prefetch=(), far_in=(), far_out=(), **more
):
    params = pltpu.CompilerParams(vmem_limit_bytes=VMEM_BYTES, **more)
    cost = pl.CostEstimate(flops=flops, bytes_accessed=moved, transcendentals=0)

    def spec(place, far, scalar=()):
        if place in scalar:
            return pl.BlockSpec(memory_space=pltpu.SMEM)
        return pl.BlockSpec(memory_space=pl.ANY if place in far else pltpu.VMEM)

    def run(*args):
        return pl.pallas_call(
            body,
            out_shape=out_shape,
            in_specs=[spec(place, far_in, prefetch) for place in range(len(args))],
            out_specs=tuple(spec(place, far_out) for place in range(len(out_shape))),
            scratch_shapes=list(scratch),
            compiler_params=params,
            cost_estimate=cost,
        )(*args)

    return run


def shape(dims, dtype=BF):
    return jax.ShapeDtypeStruct(dims, dtype)


def unit_norm(values):
    center = values - jnp.mean(values, -1, keepdims=True)
    spread = jnp.mean(center * center, -1, keepdims=True)
    inverse = lax.rsqrt(spread + EPSILON)
    return center * inverse, inverse


def norm_back(grad_rows, normed, inverse, gain):
    scaled = grad_rows * gain
    inner = (
        scaled
        - jnp.mean(scaled, -1, keepdims=True)
        - normed * jnp.mean(scaled * normed, -1, keepdims=True)
    )
    return inverse * inner, jnp.sum(grad_rows * normed, axis=0, keepdims=True)


def ids(shape_of, dim):
    return lax.broadcasted_iota(jnp.int32, shape_of, dim)


def slots_by_lane(routes, experts):
    rows = routes.shape[1]
    which = ids((experts, rows), 0).astype(F32)
    named = (routes[0:1] == which) | (routes[1:2] == which)
    before = (ids((rows, rows), 0) < ids((rows, rows), 1)).astype(F32).astype(BF)
    rank = mm(named.astype(F32).astype(BF), before)
    return jnp.where(named, rank, -1.0)


def take_rows(slots, in_ref, experts):
    count = in_ref.shape[0] // experts
    rows = slots.shape[0]
    place = ids((rows, count), 1).astype(F32)
    total = None
    for e in range(experts):
        pick = (place == slots[:, e : e + 1]).astype(F32).astype(BF)
        part = mm(pick, in_ref[e * count : (e + 1) * count, :])
        total = part if total is None else total + part
    return total


MESH = pl.DeviceIdType.MESH


def greet(axes):
    barrier = pltpu.get_barrier_semaphore()
    for name, size in axes:
        me = lax.axis_index(name)

        def hello(d, _, name=name, size=size, me=me):
            pl.semaphore_signal(
                barrier, inc=1, device_id={name: lax.rem(me + d, size)}, device_id_type=MESH
            )
            return 0

        lax.fori_loop(1, size, hello, 0)
    pl.semaphore_wait(barrier, sum(size - 1 for _, size in axes))


def remote(src, dst, send_sem, recv_sem, name, to):
    return pltpu.make_async_remote_copy(
        src_ref=src,
        dst_ref=dst,
        send_sem=send_sem,
        recv_sem=recv_sem,
        device_id={name: to},
        device_id_type=MESH,
    )


def each(size, step, first=1):
    def body(d, _):
        step(d)
        return 0

    lax.fori_loop(first, size, body, 0)


class Line:
    def __init__(self, size, own, everyone, send_sem, recv_sem):
        self.size, self.own, self.all = size, own, everyone
        self.send_sem, self.recv_sem = send_sem, recv_sem
        self.me = lax.axis_index("tensor")

    def copy(self, way, step, arriving):
        toward = 1 if way == 0 else -1
        owner = self.me - toward * (step + (1 if arriving else 0))
        src = self.own if step == 0 else self.all.at[owner]
        return remote(
            src, self.all.at[owner], self.send_sem.at[way, step], self.recv_sem.at[way, step],
            "tensor", self.me + toward,
        )

    def sends(self, way, step):
        last = self.size - 1
        if way == 0:
            return (self.me >= step) & (self.me < last)
        return (self.me <= last - step) & (self.me > 0)

    def receives(self, way, step):
        if way == 0:
            return self.me >= step + 1
        return self.me <= self.size - 2 - step

    def start(self, step):
        for way in (0, 1):
            pl.when(self.sends(way, step))(lambda way=way: self.copy(way, step, False).start())

    def arrive(self, step):
        for way in (0, 1):
            pl.when(self.receives(way, step))(
                lambda way=way: self.copy(way, step, True).wait_recv()
            )

    def finish(self):
        for step in range(self.size - 1):
            for way in (0, 1):
                pl.when(self.sends(way, step))(
                    lambda way=way, step=step: self.copy(way, step, False).wait_send()
                )


def gelu_parts(pre):
    density = jnp.exp2(pre * pre * (-0.5 * 1.4426950408889634)) * DENSITY
    t = pl.reciprocal(1.0 + jnp.abs(pre * (0.3275911 * 0.5**0.5)), approx=True)
    series = t * (
        0.254829592 * TAIL
        + t
        * (
            -0.284496736 * TAIL
            + t * (1.421413741 * TAIL + t * (-1.453152027 * TAIL + t * (1.061405429 * TAIL)))
        )
    )
    tail = series * density
    return jnp.where(pre < 0, tail, 1.0 - tail), density


class Sums:
    def __init__(self, size, own, held, send_sem, recv_sem):
        self.size, self.own, self.held = size, own, held
        self.send_sem, self.recv_sem = send_sem, recv_sem
        self.me = lax.axis_index("tensor")

    def hops(self, way):
        return self.me if way == 0 else self.size - 1 - self.me

    def block(self, way, step):
        ahead = self.size - 1 + self.hops(way) - step
        return ahead if way == 0 else self.size - 1 - ahead

    def copy(self, way, step, part, first):
        toward = 1 if way == 0 else -1
        if first:
            src = self.own(self.block(way, step), part)
        else:
            src = self.held.at[way, max(step - 1, 0), part]
        return remote(
            src, self.held.at[way, step, part],
            self.send_sem.at[way, step, part], self.recv_sem.at[way, step, part],
            "tensor", self.me + toward,
        )

    def start_first(self, way, step, part):
        pl.when(self.hops(way) == 0)(lambda: self.copy(way, step, part, True).start())

    def middle(self, way, step):
        hops = self.hops(way)
        return (hops >= 1) & (hops <= step) & (hops < self.size - 1)

    def forward(self, step, part):
        for way in (0, 1):

            def go(way=way):
                self.copy(way, step - 1, part, False).wait_recv()
                held = self.held.at[way, step - 1, part]
                mine = self.own(self.block(way, step), part)
                add_into(held, mine)
                self.copy(way, step, part, False).start()

            pl.when(self.middle(way, step))(go)

    def last(self, part):
        for way in (0, 1):
            pl.when(self.hops(way) >= 1)(
                lambda way=way: self.copy(way, self.size - 2, part, False).wait_recv()
            )

    def finish(self):
        for part in (0, 1):
            for step in range(self.size - 1):
                for way in (0, 1):
                    sends = (self.hops(way) == 0) | self.middle(way, step)
                    pl.when(sends)(
                        lambda way=way, step=step, part=part: self.copy(
                            way, step, part, False
                        ).wait_send()
                    )


def add_into(held, mine):
    rows = held.shape[0]
    block = min(rows, 128)

    def body(r, _):
        at = pl.ds(pl.multiple_of(r * block, block), block)
        held[at, :] = (held[at, :].astype(F32) + mine[at, :].astype(F32)).astype(BF)
        return 0

    lax.fori_loop(0, rows // block, body, 0)


def block_kernel(
    experts, tensor, images, group,
    routes_ref, tokens_ref, cotangent_ref, noise_ref, gain1_ref, gain2_ref, router_own,
    w_out_own, w_qkv_own, w_in_own, w_back_own,
    output_ref, tokens_grad_ref, w_sum_ref, small_sum_ref, in_grad_ref, back_grad_ref,
    w_ref, w_router_ref, w_in_all, w_back_all, narrow, x_ref, cot_ref, rows_ref, lanes_ref,
    qkv_ref, attend_ref, mixed_ref, residual_ref,
    send_ref, routed_ref, early_send, early_ref, noise_send, noise_all, router_ref,
    hidden_ref, slope_ref, back_ref, held,
    wide_ref, back_grads, pair_ref, pieces, piece_send, piece_line,
    small_ref, small_plane, small_line_send, small_line,
    own_sem, first_sems, plane_sems, pair_sems, in_sems, in_back_sems, route_sems, early_sems, noise_sems,
    back_sems, out_sems, sum_send, sum_recv, w_pair_sems, w_sems, piece_sems, final_sems,
    small_sems, small_line_sems,
):
    own_rows = tokens_ref.shape[0]
    width = w_out_own.shape[0]
    wide = 4 * width
    heads = width // HD
    slots = noise_send.shape[2]
    pairs = experts * slots
    parts = w_in_all.shape[0]
    chunk = group * slots
    me_e, me_t = lax.axis_index("expert"), lax.axis_index("tensor")
    piece = D // experts

    chips = experts // CORES
    core = lax.rem(me_e, CORES)
    half = chips * piece

    def rows_at(e):
        at = lax.rem(e, CORES) * chips + e // CORES
        return pl.ds(pl.multiple_of(at * piece, piece), piece)

    def half_at(which):
        return pl.ds(pl.multiple_of(which * half, half), half)

    def chip_after(k):
        return lax.rem(me_e + CORES * k, experts)

    def chip_place(k, arriving):
        return lax.rem(me_e + experts - CORES * k, experts) if arriving else me_e

    mine = rows_at(me_e)

    def after(d):
        return lax.rem(me_e + d, experts)

    def place(d, arriving):
        return lax.rem(me_e + experts - d, experts) if arriving else me_e

    def swap_copy(src, dst, sems, d, arriving):
        to = after(d)
        return remote(
            src.at[to], dst.at[place(d, arriving)], sems.at[0, d], sems.at[1, d], "expert", to
        )

    def line_copy(src, dst, sems, d, arriving):
        owner = lax.rem(me_t + tensor - d, tensor) if arriving else me_t
        return remote(
            src, dst(owner), sems.at[0, d], sems.at[1, d],
            "tensor", lax.rem(me_t + d, tensor),
        )

    def first_copy(which, d, arriving):
        parts_of = (slice(0, 3), slice(3, 4))[which]
        src = w_ref.at[me_t, parts_of, mine] if which else w_qkv_own.at[:, mine]
        return line_copy(
            src, lambda owner: w_ref.at[owner, parts_of, mine], first_sems.at[which], d, arriving
        )

    def plane_copy(z, k, arriving):
        owner = lax.rem(me_t + tensor - z, tensor)
        block = w_ref.at[owner, :, rows_at(chip_place(k, arriving))]
        return remote(
            block, block, plane_sems.at[0, z, k], plane_sems.at[1, z, k], "expert", chip_after(k)
        )

    def pair_copy(z, arriving):
        owner = lax.rem(me_t + tensor - z, tensor)
        block = w_ref.at[owner, :, half_at(CORES - 1 - core if arriving else core)]
        return remote(
            block, block, pair_sems.at[0, z], pair_sems.at[1, z], "expert",
            me_e + CORES - 1 - 2 * core,
        )

    def slot_rows(e):
        return pl.ds(pl.multiple_of(e * slots, slots), slots)

    def flat_copy(src, dst, sems, d, arriving):
        return remote(
            src.at[slot_rows(after(d))], dst.at[slot_rows(place(d, arriving))],
            sems.at[0, d], sems.at[1, d], "expert", after(d),
        )

    def route_copy(d, arriving):
        return flat_copy(send_ref, routed_ref, route_sems, d, arriving)

    def early_copy(d, arriving):
        return flat_copy(early_send, early_ref, early_sems, d, arriving)

    def noise_copy(d, arriving):
        return swap_copy(noise_send, noise_all, noise_sems, d, arriving)

    def back_copy(d, arriving):
        return flat_copy(early_send, back_ref, back_sems, d, arriving)

    def out_copy(d, arriving):
        return flat_copy(send_ref, early_ref, out_sems, d, arriving)

    def columns(t):
        return slice(t * wide, (t + 1) * wide)

    def w_pair_copy(t):
        return remote(
            wide_ref.at[half_at(CORES - 1 - core), columns(t)], pair_ref.at[t],
            w_pair_sems.at[0, t], w_pair_sems.at[1, t], "expert", me_e + CORES - 1 - 2 * core,
        )

    def w_copy(t, k, arriving):
        return remote(
            wide_ref.at[rows_at(chip_after(k)), columns(t)],
            pieces.at[chip_place(k, arriving) // CORES, t],
            w_sems.at[0, t, k], w_sems.at[1, t, k], "expert", chip_after(k),
        )

    def share_pair_sum(t):
        w_pair_copy(t).wait_recv()
        ours = half_at(core)
        pair_sum = wide_ref[ours, columns(t)].astype(F32) + pair_ref[t].astype(F32)
        wide_ref[ours, columns(t)] = pair_sum.astype(BF)
        each(chips, lambda k: w_copy(t, k, False).start())
        pieces[me_e // CORES, t] = wide_ref[mine, columns(t)]

    def plane_sum(t):
        each(chips, lambda k: w_copy(t, k, True).wait_recv())
        total = pieces[0, t].astype(F32)
        for e in range(1, chips):
            total = total + pieces[e, t].astype(F32)
        return total.astype(BF)

    def send_piece(t):
        piece_send[t] = plane_sum(t)
        piece_copy(t + 1, False).start()

    def piece_copy(d, arriving):
        return line_copy(piece_send.at[d - 1], lambda owner: piece_line.at[owner], piece_sems, d, arriving)

    def final_copy(k, arriving):
        block = w_sum_ref.at[rows_at(chip_place(k, arriving))]
        return remote(
            block, block, final_sems.at[0, k], final_sems.at[1, k], "expert", chip_after(k)
        )

    def final_pair_copy(arriving):
        block = w_sum_ref.at[half_at(CORES - 1 - core if arriving else core)]
        return remote(
            block, block, final_sems.at[0, 0], final_sems.at[1, 0], "expert",
            me_e + CORES - 1 - 2 * core,
        )

    def small_copy(d, arriving):
        return remote(
            small_ref, small_plane.at[place(d, arriving)], small_sems.at[0, d],
            small_sems.at[1, d], "expert", after(d),
        )

    def small_line_copy(d, arriving):
        return line_copy(
            small_line_send, lambda owner: small_line.at[owner], small_line_sems, d, arriving
        )

    greet((("expert", experts), ("tensor", tensor)))
    each(tensor, lambda d: first_copy(0, d, False).start())
    line_in = Line(tensor, w_in_own, w_in_all, in_sems.at[0], in_sems.at[1])
    line_back = Line(tensor, w_back_own, w_back_all, in_back_sems.at[0], in_back_sems.at[1])
    w_ref[me_t, 3] = w_out_own[...].T
    each(tensor, lambda d: first_copy(1, d, False).start())
    line_in.start(0)
    keep = [
        pltpu.make_async_copy(w_qkv_own, w_ref.at[me_t, 0:3], own_sem.at[0]),
        pltpu.make_async_copy(w_in_own, w_in_all.at[me_t], own_sem.at[1]),
        pltpu.make_async_copy(w_back_own, w_back_all.at[me_t], own_sem.at[2]),
    ]
    for copy in keep:
        copy.start()

    def spread(compact, to_ref, fill=0.0):
        columns = compact.shape[1]
        narrow[0:own_rows, 0:columns] = compact
        to_ref[...] = jnp.full(to_ref.shape, fill, F32)
        for i in range(images):
            to_ref[i * SP : i * SP + SEQ, 0:columns] = narrow[
                i * SEQ : (i + 1) * SEQ, 0:columns
            ]

    def compact(padded):
        for i in range(images):
            narrow[i * SEQ : (i + 1) * SEQ, :] = padded[i * SP : i * SP + SEQ, :]
        return narrow[0:own_rows, :]

    def spread_lanes(packed, fill):
        gap = jnp.full((packed.shape[0], SP - SEQ), fill, F32)
        blocks = []
        for i in range(images):
            blocks += [packed[:, i * SEQ : (i + 1) * SEQ], gap]
        return jnp.concatenate(blocks, axis=1)

    noise = spread_lanes(noise_ref[...], 0.0)
    high = noise.astype(BF).astype(F32)
    middle = (noise - high).astype(BF).astype(F32)
    low = noise - high - middle
    noise_parts = [high, middle, low]
    if noise_send.shape[1] > 3 * experts:
        noise_parts.append(jnp.zeros((noise_send.shape[1] - 3 * experts, noise.shape[1]), F32))
    noise = jnp.concatenate(noise_parts, axis=0).astype(BF)
    slots_by = slots_by_lane(spread_lanes(routes_ref[...].astype(F32), -1.0), experts)
    lanes_ref[...] = slots_by
    no_slots = jnp.zeros((LANES - experts, slots_by.shape[1]), F32)
    rows_ref[...] = jnp.concatenate([slots_by, no_slots], axis=0).T
    no_router = jnp.zeros((LANES - experts, D), F32)
    w_router_ref[...] = jnp.concatenate(
        [router_own[...].astype(F32), no_router], axis=0
    ).astype(BF)
    spread(cotangent_ref[...].astype(F32), cot_ref)
    cot_low = cot_ref[...].astype(BF)
    spot = ids((slots, lanes_ref.shape[1]), 0).astype(F32)

    def pick_of(e):
        return (spot == lanes_ref[pl.ds(e, 1), :]).astype(F32).astype(BF)

    def forward_piece(z):
        first_copy(0, z, True).wait_recv()
        first_copy(1, z, True).wait_recv()
        each(chips, lambda k: plane_copy(z, k, False).start())

    each(tensor, forward_piece)
    for d in range(1, experts + 1):
        e = after(d)
        pick = pick_of(e)
        rows_of_e = mm(pick, cot_low).astype(BF)
        noise_of_e = mm(noise, pick, NT).astype(BF)
        if d < experts:
            early_send[slot_rows(e), :] = rows_of_e
            noise_send[e] = noise_of_e
            early_copy(d, False).start()
            noise_copy(d, False).start()
        else:
            early_ref[slot_rows(e), :] = rows_of_e
            noise_all[e] = noise_of_e
    spread(tokens_ref[...].astype(F32), x_ref)
    x = x_ref[...]
    unit1, inverse1 = unit_norm(x)
    normed1 = (unit1 * gain1_ref[...]).astype(BF)
    line_in.arrive(0)
    if tensor > 2:
        line_in.start(1)

    def forward_half(z):
        each(chips, lambda k: plane_copy(z, k, True).wait_recv())
        pair_copy(z, False).start()

    each(tensor, forward_half)
    keep[0].wait()
    each(tensor, lambda z: pair_copy(z, True).wait_recv())

    def qkv_weights(t):
        return jnp.concatenate([w_ref[t, c] for c in range(3)], axis=1)

    lane = ids((SP, width), 1) // HD
    live = ids((SP, SP), 1) < SEQ
    for t in range(tensor):
        qkv_ref[t] = mm(normed1, qkv_weights(t)).astype(BF)
        for i in range(images):
            rows = slice(i * SP, (i + 1) * SP)
            q = qkv_ref[t, rows, 0:width]
            k = qkv_ref[t, rows, width : 2 * width]
            v = qkv_ref[t, rows, 2 * width : 3 * width]
            mixed = None
            for j in range(heads):
                q_j = q if heads == 1 else jnp.where(lane == j, q, jnp.zeros_like(q))
                scores = mm(q_j, k, NT) * HD ** (-0.5)
                scores = jnp.where(live, scores, -1e30)
                power = jnp.exp(scores - jnp.max(scores, -1, keepdims=True))
                attend = (power / jnp.sum(power, -1, keepdims=True)).astype(BF)
                attend_ref[i, t * heads + j] = attend
                part = mm(attend, v)
                mixed = part if mixed is None else jnp.where(lane == j, part, mixed)
            mixed_ref[t, rows, :] = mixed.astype(BF)
    residual = x
    for t in range(tensor):
        residual = residual + mm(mixed_ref[t], w_ref[t, 3], NT)
    residual_ref[...] = residual
    unit2, inverse2 = unit_norm(residual)
    normed2 = (unit2 * gain2_ref[...]).astype(BF)
    for d in range(1, experts + 1):
        e = after(d)
        rows_of_e = mm(pick_of(e), normed2).astype(BF)
        if d < experts:
            send_ref[slot_rows(e), :] = rows_of_e
            route_copy(d, False).start()
        else:
            routed_ref[slot_rows(e), :] = rows_of_e
    for step in range(1, tensor - 1):
        line_in.arrive(step)
        if step + 1 < tensor - 1:
            line_in.start(step + 1)
        if step == max(1, tensor - 3):
            line_back.start(0)
    if tensor == 2:
        line_back.start(0)
    keep[1].wait()

    fold_from, fold_to = ids((noise_all.shape[1], LANES), 0), ids((noise_all.shape[1], LANES), 1)
    fold = (
        (fold_from < 3 * experts) & (lax.rem(fold_from, experts) == fold_to)
    ).astype(F32).astype(BF)
    expert_lane = ids((chunk, LANES), 1)
    groups = experts // group

    def block_rows(at):
        return pl.ds(pl.multiple_of(at * chunk, chunk), chunk)

    def hidden_units(turn, _):
        at = lax.rem(me_e // group + groups - turn, groups)
        for k in range(group):
            d = lax.rem(me_e + experts - (at * group + k), experts)

            @pl.when(d > 0)
            def _(d=d):
                route_copy(d, True).wait_recv()
                early_copy(d, True).wait_recv()
                noise_copy(d, True).wait_recv()

        @pl.when(turn == groups // 2)
        def _():
            for step in range(0, tensor - 3):
                line_back.arrive(step)
                line_back.start(step + 1)

        rows = block_rows(at)
        came = routed_ref[rows, :]
        added = [mm(noise_all[at * group + k], fold, TN) for k in range(group)]
        added = added[0] if group == 1 else jnp.concatenate(added, axis=0)
        logits = jnp.where(expert_lane < experts, mm(came, w_router_ref[...], NT) + added, -1e30)
        power = jnp.exp(logits - jnp.max(logits, -1, keepdims=True))
        router = power / jnp.sum(power, -1, keepdims=True)
        router_ref[rows, :] = router
        gate = jnp.sum(jnp.where(expert_lane == me_e, router, 0.0), -1, keepdims=True)
        early_ref[rows, :] = (gate * early_ref[rows, :].astype(F32)).astype(BF)
        half_rows, block = chunk // 2, min(256, w_in_all.shape[2])

        def spot_of(r):
            return pl.ds(pl.multiple_of(at * chunk + r * half_rows, TILE), half_rows)

        cuts = [
            (f, n, r)
            for f in range(parts)
            for n in range(0, w_in_all.shape[2], block)
            for r in range(2)
        ]

        def pre_of(f, n, r):
            return mm(routed_ref[spot_of(r), :], w_in_all[f, :, n : n + block])

        ahead = pre_of(*cuts[0])
        for number, (f, n, r) in enumerate(cuts):
            pre = ahead
            if number + 1 < len(cuts):
                ahead = pre_of(*cuts[number + 1])
            normal, density = gelu_parts(pre)
            hidden_ref[f, spot_of(r), n : n + block] = (pre * normal).astype(BF)
            slope_ref[f, spot_of(r), n : n + block] = (normal + pre * density).astype(BF)
        return 0

    lax.fori_loop(0, groups, hidden_units, 0)

    def grads_at(block, part):
        return back_grads.at[block] if part else slope_ref.at[block, 0:D]

    sums = Sums(tensor, grads_at, held, sum_send, sum_recv)
    order = []
    for step in range(tensor):
        for f in (tensor - 1 - step, step):
            if f not in order:
                order.append(f)

    def turn_rows(ref):
        def body(at, _):
            rows = pl.ds(pl.multiple_of(at * LANES, LANES), LANES)
            wide_ref[:, rows] = ref[rows, :].T
            return 0

        lax.fori_loop(0, pairs // LANES, body, 0)

    def weight_grads(part, right):
        for f in order:
            block = mm(wide_ref[:, 0:pairs], right[f, 0:pairs, :]).astype(BF)
            grads_at(f, part)[...] = block
            for step in range(tensor - 1 if part else 1):
                for way, to in ((0, tensor - 1 - step), (1, step)):
                    if to == f:
                        sums.start_first(way, step, part)

    turn_rows(early_ref)
    weight_grads(1, hidden_ref)
    turn_rows(routed_ref)

    for step in range(max(tensor - 3, 0), tensor - 2):
        line_back.arrive(step)
        line_back.start(step + 1)
    keep[2].wait()

    def early_sent(d):
        early_copy(d, False).wait_send()
        route_copy(d, False).wait_send()

    each(experts, early_sent)

    small_ref[...] = jnp.zeros_like(small_ref)

    def near(k):
        def from_low(me):
            below = (me - k + tensor) // tensor
            return below * (me - k) + (1 - below) * k

        low = 1 - (2 * me_t) // tensor
        mirrored = tensor - 1 - from_low(tensor - 1 - me_t)
        return low * from_low(me_t) + (1 - low) * mirrored

    def unit_part(k, rows):
        f = near(k)
        w_b = w_back_all[f]
        out = mm(hidden_ref[f, rows, :], w_b)
        d_pre = (mm(early_ref[rows, :], w_b, NT) * slope_ref[f, rows, :].astype(F32)).astype(BF)
        slope_ref[f, rows, :] = d_pre
        return out, mm(d_pre, w_in_all[f], NT)

    def near_rows(at, _):
        rows = block_rows(at)
        out, back = unit_part(0, rows)
        for k in range(1, tensor - 1):
            more_out, more_back = unit_part(k, rows)
            out, back = out + more_out, back + more_back
        send_ref[rows, :] = out.astype(BF)
        early_send[rows, :] = back.astype(BF)
        return 0

    lax.fori_loop(0, groups, near_rows, 0)
    line_steps = [(step, part) for part in (1, 0) for step in range(1, tensor - 1)]

    def next_sum():
        if line_steps:
            sums.forward(*line_steps.pop(0))

    next_sum()
    line_back.arrive(tensor - 2)

    def far_rows(turn, _):
        ours, across = me_e // group, groups // 2
        at = 2 * lax.rem(ours // 2 + 1 + turn // 2, across) + lax.rem(ours + 1 + turn, 2)
        rows = block_rows(at)
        router = router_ref[rows, :]
        own_lane = expert_lane == me_e
        gate = jnp.sum(jnp.where(own_lane, router, 0.0), -1, keepdims=True)
        out, back = unit_part(tensor - 1, rows)
        out = (out + send_ref[rows, :].astype(F32)).astype(BF).astype(F32)
        back = back + early_send[rows, :].astype(F32)
        d_gate = jnp.sum(early_ref[rows, :].astype(F32) * out, -1, keepdims=True)
        d_logits = (d_gate * (own_lane.astype(F32) - router)).astype(BF)
        early_send[rows, :] = (back + mm(d_logits, w_router_ref[...])).astype(BF)
        send_ref[rows, :] = (gate * out).astype(BF)
        router_ref[rows, :] = d_logits.astype(F32)
        for k in range(group):
            e = at * group + k
            d = lax.rem(e + experts - me_e, experts)

            @pl.when(d > 0)
            def _(d=d):
                back_copy(d, False).start()

            @pl.when(d == 0)
            def _(e=e):
                back_ref[slot_rows(e), :] = early_send[slot_rows(e), :]
                early_ref[slot_rows(e), :] = send_ref[slot_rows(e), :]

        return 0

    lax.fori_loop(0, groups, far_rows, 0)

    weight_grads(0, slope_ref)

    def router_part(at, _):
        rows = block_rows(at)
        d_logits = router_ref[rows, :].astype(BF)
        small_ref[0:experts, :] += mm(d_logits, routed_ref[rows, :], TN)[0:experts]
        return 0

    lax.fori_loop(0, groups, router_part, 0)
    unit1, inverse1 = unit_norm(x_ref[...])
    normed1 = (unit1 * gain1_ref[...]).astype(BF)
    unit2, inverse2 = unit_norm(residual_ref[...])
    each(experts, lambda d: back_copy(d, True).wait_recv())
    out_copy(experts // 2, False).start()
    slots_of = rows_ref[:, 0:experts]
    d_normed2 = take_rows(slots_of, back_ref, experts)
    d_rows, norm2 = norm_back(d_normed2, unit2, inverse2, gain2_ref[...])
    small_ref[experts + 1 : experts + 2, :] = norm2
    d_residual = cot_ref[...] + d_rows
    cot_ref[...] = d_residual
    d_attention = d_residual.astype(BF)
    scaling = HD ** (-0.5)
    for turn in range(tensor):
        t = lax.rem(me_t + 1 + turn, tensor)
        first = turn * wide
        wide_ref[:, first + 3 * width : first + wide] = mm(d_attention, mixed_ref[t], TN).astype(BF)
        d_mixed = mm(d_attention, w_ref[t, 3]).astype(BF)
        for i in range(images):
            rows = slice(i * SP, (i + 1) * SP)
            q = qkv_ref[t, rows, 0:width]
            k = qkv_ref[t, rows, width : 2 * width]
            v = qkv_ref[t, rows, 2 * width : 3 * width]
            do = d_mixed[rows]
            dq = dk = dv = None
            for j in range(heads):
                own = lane == j
                do_j = do if heads == 1 else jnp.where(own, do, jnp.zeros_like(do))
                q_j = q if heads == 1 else jnp.where(own, q, jnp.zeros_like(q))
                attend_low = attend_ref[i, t * heads + j]
                attend = attend_low.astype(F32)
                part_v = mm(attend_low, do_j, TN)
                d_attend = mm(do_j, v, NT)
                inner = jnp.sum(attend * d_attend, -1, keepdims=True)
                ds = (attend * (d_attend - inner)).astype(BF)
                part_q = mm(ds, k) * scaling
                part_k = mm(ds, q_j, TN) * scaling
                dq = part_q if dq is None else jnp.where(own, part_q, dq)
                dk = part_k if dk is None else dk + part_k
                dv = part_v if dv is None else dv + part_v
            qkv_ref[t, rows, 0:width] = dq.astype(BF)
            qkv_ref[t, rows, width : 2 * width] = dk.astype(BF)
            qkv_ref[t, rows, 2 * width : 3 * width] = dv.astype(BF)
        wide_ref[:, first : first + 3 * width] = mm(normed1, qkv_ref[t], TN).astype(BF)
        w_pair_copy(turn).start()
        if turn > 0:
            share_pair_sum(turn - 1)
        if turn == 0:
            next_sum()
        if turn > 2:
            send_piece(turn - 3)
    share_pair_sum(tensor - 1)
    sent = max(tensor - 3, 0)
    for turn in range(sent, tensor - 2):
        send_piece(turn)
    d_normed1 = None
    for t in range(tensor):
        part = mm(qkv_ref[t], qkv_weights(t), NT)
        d_normed1 = part if d_normed1 is None else d_normed1 + part
    d_rows, norm1 = norm_back(d_normed1, unit1, inverse1, gain1_ref[...])
    small_ref[experts : experts + 1, :] = norm1
    send_piece(tensor - 2)
    for step in range(1, tensor - 2):
        for way in (0, 1):
            sums.start_first(way, step, 0)
    each(experts, lambda d: small_copy(d, False).start())
    each(experts // 2, lambda d: out_copy(d, False).start())
    each(experts, lambda d: out_copy(d, False).start(), experts // 2 + 1)
    for way in (0, 1):
        sums.start_first(way, tensor - 2, 0)
    next_sum()
    small_plane[me_e] = small_ref[...]
    tokens_grad_ref[...] = compact(cot_ref[...] + d_rows)

    piece_line[me_t] = plane_sum(tensor - 1)
    each(tensor, lambda d: piece_copy(d, True).wait_recv())
    total = piece_line[0].astype(F32)
    for t in range(1, tensor):
        total = total + piece_line[t].astype(F32)
    w_sum_ref[mine, :] = total.astype(BF)
    each(chips, lambda k: final_copy(k, False).start())
    each(experts, lambda d: small_copy(d, True).wait_recv())
    total = small_plane[0]
    for e in range(1, experts):
        total = total + small_plane[e]
    small_line_send[...] = total
    each(tensor, lambda d: small_line_copy(d, False).start())
    small_line[me_t] = total
    while line_steps:
        next_sum()

    each(experts, lambda d: out_copy(d, True).wait_recv())
    each(chips, lambda k: final_copy(k, True).wait_recv())
    final_pair_copy(False).start()
    output = residual_ref[...] + take_rows(slots_of, early_ref, experts)
    output_ref[...] = compact(output).astype(BF)

    each(tensor, lambda d: small_line_copy(d, True).wait_recv())
    total = small_line[0]
    for t in range(1, tensor):
        total = total + small_line[t]
    small_sum_ref[...] = total
    final_pair_copy(True).wait_recv()

    for part in (1, 0):
        sums.last(part)
        total = grads_at(me_t, part)[...].astype(F32)
        for way in (0, 1):
            came = held[way, tensor - 2, part].astype(F32)
            total = total + jnp.where(sums.hops(way) >= 1, came, jnp.zeros_like(came))
        if part == 0:
            in_grad_ref[...] = total.astype(BF)
        else:
            back_grad_ref[...] = total.T.astype(BF)

    sums.finish()
    line_in.finish()
    line_back.finish()

    def sent(d):
        noise_copy(d, False).wait_send()
        back_copy(d, False).wait_send()
        out_copy(d, False).wait_send()
        small_copy(d, False).wait_send()

    each(experts, sent)

    def sent_line(d):
        first_copy(0, d, False).wait_send()
        first_copy(1, d, False).wait_send()
        piece_copy(d, False).wait_send()
        small_line_copy(d, False).wait_send()
        pair_copy(d, False).wait_send()
        each(chips, lambda k: plane_copy(d, k, False).wait_send())

    each(tensor, sent_line)
    each(chips, lambda k: final_copy(k, False).wait_send())
    final_pair_copy(False).wait_send()
    for t in range(tensor):
        w_pair_copy(t).wait_send()
        each(chips, lambda k, t=t: w_copy(t, k, False).wait_send())


def finish_kernel(
    experts, output_in, tokens_in, w_sum_ref, small_ref, in_ref, back_ref,
    output_ref, tokens_ref, norm1_ref, qkv_ref, out_ref, norm2_ref, router_ref,
    in_grad_ref, back_grad_ref,
):
    output_ref[...] = output_in[...]
    tokens_ref[...] = tokens_in[...]
    width = out_ref.shape[0]
    for c in range(3):
        qkv_ref[c] = w_sum_ref[:, c * width : (c + 1) * width].astype(F32)
    out_ref[...] = w_sum_ref[:, 3 * width : 4 * width].T.astype(F32)
    router_ref[...] = small_ref[0:experts, :]
    norm1_ref[...] = small_ref[experts : experts + 1, :]
    norm2_ref[...] = small_ref[experts + 1 : experts + 2, :]
    in_grad_ref[...] = in_ref[...].astype(F32)
    back_grad_ref[...] = back_ref[...].astype(F32)


def per_device(
    tokens, norm1_gain, w_qkv, w_out, norm2_gain, w_router, noise, routes, w_in, w_back, cotangent
):
    own_rows = tokens.shape[0]
    experts = noise.shape[1]
    tensor = lax.axis_size("tensor")
    images = own_rows // SEQ
    rows = images * SP
    capacity = (2 * own_rows * TOP + experts - 1) // experts
    slots = up(capacity, TILE)
    group = max(g for g in range(1, experts + 1) if experts % g == 0 and g * slots <= 2 * SP)
    width = w_out.shape[0]
    hidden = w_in.shape[2]
    heads = tensor * width // HD
    piece = D // experts
    small_rows = up(experts + 2, 8)
    noise_rows = up(3 * experts, TILE)
    pairs = experts * slots
    dma = pltpu.SemaphoreType.DMA
    bf, f32 = (lambda *dims: pltpu.VMEM(dims, BF)), (lambda *dims: pltpu.VMEM(dims, F32))

    output, grad_tokens, w_sum, small, grad_in, grad_back = call(
        functools.partial(block_kernel, experts, tensor, images, group),
        (
            shape((own_rows, D)),
            shape((own_rows, D), F32),
            shape((D, 4 * width)),
            shape((small_rows, D), F32),
            shape((D, hidden)),
            shape((hidden, D)),
        ),
        scratch=(
            bf(tensor, 4, D, width),
            bf(LANES, D),
            bf(tensor, D, hidden),
            bf(tensor, hidden, D),
            f32(up(own_rows, TILE), D),
            f32(rows, D),
            f32(rows, D),
            f32(rows, LANES),
            f32(experts, rows),
            bf(tensor, rows, 3 * width),
            bf(images, heads, SP, SP),
            bf(tensor, rows, width),
            f32(rows, D),
            bf(pairs, D),
            bf(pairs, D),
            bf(pairs, D),
            bf(pairs, D),
            bf(experts, noise_rows, slots),
            bf(experts, noise_rows, slots),
            f32(pairs, LANES),
            bf(tensor, pairs, hidden),
            bf(tensor, max(pairs, D), hidden),
            bf(pairs, D),
            bf(2, tensor - 1, 2, D, hidden),
            bf(D, max(pairs, tensor * 4 * width)),
            bf(tensor, D, hidden),
            bf(tensor, D // CORES, 4 * width),
            bf(experts // CORES, tensor, piece, 4 * width),
            bf(tensor, piece, 4 * width),
            bf(tensor, piece, 4 * width),
            f32(small_rows, D),
            f32(experts, small_rows, D),
            f32(small_rows, D),
            f32(tensor, small_rows, D),
            dma((3,)),
            dma((2, 2, tensor)),
            dma((2, tensor, experts // CORES)),
            dma((2, tensor)),
            dma((2, 2, tensor - 1)),
            dma((2, 2, tensor - 1)),
            dma((2, experts)),
            dma((2, experts)),
            dma((2, experts)),
            dma((2, experts)),
            dma((2, experts)),
            dma((2, tensor - 1, 2)),
            dma((2, tensor - 1, 2)),
            dma((2, tensor)),
            dma((2, tensor, experts // CORES)),
            dma((2, tensor)),
            dma((2, experts // CORES)),
            dma((2, experts)),
            dma((2, tensor)),
        ),
        far_in=(8, 9, 10),
        collective_id=0,
        has_side_effects=True,
    )(
        routes.T, tokens, cotangent, noise.T, norm1_gain.reshape(1, D), norm2_gain.reshape(1, D),
        w_router.T, w_out, w_qkv.transpose(1, 0, 2), w_in[0], w_back[0],
    )
    output, grad_tokens, norm1, grad_qkv, grad_out, norm2, router, grad_in, grad_back = call(
        functools.partial(finish_kernel, experts),
        (
            shape((own_rows, D)),
            shape((own_rows, D), F32),
            shape((1, D), F32),
            shape((3, D, width), F32),
            shape((width, D), F32),
            shape((1, D), F32),
            shape((experts, D), F32),
            shape((D, hidden), F32),
            shape((hidden, D), F32),
        ),
    )(output, grad_tokens, w_sum, small, grad_in, grad_back)
    return (
        output,
        grad_tokens,
        norm1.reshape(D),
        grad_qkv.transpose(1, 0, 2),
        grad_out,
        norm2.reshape(D),
        router.T,
        grad_in[None],
        grad_back[None],
    )


def solution(mesh):
    rows = P(("expert", "tensor"), None)
    placed = (
        rows,
        P(),
        P(None, None, "tensor"),
        P("tensor", None),
        P(),
        P(),
        rows,
        rows,
        P("expert", None, "tensor"),
        P("expert", "tensor", None),
        rows,
    )
    return jax.shard_map(
        per_device,
        mesh=mesh,
        in_specs=placed,
        out_specs=(
            rows,
            rows,
            P(),
            P(None, None, "tensor"),
            P("tensor", None),
            P(),
            P(),
            P("expert", None, "tensor"),
            P("expert", "tensor", None),
        ),
        check_vma=False,
    )
```
